32 devices in a mesh: grp: 2 (over x), tpl: 16 (over z, y, core).
Axes of the slice: x: 2, y: 2, z: 4, core: 2. Of those that a mesh axis runs over, the one named last changes fastest.
Arguments:
- strain_slots: bfloat16 [32, 3, 2, 262144], P(('grp', 'tpl')), parts along dimension 0, may hold values from -6 to 6
- templates: bfloat16 [32, 2, 262144], P(None, None, 'tpl'), may hold values from -6 to 6
- cutoffs: int32 [32], replicated, may hold values from 32768 to 262144
- lists: int32 [16, 2], replicated, may hold values from 0 to 31, as said below
- owner: int32 [2], P('grp'), parts along dimension 0, may hold values from 0 to 15
- slides: int32 [6], P('grp'), parts along dimension 0, may hold values from 0 to 262143
Outputs:
- peaks: float32 [64], P(('grp', 'tpl')), parts along dimension 0
- norms: float32 [64], P(('grp', 'tpl')), parts along dimension 0
The draws below stay inside these ranges and needn't reach their ends.
There are 2 independent parts, one for each index of `grp`. The reference program is written for one: setup_inputs(seed, part) draws one part's arguments, and reference() takes and returns one part's arrays. A program takes and returns all parts, laid end to end along the dimension named above; an argument that names none is the same for every part. Nothing has to cross between parts.
Inputs may be any that keep to these rules, and one draw needn't show every extreme that they name: Every template appears once in lists; list positions in row-major order run through the templates by falling cutoffs. One template has cutoff 262144, one has 32768.
All inputs are finite; a program needn't handle non-finite values.
Results may differ from the reference program's by a relative error of at most 0.0021.
Values may be sent and summed in bfloat16 or wider, within the bound.
No kernel may reach another device: no remote copies, remote signals or barrier semaphores. Data moves between devices by JAX's collectives and lax.ppermute only.
A program may use at most 128 MiB of HBM per device.

```python
import jax
import jax.numpy as jnp
from jax import lax

DET = 3
ROWS = 512
COLS = 512
TPL_DEV = 2
BINS = 262144
TEMPLATES = 32
SLOTS = 16
N_TPL = 16


def bank_draw(key):
    keys = jax.random.split(jax.random.fold_in(key, 7), 3)
    cutoff_bins = jax.random.randint(keys[0], (TEMPLATES,), BINS // 8, BINS + 1)
    marks = jax.random.permutation(keys[1], TEMPLATES)
    cutoff_bins = jnp.where(marks == 0, BINS, cutoff_bins)
    cutoff_bins = jnp.where(marks == 1, BINS // 8, cutoff_bins)
    breakers = jax.random.permutation(keys[2], TEMPLATES)
    scores = cutoff_bins * TEMPLATES + breakers
    ordered = jnp.argsort(-scores, stable=True)
    return (cutoff_bins.astype(jnp.int32), ordered.astype(jnp.int32).reshape(TEMPLATES // TPL_DEV, TPL_DEV))


def draw_cutoffs(key, part):
    return bank_draw(key)[0]


def draw_lists(key, part):
    return bank_draw(key)[1]


def level_of(rng, shape, cuts, least, largest):
    factor_of, own = 1.0, jax.random.fold_in(rng, 6)
    for axis_at, parts in cuts:
        draws = jnp.exp(jax.random.uniform(jax.random.fold_in(own, axis_at), (parts,), jnp.float32, least / len(cuts), largest / len(cuts)))
        factor_of = factor_of * jnp.repeat(draws, shape[axis_at] // parts).reshape([-1 if axis == axis_at else 1 for axis in range(len(shape))])
    return factor_of


def normal_values(key, shape, scale, bound, shards=(), held_as=jnp.bfloat16):
    level = level_of(key, shape, shards, -0.22, 0.18) if shards else 1.0
    result = jax.random.normal(key, shape, jnp.float32) * scale * level
    return jnp.minimum(jnp.maximum(result, -bound), bound).astype(held_as)


def setup_inputs(seed: int = 0, part: int = 0) -> dict:
    key_list = jax.random.split(jax.random.key(seed), 7)
    part_splits = jax.random.split(jax.random.fold_in(key_list[6], part), 7)
    return {
        "strain_slots": normal_values(part_splits[0], (SLOTS, DET, 2, BINS), 1.0, 6.0, ((0, 16),)),
        "templates": normal_values(key_list[1], (TEMPLATES, 2, BINS), 1.0, 6.0, ((2, 16),)),
        "cutoffs": draw_cutoffs(jax.random.fold_in(key_list[6], 71), part),
        "lists": draw_lists(jax.random.fold_in(key_list[6], 71), part),
        "owner": jax.random.randint(part_splits[4], (1,), 0, N_TPL).astype(jnp.int32),
        "slides": jax.random.randint(part_splits[5], (DET,), 0, BINS).astype(jnp.int32),
    }


two_pi = 6.283185307179586
eps_norm = 1e-6


def turn_table(left_ids, right_ids, period):
    product_idx = (left_ids[:, None] * right_ids[None, :]) % period
    angles = product_idx.astype(jnp.float32) * (two_pi / period)
    return jnp.cos(angles), jnp.sin(angles)


def slide_phases(slides):
    total = ROWS * COLS
    bin_ids = jnp.arange(total, dtype=jnp.int32)
    row_ids = bin_ids // COLS
    col_ids = bin_ids % COLS
    stride = (COLS * slides) % total
    turns = ((row_ids[None, :] * stride[:, None]) % total + (col_ids[None, :] * slides[:, None]) % total) % total
    angles = turns.astype(jnp.float32) * (two_pi / total)
    return jnp.cos(angles), jnp.sin(angles)


def rounded(values):
    return lax.optimization_barrier(values.astype(jnp.bfloat16)).astype(jnp.float32)


def reference(strain_slots, templates, cutoffs, lists, owner, slides):
    total = ROWS * COLS
    strain = lax.dynamic_index_in_dim(strain_slots, owner[0], 0, keepdims=False).astype(jnp.float32)
    row_ids = jnp.arange(ROWS, dtype=jnp.int32)
    col_ids = jnp.arange(COLS, dtype=jnp.int32)
    row_cos, row_sin = turn_table(row_ids, row_ids, ROWS)
    row_table = rounded(jnp.concatenate([jnp.concatenate([row_cos, -row_sin], 1), jnp.concatenate([row_sin, row_cos], 1)], 0))
    twiddle_cos, twiddle_sin = turn_table(row_ids, col_ids, total)
    col_cos, col_sin = turn_table(col_ids, col_ids, COLS)
    col_table = rounded(jnp.concatenate([jnp.concatenate([col_cos, col_sin], 1), jnp.concatenate([-col_sin, col_cos], 1)], 0))
    phase_cos, phase_sin = slide_phases(slides)
    data_re = strain[:, 0]
    data_im = strain[:, 1]

    def filter_one(template_id):
        waveform = lax.dynamic_index_in_dim(templates, template_id, 0, keepdims=False).astype(jnp.float32)
        cutoff = lax.dynamic_index_in_dim(cutoffs, template_id, 0, keepdims=False)
        inside = jnp.arange(total, dtype=jnp.int32) < cutoff
        wave_re = waveform[0]
        wave_im = waveform[1]
        real_part = data_re * wave_re + data_im * wave_im
        imag_part = data_im * wave_re - data_re * wave_im
        prod_re = jnp.where(inside, real_part * phase_cos - imag_part * phase_sin, jnp.float32(0.0))
        prod_im = jnp.where(inside, real_part * phase_sin + imag_part * phase_cos, jnp.float32(0.0))
        stacked = rounded(jnp.concatenate([prod_re.reshape(DET, ROWS, COLS), prod_im.reshape(DET, ROWS, COLS)], 1))
        section_one = jnp.einsum("ab,dbc->dac", row_table, stacked, precision=lax.Precision.HIGHEST)
        first_re = section_one[:, :ROWS]
        first_im = section_one[:, ROWS:]
        twisted = rounded(jnp.concatenate([first_re * twiddle_cos - first_im * twiddle_sin, first_re * twiddle_sin + first_im * twiddle_cos], 2))
        series = jnp.einsum("dab,bc->dac", twisted, col_table, precision=lax.Precision.HIGHEST)
        series_re = series[:, :, :COLS]
        series_im = series[:, :, COLS:]
        power_sum = jnp.sum(series_re * series_re + series_im * series_im, axis=0)
        sigmasq = jnp.sum(jnp.where(inside, wave_re * wave_re + wave_im * wave_im, jnp.float32(0.0)))
        return jnp.max(power_sum) / (2.0 * (sigmasq + eps_norm)), sigmasq / total

    peaks, norms = lax.map(filter_one, lists.reshape(-1).astype(jnp.int32))
    return peaks, norms
```

```python
import functools

import jax
import jax.numpy as jnp
import numpy as np
from jax import lax
from jax.experimental import pallas as pl
from jax.experimental.pallas import tpu as pltpu
from jax.sharding import PartitionSpec as P

DET = 3
ROWS = 512
COLS = 512
COL_BLOCK = 256
ROW_BLOCK = 128


two_pi = 6.283185307179586
eps_norm = 1e-06


def turn_table(left_ids, right_ids, period):
    angles = (left_ids[:, None] * right_ids[None, :] % period).astype(np.float64) * (2 * np.pi / period)
    return np.cos(angles), np.sin(angles)


def tables():
    row_ids, col_ids = np.arange(ROWS), np.arange(COLS)
    row_cos, row_sin = turn_table(row_ids, row_ids, ROWS)
    row_table = np.block([[row_cos, -row_sin], [row_sin, row_cos]])
    col_cos, col_sin = turn_table(col_ids, col_ids, COLS)
    col_table = np.block([[col_cos, col_sin], [-col_sin, col_cos]])
    twiddle = np.stack(turn_table(row_ids, col_ids, ROWS * COLS))
    return (
        jnp.asarray(row_table, jnp.float32).astype(jnp.bfloat16),
        jnp.asarray(col_table, jnp.float32).astype(jnp.bfloat16),
        jnp.asarray(twiddle, jnp.float32),
    )


def spread(block, axis, owner):
    block = jnp.where(lax.axis_index(axis) == owner, block, jnp.zeros_like(block))
    return lax.psum(block, axis)


def slide_turns(slides):
    total = ROWS * COLS
    row_turns = (jnp.arange(ROWS, dtype=jnp.int32)[None, :] * (COLS * slides % total)[:, None]) % total
    col_turns = (jnp.arange(COLS, dtype=jnp.int32)[None, :] * slides[:, None]) % total
    row_angles = row_turns.astype(jnp.float32) * (two_pi / total)
    col_angles = col_turns.astype(jnp.float32) * (two_pi / total)
    rows = jnp.stack([jnp.cos(row_angles), jnp.sin(row_angles)], 1)[..., None]
    cols = jnp.stack([jnp.cos(col_angles), jnp.sin(col_angles)], 1)[:, :, None, :]
    return rows, cols


def filter_kernel(cut_ref, strain_ref, wave_ref, rphase_ref, cphase_ref, row_ref, col_ref, twiddle_ref,
                  peaks_ref, norms_ref, slid, stacked, twisted, power, sigma):
    det, tpl = pl.program_id(0), pl.program_id(1)
    cutoff = cut_ref[tpl]

    @pl.when(tpl == 0)
    def _():
        rc, rs = rphase_ref[0, 0], rphase_ref[0, 1]
        cc, cs = cphase_ref[0, 0], cphase_ref[0, 1]
        for at in range(0, ROWS, ROW_BLOCK):
            rows = slice(at, at + ROW_BLOCK)
            turn_re = rc[rows] * cc - rs[rows] * cs
            turn_im = rc[rows] * cs + rs[rows] * cc
            data_re = strain_ref[0, 0, rows, :].astype(jnp.float32)
            data_im = strain_ref[0, 1, rows, :].astype(jnp.float32)
            slid[0, rows, :] = data_re * turn_re - data_im * turn_im
            slid[1, rows, :] = data_re * turn_im + data_im * turn_re

    def masked(rows, cols):
        bins = (lax.broadcasted_iota(jnp.int32, (ROW_BLOCK, COL_BLOCK), 0) + rows.start) * COLS
        bins = bins + lax.broadcasted_iota(jnp.int32, (ROW_BLOCK, COL_BLOCK), 1) + cols.start
        inside = bins < cutoff
        wave_re = jnp.where(inside, wave_ref[0, 0, rows, cols].astype(jnp.float32), 0.0)
        wave_im = jnp.where(inside, wave_ref[0, 1, rows, cols].astype(jnp.float32), 0.0)
        return wave_re, wave_im

    @pl.when(det == 0)
    def _():
        total = jnp.zeros((8, COL_BLOCK), jnp.float32)
        for row_at in range(0, ROWS, ROW_BLOCK):
            for col_at in range(0, COLS, COL_BLOCK):
                wave_re, wave_im = masked(slice(row_at, row_at + ROW_BLOCK), slice(col_at, col_at + COL_BLOCK))
                squares = wave_re * wave_re + wave_im * wave_im
                total = total + jnp.sum(squares.reshape(-1, 8, COL_BLOCK), axis=0)
        sigma[tpl] = jnp.sum(total)

    for col_at in range(0, COLS, COL_BLOCK):
        cols = slice(col_at, col_at + COL_BLOCK)
        for row_at in range(0, ROWS, ROW_BLOCK):
            rows = slice(row_at, row_at + ROW_BLOCK)
            wave_re, wave_im = masked(rows, cols)
            data_re, data_im = slid[0, rows, cols], slid[1, rows, cols]
            stacked[rows, cols] = (data_re * wave_re + data_im * wave_im).astype(jnp.bfloat16)
            low = slice(ROWS + row_at, ROWS + row_at + ROW_BLOCK)
            stacked[low, cols] = (data_im * wave_re - data_re * wave_im).astype(jnp.bfloat16)
        for row_at in range(0, ROWS, ROW_BLOCK):
            rows = slice(row_at, row_at + ROW_BLOCK)
            low = slice(ROWS + row_at, ROWS + row_at + ROW_BLOCK)
            first_re = jnp.dot(row_ref[rows, :], stacked[:, cols], preferred_element_type=jnp.float32)
            first_im = jnp.dot(row_ref[low, :], stacked[:, cols], preferred_element_type=jnp.float32)
            turn_re, turn_im = twiddle_ref[0, rows, cols], twiddle_ref[1, rows, cols]
            twisted[rows, cols] = (first_re * turn_re - first_im * turn_im).astype(jnp.bfloat16)
            right = slice(COLS + col_at, COLS + col_at + COL_BLOCK)
            twisted[rows, right] = (first_re * turn_im + first_im * turn_re).astype(jnp.bfloat16)

    for row_at in range(0, ROWS, ROW_BLOCK):
        rows = slice(row_at, row_at + ROW_BLOCK)
        series = jnp.dot(twisted[rows, :], col_ref[...], preferred_element_type=jnp.float32)
        series_re, series_im = series[:, :COLS], series[:, COLS:]
        squares = series_re * series_re + series_im * series_im

        @pl.when(det == 0)
        def _():
            power[tpl, rows, :] = squares

        @pl.when(det > 0)
        def _():
            power[tpl, rows, :] += squares

    @pl.when(det == DET - 1)
    def _():
        largest = jnp.max(power[tpl])
        peaks_ref[tpl] = largest / (2.0 * (sigma[tpl] + eps_norm))
        norms_ref[tpl] = sigma[tpl] / (ROWS * COLS)


def filtered(strain, waves, cutoffs, slides):
    count = waves.shape[0]
    rows, cols = slide_turns(slides)
    row_table, col_table, twiddle = tables()
    whole = lambda *shape: pl.BlockSpec(shape, lambda det, tpl: (0,) * len(shape))
    return pl.pallas_call(
        filter_kernel,
        grid=(DET, count),
        out_shape=(jax.ShapeDtypeStruct((count,), jnp.float32),) * 2,
        in_specs=[
            pl.BlockSpec(memory_space=pltpu.SMEM),
            pl.BlockSpec((1, 2, ROWS, COLS), lambda det, tpl: (det, 0, 0, 0)),
            pl.BlockSpec((1, 2, ROWS, COLS), lambda det, tpl: (tpl, 0, 0, 0)),
            pl.BlockSpec((1, 2, ROWS, 1), lambda det, tpl: (det, 0, 0, 0)),
            pl.BlockSpec((1, 2, 1, COLS), lambda det, tpl: (det, 0, 0, 0)),
            whole(2 * ROWS, 2 * ROWS),
            whole(2 * COLS, 2 * COLS),
            whole(2, ROWS, COLS),
        ],
        out_specs=(pl.BlockSpec(memory_space=pltpu.SMEM),) * 2,
        scratch_shapes=[
            pltpu.VMEM((2, ROWS, COLS), jnp.float32),
            pltpu.VMEM((2 * ROWS, COLS), jnp.bfloat16),
            pltpu.VMEM((ROWS, 2 * COLS), jnp.bfloat16),
            pltpu.VMEM((count, ROWS, COLS), jnp.float32),
            pltpu.SMEM((count,), jnp.float32),
        ],
        compiler_params=pltpu.CompilerParams(vmem_limit_bytes=48 * 1024 * 1024),
    )(cutoffs, strain, waves, rows, cols, row_table, col_table, twiddle)


def body(strain_slots, templates, cutoffs, lists, owner, slides):
    devices = lax.axis_size("tpl")
    own_index = lax.axis_index("tpl")
    per_device = lists.shape[1]
    strain = spread(strain_slots[0], "tpl", owner[0])
    picked = templates[lists.reshape(-1)]
    picked = picked.reshape(devices, per_device, 2, templates.shape[2])
    arrived = lax.all_to_all(picked, "tpl", split_axis=0, concat_axis=3, tiled=True)[0]
    own_ids = lax.dynamic_index_in_dim(lists, own_index, 0, keepdims=False)
    return filtered(
        strain.reshape(DET, 2, ROWS, COLS),
        arrived.reshape(per_device, 2, ROWS, COLS),
        cutoffs[own_ids],
        slides,
    )


def solution(mesh):
    in_specs = (
        P(("grp", "tpl"), None, None, None),
        P(None, None, "tpl"),
        P(),
        P(),
        P("grp"),
        P("grp"),
    )
    out_specs = (P(("grp", "tpl")), P(("grp", "tpl")))
    return jax.shard_map(body, mesh=mesh, in_specs=in_specs, out_specs=out_specs, check_vma=False)
```

```python
import functools

import jax
import jax.numpy as jnp
import numpy as np
from jax import lax
from jax.experimental import pallas as pl
from jax.experimental.pallas import tpu as pltpu
from jax.sharding import PartitionSpec as P

DET = 3
ROWS = 512
COLS = 512
COL_BLOCK = 256
ROW_BLOCK = 128
WAVE_ROWS = 32
HALF_CHUNKS = 4
LAG = 2
CORES = 2


two_pi = 6.283185307179586
eps_norm = 1e-06


def turn_table(left_ids, right_ids, period):
    angles = (left_ids[:, None] * right_ids[None, :] % period).astype(np.float64) * (2 * np.pi / period)
    return np.cos(angles), np.sin(angles)


def tables():
    row_ids, col_ids = np.arange(ROWS), np.arange(COLS)
    row_cos, row_sin = turn_table(row_ids, row_ids, ROWS)
    row_table = np.block([[row_cos, -row_sin], [row_sin, row_cos]])
    col_cos, col_sin = turn_table(col_ids, col_ids, COLS)
    col_table = np.block([[col_cos, col_sin], [-col_sin, col_cos]])
    twiddle = np.stack(turn_table(row_ids, col_ids, ROWS * COLS))
    return (
        jnp.asarray(row_table, jnp.float32).astype(jnp.bfloat16),
        jnp.asarray(col_table, jnp.float32).astype(jnp.bfloat16),
        jnp.asarray(twiddle, jnp.float32),
    )


def slide_turns(slides):
    total = ROWS * COLS
    row_turns = (jnp.arange(ROWS, dtype=jnp.int32)[None, :] * (COLS * slides % total)[:, None]) % total
    col_turns = (jnp.arange(COLS, dtype=jnp.int32)[None, :] * slides[:, None]) % total
    row_angles = row_turns.astype(jnp.float32) * (two_pi / total)
    col_angles = col_turns.astype(jnp.float32) * (two_pi / total)
    rows = jnp.stack([jnp.cos(row_angles), jnp.sin(row_angles)], 1)[..., None]
    cols = jnp.stack([jnp.cos(col_angles), jnp.sin(col_angles)], 1)[:, :, None, :]
    return rows, cols


def ring_order(chips):
    return list(range(0, chips, 2)) + list(range(chips - 1 - chips % 2, 0, -2))


def spread(own, owner):
    devices = lax.axis_size("tpl")
    chips = devices // CORES
    order = ring_order(chips)
    chip, core = lax.axis_index("tpl") // CORES, lax.axis_index("tpl") % CORES
    half = ROWS // CORES
    rows = half // HALF_CHUNKS
    to_partner = [(i, i ^ 1) for i in range(devices)]
    along = []
    for at in range(chips):
        along.append((order[at] * CORES, order[(at + 1) % chips] * CORES))
        along.append((order[(at + 1) % chips] * CORES + 1, order[at] * CORES + 1))
    on_owner_core = core == owner % CORES
    on_owner_chip = chip == owner // CORES
    chunks = []
    for det in range(DET):
        mine = lax.dynamic_slice_in_dim(own[det], core * half, half, 1)
        theirs = lax.dynamic_slice_in_dim(own[det], (1 - core) * half, half, 1)
        got = lax.ppermute(theirs, "tpl", to_partner)
        first = jnp.where(on_owner_core, mine, got)
        chunks += [first[:, rows * at : rows * (at + 1)] for at in range(HALF_CHUNKS)]
    sent, arrived = [], []
    count = len(chunks)
    for slot in range(count + LAG * (chips - 1)):
        if slot < LAG:
            here = chunks[slot]
        elif slot < count:
            here = jnp.where(on_owner_chip, chunks[slot], arrived[slot - LAG])
        else:
            here = arrived[slot - LAG]
        sent.append(here)
        if slot < count + LAG * (chips - 2):
            arrived.append(lax.ppermute(here, "tpl", along))
    shared = [lax.ppermute(here, "tpl", to_partner) for here in sent]
    place = lambda at: jnp.where(at % 2 == 0, at // 2, chips - 1 - at // 2)
    forward = (place(chip) - place(owner // CORES)) % chips
    backward = (place(owner // CORES) - place(chip)) % chips
    near = jnp.where(core == 0, forward, backward)
    far = jnp.where(core == 0, backward, forward)
    return sent, shared, jnp.stack([core, near, far]).astype(jnp.int32)


def collect(templates, lists):
    devices, groups = lax.axis_size("tpl"), lax.axis_size("grp")
    own_group = lax.axis_index("grp")
    per_device = lists.shape[1]
    bins = templates.shape[2]
    rows = bins // COLS
    pieces = per_device * 2
    if pieces % groups:
        groups, own_group = 1, 0
    size = pieces // groups
    whole_waves = size % 2 == 0
    if whole_waves:
        each = size // 2
        ids = lax.dynamic_slice_in_dim(lists, own_group * each, each, 1)
        picked = templates[ids.reshape(-1)].reshape(devices, each * 2, rows, COLS)
    else:
        picked = templates[lists.reshape(-1)].reshape(devices, pieces, rows, COLS)
        picked = lax.dynamic_slice_in_dim(picked, own_group * size, size, 1)
    own = lax.all_to_all(picked, "tpl", split_axis=0, concat_axis=0, tiled=True)
    found = [own]
    for turn in range(1, groups):
        found.append(lax.ppermute(own, "grp", [(i, (i + turn) % groups) for i in range(groups)]))
    if whole_waves and rows == WAVE_ROWS:
        waves, places = [], []
        for turn, block in enumerate(found):
            for at in range(each):
                waves.append(block[:, 2 * at : 2 * at + 2])
                places.append((own_group - turn) % groups * each + at)
        return waves, jnp.stack([jnp.asarray(place, jnp.int32) for place in places])
    found = jnp.stack(found)[(own_group - jnp.arange(groups)) % groups]
    found = found.transpose(0, 2, 1, 3, 4).reshape(per_device, 2, ROWS // WAVE_ROWS, WAVE_ROWS, COLS)
    return [found[at].transpose(1, 0, 2, 3) for at in range(per_device)], jnp.arange(per_device, dtype=jnp.int32)


def filter_kernel(chips, count, cut_ref, where_ref, *refs):
    slots = DET * HALF_CHUNKS + LAG * (chips - 1)
    near_refs, refs = refs[:slots], refs[slots:]
    far_refs, refs = refs[:slots], refs[slots:]
    wave_refs, refs = refs[:count], refs[count:]
    (rphase_ref, cphase_ref, row_hbm, col_hbm, twiddle_hbm, peaks_ref, norms_ref,
     strain_ref, wave_ref, row_ref, col_ref, twiddle_ref, slid, stacked, twisted, power, sigma,
     strain_sem, wave_sem, table_sem) = refs
    core, near, far = where_ref[0], where_ref[1], where_ref[2]
    half = ROWS // CORES
    rows = half // HALF_CHUNKS

    table_copies = [
        pltpu.make_async_copy(row_hbm, row_ref, table_sem.at[0]),
        pltpu.make_async_copy(twiddle_hbm, twiddle_ref, table_sem.at[1]),
        pltpu.make_async_copy(col_hbm, col_ref, table_sem.at[2]),
    ]
    wave_copies = [pltpu.make_async_copy(wave_refs[at], wave_ref.at[at], wave_sem.at[at]) for at in range(count)]

    def start_chunks(det):
        for slot_refs, distance, side in ((near_refs, near, core), (far_refs, far, 1 - core)):
            for away in range(chips):
                @pl.when(distance == away)
                def _():
                    for at in range(HALF_CHUNKS):
                        into = pl.ds(pl.multiple_of(side * half + at * rows, rows), rows)
                        copy = pltpu.make_async_copy(
                            slot_refs[det * HALF_CHUNKS + at + LAG * away],
                            strain_ref.at[det, :, into, :],
                            strain_sem.at[det],
                        )
                        copy.start()

    start_chunks(0)
    wave_copies[0].start()
    table_copies[0].start()
    table_copies[1].start()
    table_copies[2].start()
    for copy in wave_copies[1:]:
        copy.start()
    for det in range(1, DET):
        start_chunks(det)
    for copy in wave_copies:
        copy.wait()

    def wave(tpl, block, cutoff):
        bins = (lax.broadcasted_iota(jnp.int32, (WAVE_ROWS, COLS), 0) + block * WAVE_ROWS) * COLS
        bins = bins + lax.broadcasted_iota(jnp.int32, (WAVE_ROWS, COLS), 1)
        inside = bins < cutoff
        wave_re = jnp.where(inside, wave_ref[tpl, block, 0].astype(jnp.float32), 0.0)
        wave_im = jnp.where(inside, wave_ref[tpl, block, 1].astype(jnp.float32), 0.0)
        return wave_re, wave_im

    @pl.loop(0, count)
    def _(tpl):
        cutoff = cut_ref[tpl]
        total = jnp.zeros((8, COLS), jnp.float32)
        for block in range(ROWS // WAVE_ROWS):
            wave_re, wave_im = wave(tpl, block, cutoff)
            squares = wave_re * wave_re + wave_im * wave_im
            total = total + jnp.sum(squares.reshape(-1, 8, COLS), axis=0)
        sigma[tpl] = jnp.sum(total)
        power[tpl] = jnp.zeros((ROWS, COLS), jnp.float32)

    for copy in table_copies:
        copy.wait()

    @pl.loop(0, DET)
    def _(det):
        pltpu.make_async_copy(strain_ref.at[det], strain_ref.at[det], strain_sem.at[det]).wait()
        rc, rs = rphase_ref[det, 0], rphase_ref[det, 1]
        cc, cs = cphase_ref[det, 0], cphase_ref[det, 1]
        for at in range(0, ROWS, ROW_BLOCK):
            part = slice(at, at + ROW_BLOCK)
            turn_re = rc[part] * cc - rs[part] * cs
            turn_im = rc[part] * cs + rs[part] * cc
            data_re = strain_ref[det, 0, part, :].astype(jnp.float32)
            data_im = strain_ref[det, 1, part, :].astype(jnp.float32)
            slid[0, part, :] = data_re * turn_re - data_im * turn_im
            slid[1, part, :] = data_re * turn_im + data_im * turn_re

        @pl.loop(0, count)
        def _(tpl):
            cutoff = cut_ref[tpl]
            for block in range(ROWS // WAVE_ROWS):
                part = slice(block * WAVE_ROWS, block * WAVE_ROWS + WAVE_ROWS)
                wave_re, wave_im = wave(tpl, block, cutoff)
                data_re, data_im = slid[0, part, :], slid[1, part, :]
                stacked[part, :] = (data_re * wave_re + data_im * wave_im).astype(jnp.bfloat16)
                low = slice(ROWS + part.start, ROWS + part.stop)
                stacked[low, :] = (data_im * wave_re - data_re * wave_im).astype(jnp.bfloat16)
            for col_at in range(0, COLS, COL_BLOCK):
                cols = slice(col_at, col_at + COL_BLOCK)
                for row_at in range(0, ROWS, ROW_BLOCK):
                    part = slice(row_at, row_at + ROW_BLOCK)
                    low = slice(ROWS + row_at, ROWS + row_at + ROW_BLOCK)
                    first_re = jnp.dot(row_ref[part, :], stacked[:, cols], preferred_element_type=jnp.float32)
                    first_im = jnp.dot(row_ref[low, :], stacked[:, cols], preferred_element_type=jnp.float32)
                    turn_re, turn_im = twiddle_ref[0, part, cols], twiddle_ref[1, part, cols]
                    twisted[part, cols] = (first_re * turn_re - first_im * turn_im).astype(jnp.bfloat16)
                    right = slice(COLS + col_at, COLS + col_at + COL_BLOCK)
                    twisted[part, right] = (first_re * turn_im + first_im * turn_re).astype(jnp.bfloat16)
            for row_at in range(0, ROWS, ROW_BLOCK):
                part = slice(row_at, row_at + ROW_BLOCK)
                series = jnp.dot(twisted[part, :], col_ref[...], preferred_element_type=jnp.float32)
                series_re, series_im = series[:, :COLS], series[:, COLS:]
                power[tpl, part, :] += series_re * series_re + series_im * series_im

    for tpl in range(count):
        largest = jnp.max(power[tpl])
        peaks_ref[tpl] = largest / (2.0 * (sigma[tpl] + eps_norm))
        norms_ref[tpl] = sigma[tpl] / (ROWS * COLS)


def filtered(sent, shared, where, chips, waves, cutoffs, slides):
    count = len(waves)
    rows, cols = slide_turns(slides)
    row_table, col_table, twiddle = tables()
    smem = pl.BlockSpec(memory_space=pltpu.SMEM)
    vmem = pl.BlockSpec(memory_space=pltpu.VMEM)
    hbm = pl.BlockSpec(memory_space=pl.ANY)
    operands = [*sent, *shared, *waves]
    return pl.pallas_call(
        functools.partial(filter_kernel, chips, count),
        out_shape=(jax.ShapeDtypeStruct((count,), jnp.float32),) * 2,
        in_specs=[smem, smem] + [hbm] * len(operands) + [vmem, vmem, hbm, hbm, hbm],
        out_specs=(smem, smem),
        scratch_shapes=[
            pltpu.VMEM((DET, 2, ROWS, COLS), jnp.bfloat16),
            pltpu.VMEM((count, ROWS // WAVE_ROWS, 2, WAVE_ROWS, COLS), jnp.bfloat16),
            pltpu.VMEM((2 * ROWS, 2 * ROWS), jnp.bfloat16),
            pltpu.VMEM((2 * COLS, 2 * COLS), jnp.bfloat16),
            pltpu.VMEM((2, ROWS, COLS), jnp.float32),
            pltpu.VMEM((2, ROWS, COLS), jnp.float32),
            pltpu.VMEM((2 * ROWS, COLS), jnp.bfloat16),
            pltpu.VMEM((ROWS, 2 * COLS), jnp.bfloat16),
            pltpu.VMEM((count, ROWS, COLS), jnp.float32),
            pltpu.SMEM((count,), jnp.float32),
            pltpu.SemaphoreType.DMA((DET,)),
            pltpu.SemaphoreType.DMA((count,)),
            pltpu.SemaphoreType.DMA((3,)),
        ],
        compiler_params=pltpu.CompilerParams(vmem_limit_bytes=56 * 1024 * 1024),
    )(cutoffs, where, *operands, rows, cols, row_table, col_table, twiddle)


def body(strain_slots, templates, cutoffs, lists, owner, slides):
    devices = lax.axis_size("tpl")
    own_index = lax.axis_index("tpl")
    own = strain_slots[0].reshape(DET, 2, ROWS, COLS)
    sent, shared, where = spread(own, owner[0])
    waves, places = collect(templates, lists)
    own_ids = lax.dynamic_index_in_dim(lists, own_index, 0, keepdims=False)
    peaks, norms = filtered(sent, shared, where, devices // CORES, waves, cutoffs[own_ids[places]], slides)
    spot = places[:, None] == jnp.arange(len(waves))[None, :]
    return tuple(jnp.sum(jnp.where(spot, values[:, None], 0.0), axis=0) for values in (peaks, norms))


def solution(mesh):
    in_specs = (
        P(("grp", "tpl"), None, None, None),
        P(None, None, "tpl"),
        P(),
        P(),
        P("grp"),
        P("grp"),
    )
    out_specs = (P(("grp", "tpl")), P(("grp", "tpl")))
    return jax.shard_map(body, mesh=mesh, in_specs=in_specs, out_specs=out_specs, check_vma=False)
```

```python
import functools

import jax
import jax.numpy as jnp
import numpy as np
from jax import lax
from jax.experimental import pallas as pl
from jax.experimental.pallas import tpu as pltpu
from jax.sharding import PartitionSpec as P

DET = 3
ROWS = 512
COLS = 512
RADIX = 4
PART = 128
ROW_STEP = 16
WAVE_ROWS = 32
HALF_CHUNKS = 2
LAG = 2
CORES = 2


two_pi = 6.283185307179586
eps_norm = 1e-06


def turn_table(left_ids, right_ids, period):
    angles = (left_ids[:, None] * right_ids[None, :] % period).astype(np.float64) * (2 * np.pi / period)
    return np.cos(angles), np.sin(angles)


def tables():
    part_ids, col_ids = np.arange(PART), np.arange(COLS)
    row_tables, col_tables, turns = [], [], []
    for residue in range(RADIX):
        cos, sin = turn_table(RADIX * part_ids + residue, part_ids, ROWS)
        row_tables.append(np.block([[cos, -sin], [sin, cos]]))
        col_tables.append(np.block([[cos.T, sin.T], [-sin.T, cos.T]]))
        turns.append(np.stack(turn_table(RADIX * part_ids + residue, col_ids, ROWS * COLS)))
    return (
        jnp.asarray(np.stack(row_tables), jnp.float32).astype(jnp.bfloat16),
        jnp.asarray(np.stack(col_tables), jnp.float32).astype(jnp.bfloat16),
        jnp.asarray(np.stack(turns), jnp.float32),
    )


def slide_turns(slides):
    total = ROWS * COLS
    row_turns = (jnp.arange(ROWS, dtype=jnp.int32)[None, :] * (COLS * slides % total)[:, None]) % total
    col_turns = (jnp.arange(COLS, dtype=jnp.int32)[None, :] * slides[:, None]) % total
    row_angles = row_turns.astype(jnp.float32) * (two_pi / total)
    col_angles = col_turns.astype(jnp.float32) * (two_pi / total)
    rows = jnp.stack([jnp.cos(row_angles), jnp.sin(row_angles)], 1)[..., None]
    cols = jnp.stack([jnp.cos(col_angles), jnp.sin(col_angles)], 1)[:, :, None, :]
    return rows, cols


def ring_order(chips):
    return list(range(0, chips, 2)) + list(range(chips - 1 - chips % 2, 0, -2))


def spread(strain_slots, owner):
    devices = lax.axis_size("tpl")
    chips = devices // CORES
    order = ring_order(chips)
    chip, core = lax.axis_index("tpl") // CORES, lax.axis_index("tpl") % CORES
    half = ROWS * COLS // CORES
    bins = half // HALF_CHUNKS
    to_partner = [(i, i ^ 1) for i in range(devices)]
    along = []
    for at in range(chips):
        along.append((order[at] * CORES, order[(at + 1) % chips] * CORES))
        along.append((order[(at + 1) % chips] * CORES + 1, order[at] * CORES + 1))
    on_owner_core = core == owner % CORES
    on_owner_chip = chip == owner // CORES
    chunks = []
    for det in range(DET):
        side = lambda which: lax.dynamic_slice(strain_slots, (0, det, 0, which * half), (1, 1, 2, half))[0, 0]
        got = lax.ppermute(side(1 - core), "tpl", to_partner)
        first = jnp.where(on_owner_core, side(core), got)
        strain_slots, first = lax.optimization_barrier((strain_slots, first))
        for at in range(HALF_CHUNKS):
            chunks.append(first[:, bins * at : bins * (at + 1)].reshape(2, bins // COLS, COLS))
    sent, arrived = [], []
    count = len(chunks)
    for slot in range(count + LAG * (chips - 1)):
        if slot < LAG:
            here = chunks[slot]
        elif slot < count:
            here = jnp.where(on_owner_chip, chunks[slot], arrived[slot - LAG])
        else:
            here = arrived[slot - LAG]
        sent.append(here)
        if slot < count + LAG * (chips - 2):
            arrived.append(lax.ppermute(here, "tpl", along))
    shared = [lax.ppermute(here, "tpl", to_partner) for here in sent]
    place = lambda at: jnp.where(at % 2 == 0, at // 2, chips - 1 - at // 2)
    forward = (place(chip) - place(owner // CORES)) % chips
    backward = (place(owner // CORES) - place(chip)) % chips
    near = jnp.where(core == 0, forward, backward)
    far = jnp.where(core == 0, backward, forward)
    return sent, shared, [core, near, far]


def pick_kernel(list_ref, group_ref, templates_ref, picked_ref, sem):
    devices = picked_ref.shape[0]
    for device in range(devices):
        which = list_ref[device, group_ref[0]]
        pltpu.make_async_copy(templates_ref.at[which], picked_ref.at[device], sem).start()
    pltpu.make_async_copy(picked_ref, picked_ref, sem).wait()


def pick(templates, lists, own_group):
    devices = lists.shape[0]
    smem, hbm = pl.BlockSpec(memory_space=pltpu.SMEM), pl.BlockSpec(memory_space=pl.ANY)
    return pl.pallas_call(
        pick_kernel,
        out_shape=jax.ShapeDtypeStruct((devices, *templates.shape[1:]), templates.dtype),
        in_specs=[smem, smem, hbm],
        out_specs=hbm,
        scratch_shapes=[pltpu.SemaphoreType.DMA],
        compiler_params=pltpu.CompilerParams(vmem_limit_bytes=56 * 1024 * 1024),
    )(lists, own_group.reshape(1).astype(jnp.int32), templates)


def collect(templates, lists):
    devices, groups = lax.axis_size("tpl"), lax.axis_size("grp")
    own_group = lax.axis_index("grp")
    per_device = lists.shape[1]
    rows = templates.shape[2] // COLS
    pieces = per_device * 2
    if pieces % groups:
        groups, own_group = 1, jnp.int32(0)
    size = pieces // groups
    direct = size == 2 and rows == WAVE_ROWS
    if direct:
        picked = pick(templates, lists, own_group).reshape(devices, size, rows, COLS)
    else:
        picked = templates[lists.reshape(-1)].reshape(devices, pieces, rows, COLS)
        picked = lax.dynamic_slice_in_dim(picked, own_group * size, size, 1)
    own = lax.all_to_all(picked, "tpl", split_axis=0, concat_axis=0, tiled=True)
    found = [own]
    for turn in range(1, groups):
        found.append(lax.ppermute(own, "grp", [(i, (i + turn) % groups) for i in range(groups)]))
    if direct:
        return found, [(own_group - turn) % groups for turn in range(groups)]
    found = jnp.stack(found)[(own_group - jnp.arange(groups)) % groups]
    found = found.transpose(0, 2, 1, 3, 4).reshape(per_device, 2, ROWS // WAVE_ROWS, WAVE_ROWS, COLS)
    return [found[at].transpose(1, 0, 2, 3) for at in range(per_device)], [jnp.int32(at) for at in range(per_device)]


def held(values):
    return values.astype(jnp.bfloat16).astype(jnp.float32)


def quarters(parts):
    (re0, im0), (re1, im1), (re2, im2), (re3, im3) = parts
    even_re, even_im, odd_re, odd_im = re0 + re2, im0 + im2, re1 + re3, im1 + im3
    left_re, left_im, right_re, right_im = re0 - re2, im0 - im2, re1 - re3, im1 - im3
    return (
        (even_re + odd_re, even_im + odd_im),
        (left_re - right_im, left_im + right_re),
        (even_re - odd_re, even_im - odd_im),
        (left_re + right_im, left_im - right_re),
    )


def filter_kernel(chips, count, cut_ref, list_ref, where_ref, *refs):
    slots = DET * HALF_CHUNKS + LAG * (chips - 1)
    near_refs, refs = refs[:slots], refs[slots:]
    far_refs, refs = refs[:slots], refs[slots:]
    wave_refs, refs = refs[:count], refs[count:]
    (rphase_ref, cphase_ref, row_hbm, col_hbm, twiddle_hbm, peaks_ref, norms_ref,
     strain_ref, wave_ref, row_ref, col_ref, twiddle_ref, slid, masked, stacked, twisted, power, sigma,
     strain_sem, wave_sem, table_sem) = refs
    core, near, far, own = where_ref[0], where_ref[1], where_ref[2], where_ref[3]
    half = ROWS // CORES
    rows = half // HALF_CHUNKS

    table_copies = [
        pltpu.make_async_copy(row_hbm, row_ref, table_sem.at[0]),
        pltpu.make_async_copy(twiddle_hbm, twiddle_ref, table_sem.at[1]),
        pltpu.make_async_copy(col_hbm, col_ref, table_sem.at[2]),
    ]
    wave_copies = [pltpu.make_async_copy(wave_refs[at], wave_ref.at[at], wave_sem.at[at]) for at in range(count)]

    def start_chunks(det):
        for slot_refs, distance, side in ((near_refs, near, core), (far_refs, far, 1 - core)):
            for away in range(chips):
                @pl.when(distance == away)
                def _():
                    for at in range(HALF_CHUNKS):
                        into = pl.ds(pl.multiple_of(side * half + at * rows, rows), rows)
                        copy = pltpu.make_async_copy(
                            slot_refs[det * HALF_CHUNKS + at + LAG * away],
                            strain_ref.at[det, :, into, :],
                            strain_sem.at[det],
                        )
                        copy.start()

    for copy in wave_copies:
        copy.start()
    start_chunks(0)
    for copy in table_copies:
        copy.start()
    for det in range(1, DET):
        start_chunks(det)

    for tpl in range(count):
        wave_copies[tpl].wait()
        cutoff = cut_ref[list_ref[own, where_ref[4 + tpl]]]
        total = jnp.zeros((8, COLS), jnp.float32)
        for block in range(ROWS // WAVE_ROWS):
            bins = (lax.broadcasted_iota(jnp.int32, (WAVE_ROWS, COLS), 0) + block * WAVE_ROWS) * COLS
            bins = bins + lax.broadcasted_iota(jnp.int32, (WAVE_ROWS, COLS), 1)
            inside = bins < cutoff
            wave_re = jnp.where(inside, wave_ref[tpl, block, 0].astype(jnp.float32), 0.0)
            wave_im = jnp.where(inside, wave_ref[tpl, block, 1].astype(jnp.float32), 0.0)
            part = slice(block * WAVE_ROWS, (block + 1) * WAVE_ROWS)
            masked[tpl, 0, part, :] = wave_re.astype(jnp.bfloat16)
            masked[tpl, 1, part, :] = wave_im.astype(jnp.bfloat16)
            squares = wave_re * wave_re + wave_im * wave_im
            total = total + jnp.sum(squares.reshape(-1, 8, COLS), axis=0)
        sigma[tpl] = jnp.sum(total)

    for copy in table_copies:
        copy.wait()

    def one(det, tpl):
        for at in range(0, PART, ROW_STEP):
            for col_at in range(0, COLS, PART):
                cols = slice(col_at, col_at + PART)
                parts = []
                for quarter in range(RADIX):
                    spot = slice(quarter * PART + at, quarter * PART + at + ROW_STEP)
                    wave_re = masked[tpl, 0, spot, cols].astype(jnp.float32)
                    wave_im = masked[tpl, 1, spot, cols].astype(jnp.float32)
                    data_re, data_im = slid[0, spot, cols], slid[1, spot, cols]
                    parts.append((held(data_re * wave_re + data_im * wave_im), held(data_im * wave_re - data_re * wave_im)))
                for residue, (re, im) in enumerate(quarters(parts)):
                    stacked[residue, at : at + ROW_STEP, cols] = re.astype(jnp.bfloat16)
                    stacked[residue, PART + at : PART + at + ROW_STEP, cols] = im.astype(jnp.bfloat16)
        for residue in range(RADIX):
            section = jnp.dot(row_ref[residue], stacked[residue], preferred_element_type=jnp.float32)
            for at in range(0, PART, ROW_STEP):
                parts = []
                for quarter in range(RADIX):
                    cols = slice(quarter * PART, (quarter + 1) * PART)
                    re, im = section[at : at + ROW_STEP, cols], section[PART + at : PART + at + ROW_STEP, cols]
                    turn_re = twiddle_ref[residue, 0, at : at + ROW_STEP, cols]
                    turn_im = twiddle_ref[residue, 1, at : at + ROW_STEP, cols]
                    parts.append((held(re * turn_re - im * turn_im), held(re * turn_im + im * turn_re)))
                spot = slice(residue * PART + at, residue * PART + at + ROW_STEP)
                for other, (re, im) in enumerate(quarters(parts)):
                    twisted[other, spot, :PART] = re.astype(jnp.bfloat16)
                    twisted[other, spot, PART:] = im.astype(jnp.bfloat16)
        for other in range(RADIX):
            series = jnp.dot(twisted[other], col_ref[other], preferred_element_type=jnp.float32)
            squares = series[:, :PART] * series[:, :PART] + series[:, PART:] * series[:, PART:]
            cols = slice(other * PART, (other + 1) * PART)
            power[tpl, :, cols] = jnp.where(det == 0, squares, power[tpl, :, cols] + squares)

    @pl.loop(0, DET)
    def _(det):
        pltpu.make_async_copy(strain_ref.at[det], strain_ref.at[det], strain_sem.at[det]).wait()
        rc, rs = rphase_ref[det, 0], rphase_ref[det, 1]
        cc, cs = cphase_ref[det, 0], cphase_ref[det, 1]
        for at in range(0, ROWS, PART):
            part = slice(at, at + PART)
            turn_re = rc[part] * cc - rs[part] * cs
            turn_im = rc[part] * cs + rs[part] * cc
            data_re = strain_ref[det, 0, part, :].astype(jnp.float32)
            data_im = strain_ref[det, 1, part, :].astype(jnp.float32)
            slid[0, part, :] = data_re * turn_re - data_im * turn_im
            slid[1, part, :] = data_re * turn_im + data_im * turn_re

        @pl.loop(0, count)
        def _(tpl):
            one(det, tpl)

    for tpl in range(count):
        largest = jnp.max(power[tpl])
        place = where_ref[4 + tpl]
        peaks_ref[place] = largest / (2.0 * (sigma[tpl] + eps_norm))
        norms_ref[place] = sigma[tpl] / (ROWS * COLS)


def filtered(sent, shared, where, chips, waves, cutoffs, lists, turns):
    count = len(waves)
    rows, cols = turns
    row_table, col_table, twiddle = tables()
    smem = pl.BlockSpec(memory_space=pltpu.SMEM)
    vmem = pl.BlockSpec(memory_space=pltpu.VMEM)
    hbm = pl.BlockSpec(memory_space=pl.ANY)
    operands = [*sent, *shared, *waves]
    return pl.pallas_call(
        functools.partial(filter_kernel, chips, count),
        out_shape=(jax.ShapeDtypeStruct((count,), jnp.float32),) * 2,
        in_specs=[smem, smem, smem] + [hbm] * len(operands) + [vmem, vmem, hbm, hbm, hbm],
        out_specs=(smem, smem),
        scratch_shapes=[
            pltpu.VMEM((DET, 2, ROWS, COLS), jnp.bfloat16),
            pltpu.VMEM((count, ROWS // WAVE_ROWS, 2, WAVE_ROWS, COLS), jnp.bfloat16),
            pltpu.VMEM(row_table.shape, jnp.bfloat16),
            pltpu.VMEM(col_table.shape, jnp.bfloat16),
            pltpu.VMEM(twiddle.shape, jnp.float32),
            pltpu.VMEM((2, ROWS, COLS), jnp.float32),
            pltpu.VMEM((count, 2, ROWS, COLS), jnp.bfloat16),
            pltpu.VMEM((RADIX, 2 * PART, COLS), jnp.bfloat16),
            pltpu.VMEM((RADIX, ROWS, 2 * PART), jnp.bfloat16),
            pltpu.VMEM((count, ROWS, COLS), jnp.float32),
            pltpu.SMEM((count,), jnp.float32),
            pltpu.SemaphoreType.DMA((DET,)),
            pltpu.SemaphoreType.DMA((count,)),
            pltpu.SemaphoreType.DMA((3,)),
        ],
        compiler_params=pltpu.CompilerParams(vmem_limit_bytes=56 * 1024 * 1024),
    )(cutoffs, lists, where, *operands, rows, cols, row_table, col_table, twiddle)


def body(strain_slots, templates, cutoffs, lists, owner, slides):
    devices = lax.axis_size("tpl")
    sent, shared, where = spread(strain_slots, owner[0])
    waves, places = collect(templates, lists)
    where = jnp.stack([jnp.asarray(at, jnp.int32) for at in (*where, lax.axis_index("tpl"), *places)])
    return filtered(sent, shared, where, devices // CORES, waves, cutoffs, lists, slide_turns(slides))


def solution(mesh):
    in_specs = (
        P(("grp", "tpl"), None, None, None),
        P(None, None, "tpl"),
        P(),
        P(),
        P("grp"),
        P("grp"),
    )
    out_specs = (P(("grp", "tpl")), P(("grp", "tpl")))
    return jax.shard_map(body, mesh=mesh, in_specs=in_specs, out_specs=out_specs, check_vma=False)
```

```python
import functools

import jax
import jax.numpy as jnp
import numpy as np
from jax import lax
from jax.experimental import pallas as pl
from jax.experimental.pallas import tpu as pltpu
from jax.sharding import PartitionSpec as P

DET = 3
ROWS = 512
COLS = 512
RADIX = 4
PART = 128
ROW_STEP = 16
WAVE_ROWS = 32
HALF_CHUNKS = 2
LAG = 1
CORES = 2


two_pi = 6.283185307179586
eps_norm = 1e-06


def turn_table(left_ids, right_ids, period):
    angles = (left_ids[:, None] * right_ids[None, :] % period).astype(np.float64) * (2 * np.pi / period)
    return np.cos(angles), np.sin(angles)


def tables():
    part_ids, col_ids = np.arange(PART), np.arange(COLS)
    row_tables, col_tables, turns = [], [], []
    for residue in range(RADIX):
        cos, sin = turn_table(RADIX * part_ids + residue, part_ids, ROWS)
        row_tables.append(np.block([[cos, -sin], [sin, cos]]))
        col_tables.append(np.block([[cos.T, sin.T], [-sin.T, cos.T]]))
        turns.append(np.stack(turn_table(RADIX * part_ids + residue, col_ids, ROWS * COLS)))
    return (
        jnp.asarray(np.stack(row_tables), jnp.float32).astype(jnp.bfloat16),
        jnp.asarray(np.stack(col_tables), jnp.float32).astype(jnp.bfloat16),
        jnp.asarray(np.stack(turns), jnp.float32),
    )


def slide_turns(slides):
    total = ROWS * COLS
    row_turns = (jnp.arange(ROWS, dtype=jnp.int32)[None, :] * (COLS * slides % total)[:, None]) % total
    col_turns = (jnp.arange(COLS, dtype=jnp.int32)[None, :] * slides[:, None]) % total
    row_angles = row_turns.astype(jnp.float32) * (two_pi / total)
    col_angles = col_turns.astype(jnp.float32) * (two_pi / total)
    rows = jnp.stack([jnp.cos(row_angles), jnp.sin(row_angles)], 1)[..., None]
    cols = jnp.stack([jnp.cos(col_angles), jnp.sin(col_angles)], 1)[:, :, None, :]
    return rows, cols


def ring_order(chips):
    return list(range(0, chips, 2)) + list(range(chips - 1 - chips % 2, 0, -2))


def to_partner():
    return [(i, i ^ 1) for i in range(lax.axis_size("tpl"))]


def halves(strain_slots, owner):
    core = lax.axis_index("tpl") % CORES
    half = ROWS * COLS // CORES
    bins = half // HALF_CHUNKS
    on_owner_core = core == owner % CORES
    chunks = []
    for det in range(DET):
        side = lambda which: lax.dynamic_slice(strain_slots, (0, det, 0, which * half), (1, 1, 2, half))[0, 0]
        got = lax.ppermute(side(1 - core), "tpl", to_partner())
        first = jnp.where(on_owner_core, side(core), got)
        strain_slots, first = lax.optimization_barrier((strain_slots, first))
        for at in range(HALF_CHUNKS):
            chunks.append(first[:, bins * at : bins * (at + 1)].reshape(2, bins // COLS, COLS))
    return chunks


def spread(chunks, owner, early):
    devices = lax.axis_size("tpl")
    chips = devices // CORES
    order = ring_order(chips)
    chip, core = lax.axis_index("tpl") // CORES, lax.axis_index("tpl") % CORES
    on_owner_chip = chip == owner // CORES
    along = []
    for at in range(chips):
        along.append((order[at] * CORES, order[(at + 1) % chips] * CORES))
        along.append((order[(at + 1) % chips] * CORES + 1, order[at] * CORES + 1))
    sent, arrived = [], []
    count = len(chunks)
    for slot in range(count + LAG * (chips - 1)):
        if slot < LAG:
            here = chunks[slot]
        elif slot < count:
            here = jnp.where(on_owner_chip, chunks[slot], arrived[slot - LAG])
        else:
            here = arrived[slot - LAG]
        if slot == count // 2:
            here, early = lax.optimization_barrier((here, early))
        sent.append(here)
        if slot < count + LAG * (chips - 2):
            arrived.append(lax.ppermute(here, "tpl", along))
    shared = [lax.ppermute(here, "tpl", to_partner()) for here in sent]
    place = lambda at: jnp.where(at % 2 == 0, at // 2, chips - 1 - at // 2)
    forward = (place(chip) - place(owner // CORES)) % chips
    backward = (place(owner // CORES) - place(chip)) % chips
    near = jnp.where(core == 0, forward, backward)
    far = jnp.where(core == 0, backward, forward)
    return sent, shared, [core, near, far], early


def collect(templates, lists, first):
    devices, groups = lax.axis_size("tpl"), lax.axis_size("grp")
    own_group = lax.axis_index("grp")
    per_device = lists.shape[1]
    rows = templates.shape[2] // COLS
    pieces = per_device * 2
    if pieces % groups:
        groups, own_group = 1, jnp.int32(0)
    size = pieces // groups
    direct = size == 2 and rows == WAVE_ROWS
    if direct:
        picked = templates[lax.dynamic_index_in_dim(lists, own_group, 1, keepdims=False)]
        picked, first = lax.optimization_barrier((picked.reshape(devices, size, rows, COLS), first))
    else:
        picked = templates[lists.reshape(-1)].reshape(devices, pieces, rows, COLS)
        picked = lax.dynamic_slice_in_dim(picked, own_group * size, size, 1)
    own = lax.all_to_all(picked, "tpl", split_axis=0, concat_axis=0, tiled=True)
    found = [own]
    for turn in range(1, groups):
        found.append(lax.ppermute(own, "grp", [(i, (i + turn) % groups) for i in range(groups)]))
    if direct:
        return found, [(own_group - turn) % groups for turn in range(groups)], first
    found = jnp.stack(found)[(own_group - jnp.arange(groups)) % groups]
    found = found.transpose(0, 2, 1, 3, 4).reshape(per_device, 2, ROWS // WAVE_ROWS, WAVE_ROWS, COLS)
    found = [found[at].transpose(1, 0, 2, 3) for at in range(per_device)]
    return found, [jnp.int32(at) for at in range(per_device)], first


def held(values):
    scaled = values * 65537.0
    return scaled - (scaled - values)


def quarters(parts):
    (re0, im0), (re1, im1), (re2, im2), (re3, im3) = parts
    even_re, even_im, odd_re, odd_im = re0 + re2, im0 + im2, re1 + re3, im1 + im3
    left_re, left_im, right_re, right_im = re0 - re2, im0 - im2, re1 - re3, im1 - im3
    return (
        (even_re + odd_re, even_im + odd_im),
        (left_re - right_im, left_im + right_re),
        (even_re - odd_re, even_im - odd_im),
        (left_re + right_im, left_im - right_re),
    )


def filter_kernel(chips, count, cut_ref, list_ref, where_ref, *refs):
    slots = DET * HALF_CHUNKS + LAG * (chips - 1)
    near_refs, refs = refs[:slots], refs[slots:]
    far_refs, refs = refs[:slots], refs[slots:]
    wave_refs, refs = refs[:count], refs[count:]
    (rphase_ref, cphase_ref, row_hbm, col_hbm, twiddle_hbm, peaks_ref, norms_ref,
     strain_ref, wave_ref, row_ref, col_ref, twiddle_ref, slid, masked, stacked, twisted, power, sigma,
     strain_sem, wave_sem, table_sem) = refs
    core, near, far, own = where_ref[0], where_ref[1], where_ref[2], where_ref[3]
    half = ROWS // CORES
    rows = half // HALF_CHUNKS

    table_copies = [
        pltpu.make_async_copy(row_hbm, row_ref, table_sem.at[0]),
        pltpu.make_async_copy(twiddle_hbm, twiddle_ref, table_sem.at[1]),
        pltpu.make_async_copy(col_hbm, col_ref, table_sem.at[2]),
    ]
    wave_copies = [pltpu.make_async_copy(wave_refs[at], wave_ref.at[at], wave_sem.at[at]) for at in range(count)]

    def start_chunks(det):
        for slot_refs, distance, side in ((near_refs, near, core), (far_refs, far, 1 - core)):
            for away in range(chips):
                @pl.when(distance == away)
                def _():
                    for at in range(HALF_CHUNKS):
                        into = pl.ds(pl.multiple_of(side * half + at * rows, rows), rows)
                        copy = pltpu.make_async_copy(
                            slot_refs[det * HALF_CHUNKS + at + LAG * away],
                            strain_ref.at[det, :, into, :],
                            strain_sem.at[det],
                        )
                        copy.start()

    for copy in wave_copies:
        copy.start()
    start_chunks(0)
    for copy in table_copies:
        copy.start()
    for det in range(1, DET):
        start_chunks(det)

    for tpl in range(count):
        wave_copies[tpl].wait()
        cutoff = cut_ref[list_ref[own, where_ref[4 + tpl]]]
        total = jnp.zeros((8, COLS), jnp.float32)
        for block in range(ROWS // WAVE_ROWS):
            bins = (lax.broadcasted_iota(jnp.int32, (WAVE_ROWS, COLS), 0) + block * WAVE_ROWS) * COLS
            bins = bins + lax.broadcasted_iota(jnp.int32, (WAVE_ROWS, COLS), 1)
            inside = bins < cutoff
            wave_re = jnp.where(inside, wave_ref[tpl, block, 0].astype(jnp.float32), 0.0)
            wave_im = jnp.where(inside, wave_ref[tpl, block, 1].astype(jnp.float32), 0.0)
            part = slice(block * WAVE_ROWS, (block + 1) * WAVE_ROWS)
            masked[tpl, 0, part, :] = wave_re.astype(jnp.bfloat16)
            masked[tpl, 1, part, :] = wave_im.astype(jnp.bfloat16)
            squares = wave_re * wave_re + wave_im * wave_im
            total = total + jnp.sum(squares.reshape(-1, 8, COLS), axis=0)
        sigma[tpl] = jnp.sum(total)

    for copy in table_copies:
        copy.wait()

    def one(det, tpl):
        for at in range(0, PART, ROW_STEP):
            for col_at in range(0, COLS, PART):
                cols = slice(col_at, col_at + PART)
                parts = []
                for quarter in range(RADIX):
                    spot = slice(quarter * PART + at, quarter * PART + at + ROW_STEP)
                    wave_re = masked[tpl, 0, spot, cols].astype(jnp.float32)
                    wave_im = masked[tpl, 1, spot, cols].astype(jnp.float32)
                    data_re, data_im = slid[0, spot, cols], slid[1, spot, cols]
                    parts.append((held(data_re * wave_re + data_im * wave_im), held(data_im * wave_re - data_re * wave_im)))
                for residue, (re, im) in enumerate(quarters(parts)):
                    stacked[residue, at : at + ROW_STEP, cols] = re.astype(jnp.bfloat16)
                    stacked[residue, PART + at : PART + at + ROW_STEP, cols] = im.astype(jnp.bfloat16)
        for residue in range(RADIX):
            section = jnp.dot(row_ref[residue], stacked[residue], preferred_element_type=jnp.float32)
            for at in range(0, PART, ROW_STEP):
                parts = []
                for quarter in range(RADIX):
                    cols = slice(quarter * PART, (quarter + 1) * PART)
                    re, im = section[at : at + ROW_STEP, cols], section[PART + at : PART + at + ROW_STEP, cols]
                    turn_re = twiddle_ref[residue, 0, at : at + ROW_STEP, cols]
                    turn_im = twiddle_ref[residue, 1, at : at + ROW_STEP, cols]
                    parts.append((held(re * turn_re - im * turn_im), held(re * turn_im + im * turn_re)))
                spot = slice(residue * PART + at, residue * PART + at + ROW_STEP)
                for other, (re, im) in enumerate(quarters(parts)):
                    twisted[other, spot, :PART] = re.astype(jnp.bfloat16)
                    twisted[other, spot, PART:] = im.astype(jnp.bfloat16)
        for other in range(RADIX):
            series = jnp.dot(twisted[other], col_ref[other], preferred_element_type=jnp.float32)
            squares = series[:, :PART] * series[:, :PART] + series[:, PART:] * series[:, PART:]
            cols = slice(other * PART, (other + 1) * PART)
            power[tpl, :, cols] = jnp.where(det == 0, squares, power[tpl, :, cols] + squares)

    @pl.loop(0, DET)
    def _(det):
        pltpu.make_async_copy(strain_ref.at[det], strain_ref.at[det], strain_sem.at[det]).wait()
        rc, rs = rphase_ref[det, 0], rphase_ref[det, 1]
        cc, cs = cphase_ref[det, 0], cphase_ref[det, 1]
        for at in range(0, ROWS, PART):
            part = slice(at, at + PART)
            turn_re = rc[part] * cc - rs[part] * cs
            turn_im = rc[part] * cs + rs[part] * cc
            data_re = strain_ref[det, 0, part, :].astype(jnp.float32)
            data_im = strain_ref[det, 1, part, :].astype(jnp.float32)
            slid[0, part, :] = data_re * turn_re - data_im * turn_im
            slid[1, part, :] = data_re * turn_im + data_im * turn_re

        @pl.loop(0, count)
        def _(tpl):
            one(det, tpl)

    for tpl in range(count):
        largest = jnp.max(power[tpl])
        place = where_ref[4 + tpl]
        peaks_ref[place] = largest / (2.0 * (sigma[tpl] + eps_norm))
        norms_ref[place] = sigma[tpl] / (ROWS * COLS)


def filtered(sent, shared, where, chips, waves, cutoffs, lists, turns):
    count = len(waves)
    rows, cols = turns
    row_table, col_table, twiddle = tables()
    smem = pl.BlockSpec(memory_space=pltpu.SMEM)
    vmem = pl.BlockSpec(memory_space=pltpu.VMEM)
    hbm = pl.BlockSpec(memory_space=pl.ANY)
    operands = [*sent, *shared, *waves]
    return pl.pallas_call(
        functools.partial(filter_kernel, chips, count),
        out_shape=(jax.ShapeDtypeStruct((count,), jnp.float32),) * 2,
        in_specs=[smem, smem, smem] + [hbm] * len(operands) + [vmem, vmem, hbm, hbm, hbm],
        out_specs=(smem, smem),
        scratch_shapes=[
            pltpu.VMEM((DET, 2, ROWS, COLS), jnp.bfloat16),
            pltpu.VMEM((count, ROWS // WAVE_ROWS, 2, WAVE_ROWS, COLS), jnp.bfloat16),
            pltpu.VMEM(row_table.shape, jnp.bfloat16),
            pltpu.VMEM(col_table.shape, jnp.bfloat16),
            pltpu.VMEM(twiddle.shape, jnp.float32),
            pltpu.VMEM((2, ROWS, COLS), jnp.float32),
            pltpu.VMEM((count, 2, ROWS, COLS), jnp.bfloat16),
            pltpu.VMEM((RADIX, 2 * PART, COLS), jnp.bfloat16),
            pltpu.VMEM((RADIX, ROWS, 2 * PART), jnp.bfloat16),
            pltpu.VMEM((count, ROWS, COLS), jnp.float32),
            pltpu.SMEM((count,), jnp.float32),
            pltpu.SemaphoreType.DMA((DET,)),
            pltpu.SemaphoreType.DMA((count,)),
            pltpu.SemaphoreType.DMA((3,)),
        ],
        compiler_params=pltpu.CompilerParams(vmem_limit_bytes=56 * 1024 * 1024),
    )(cutoffs, lists, where, *operands, rows, cols, row_table, col_table, twiddle)


def body(strain_slots, templates, cutoffs, lists, owner, slides):
    devices = lax.axis_size("tpl")
    chunks = halves(strain_slots, owner[0])
    waves, places, chunks[1] = collect(templates, lists, chunks[1])
    sent, shared, where, turns = spread(chunks, owner[0], slide_turns(slides))
    where = jnp.stack([jnp.asarray(at, jnp.int32) for at in (*where, lax.axis_index("tpl"), *places)])
    return filtered(sent, shared, where, devices // CORES, waves, cutoffs, lists, turns)


def solution(mesh):
    in_specs = (
        P(("grp", "tpl"), None, None, None),
        P(None, None, "tpl"),
        P(),
        P(),
        P("grp"),
        P("grp"),
    )
    out_specs = (P(("grp", "tpl")), P(("grp", "tpl")))
    return jax.shard_map(body, mesh=mesh, in_specs=in_specs, out_specs=out_specs, check_vma=False)
```

```python
import functools

import jax
import jax.numpy as jnp
import numpy as np
from jax import lax
from jax.experimental import pallas as pl
from jax.experimental.pallas import tpu as pltpu
from jax.sharding import PartitionSpec as P

DET = 3
ROWS = 512
COLS = 512
RADIX = 4
PART = 128
ROW_STEP = 16
WAVE_ROWS = 32
CORES = 2
PAIR = 2
QUAD = CORES * PAIR
VMEM_LIMIT = 24 * 1024 * 1024


two_pi = 6.283185307179586
eps_norm = 1e-06


def turn_table(left_ids, right_ids, period):
    angles = (left_ids[:, None] * right_ids[None, :] % period).astype(np.float64) * (2 * np.pi / period)
    return np.cos(angles), np.sin(angles)


def tables():
    part_ids, col_ids = np.arange(PART), np.arange(COLS)
    row_tables, col_tables, turns = [], [], []
    for residue in range(RADIX):
        cos, sin = turn_table(RADIX * part_ids + residue, part_ids, ROWS)
        row_tables.append(np.block([[cos, -sin], [sin, cos]]))
        col_tables.append(np.block([[cos.T, sin.T], [-sin.T, cos.T]]))
        turns.append(np.stack(turn_table(RADIX * part_ids + residue, col_ids, ROWS * COLS)))
    return (
        jnp.asarray(np.stack(row_tables), jnp.float32).astype(jnp.bfloat16),
        jnp.asarray(np.stack(col_tables), jnp.float32).astype(jnp.bfloat16),
        jnp.asarray(np.stack(turns), jnp.float32),
    )


def slide_turns(slides):
    total = ROWS * COLS
    row_turns = (jnp.arange(ROWS, dtype=jnp.int32)[None, :] * (COLS * slides % total)[:, None]) % total
    col_turns = (jnp.arange(COLS, dtype=jnp.int32)[None, :] * slides[:, None]) % total
    row_angles = row_turns.astype(jnp.float32) * (two_pi / total)
    col_angles = col_turns.astype(jnp.float32) * (two_pi / total)
    rows = jnp.stack([jnp.cos(row_angles), jnp.sin(row_angles)], 1)[..., None]
    cols = jnp.stack([jnp.cos(col_angles), jnp.sin(col_angles)], 1)[:, :, None, :]
    return rows, cols


def partner(flip):
    return [(at, at ^ flip) for at in range(lax.axis_size("tpl"))]


def swap(block, flip):
    return lax.ppermute(block, "tpl", partner(flip))


def quarter_of(strain_slots, det, owner):
    me = lax.axis_index("tpl")
    core, chip = me % CORES, me // CORES % PAIR
    half = ROWS * COLS // CORES
    bins = half // PAIR
    side = lambda which: lax.dynamic_slice(strain_slots, (0, det, 0, which * half), (1, 1, 2, half))[0, 0]
    got = swap(side(1 - core), 1)
    kept = jnp.where(core == owner % CORES, side(core), got)
    got = swap(jnp.where(chip == 0, kept[:, bins:], kept[:, :bins]), CORES)
    kept = jnp.where(chip == 0, kept[:, :bins], kept[:, bins:])
    return jnp.where(chip == owner // CORES % PAIR, kept, got).reshape(2, ROWS // QUAD, COLS)


def along_line(quarter, owner):
    lines = lax.axis_size("tpl") // QUAD
    line, from_line = lax.axis_index("tpl") // QUAD, owner // QUAD
    if lines == 1:
        return quarter
    odd = line % 2 == 1
    quarter = jnp.where(line % 2 == from_line % 2, quarter, swap(quarter, QUAD))
    if lines == 2:
        return quarter
    rows = quarter.shape[1] // 2
    piece = jnp.where(odd, quarter[:, rows:], quarter[:, :rows])
    bit = 2
    while bit < lines:
        piece = jnp.where(line // bit % 2 == from_line // bit % 2, piece, swap(piece, bit * QUAD))
        bit *= 2
    other = swap(piece, QUAD)
    return jnp.concatenate([jnp.where(odd, other, piece), jnp.where(odd, piece, other)], 1)


def all_quarters(quarter):
    beside = swap(quarter, CORES)
    return quarter, beside, swap(quarter, 1), swap(beside, 1)


def collect(templates, lists, first):
    devices, groups = lax.axis_size("tpl"), lax.axis_size("grp")
    own_group = lax.axis_index("grp")
    per_device = lists.shape[1]
    rows = templates.shape[2] // COLS
    pieces = per_device * 2
    if pieces % groups:
        groups, own_group = 1, jnp.int32(0)
    size = pieces // groups
    direct = size == 2 and rows == WAVE_ROWS
    if direct:
        picked = templates[lax.dynamic_index_in_dim(lists, own_group, 1, keepdims=False)]
        picked, first = lax.optimization_barrier((picked.reshape(devices, size, rows, COLS), first))
    else:
        picked = templates[lists.reshape(-1)].reshape(devices, pieces, rows, COLS)
        picked = lax.dynamic_slice_in_dim(picked, own_group * size, size, 1)
    own = lax.all_to_all(picked, "tpl", split_axis=0, concat_axis=0, tiled=True)
    found = [own]
    for turn in range(1, groups):
        found.append(lax.ppermute(own, "grp", [(i, (i + turn) % groups) for i in range(groups)]))
    if direct:
        return found, [(own_group - turn) % groups for turn in range(groups)], first
    found = jnp.stack(found)[(own_group - jnp.arange(groups)) % groups]
    found = found.transpose(0, 2, 1, 3, 4).reshape(per_device, 2, ROWS // WAVE_ROWS, WAVE_ROWS, COLS)
    found = [found[at].transpose(1, 0, 2, 3) for at in range(per_device)]
    return found, [jnp.int32(at) for at in range(per_device)], first


def held(values):
    scaled = values * 65537.0
    return scaled - (scaled - values)


def quarters(parts):
    (re0, im0), (re1, im1), (re2, im2), (re3, im3) = parts
    even_re, even_im, odd_re, odd_im = re0 + re2, im0 + im2, re1 + re3, im1 + im3
    left_re, left_im, right_re, right_im = re0 - re2, im0 - im2, re1 - re3, im1 - im3
    return (
        (even_re + odd_re, even_im + odd_im),
        (left_re - right_im, left_im + right_re),
        (even_re - odd_re, even_im - odd_im),
        (left_re + right_im, left_im - right_re),
    )


def prepare_kernel(cut_ref, list_ref, where_ref, *refs):
    count = where_ref.shape[0] - 3
    wave_refs, (masked_ref, sigma_ref) = refs[:count], refs[count:]
    for tpl in range(count):
        cutoff = cut_ref[list_ref[where_ref[2], where_ref[3 + tpl]]]
        total = jnp.zeros((8, COLS), jnp.float32)
        for block in range(ROWS // WAVE_ROWS):
            bins = (lax.broadcasted_iota(jnp.int32, (WAVE_ROWS, COLS), 0) + block * WAVE_ROWS) * COLS
            bins = bins + lax.broadcasted_iota(jnp.int32, (WAVE_ROWS, COLS), 1)
            inside = bins < cutoff
            wave_re = jnp.where(inside, wave_refs[tpl][block, 0].astype(jnp.float32), 0.0)
            wave_im = jnp.where(inside, wave_refs[tpl][block, 1].astype(jnp.float32), 0.0)
            part = slice(block * WAVE_ROWS, (block + 1) * WAVE_ROWS)
            masked_ref[tpl, 0, part, :] = wave_re.astype(jnp.bfloat16)
            masked_ref[tpl, 1, part, :] = wave_im.astype(jnp.bfloat16)
            squares = wave_re * wave_re + wave_im * wave_im
            total = total + jnp.sum(squares.reshape(-1, 8, COLS), axis=0)
        sigma_ref[tpl] = jnp.sum(total)


def detector_kernel(det, where_ref, sigma_ref, *refs):
    first, last = det == 0, det == DET - 1
    quarter_refs, refs = refs[:QUAD], refs[QUAD:]
    masked, rphase_ref, cphase_ref, row_ref, col_ref, twiddle_ref = refs[:6]
    refs = refs[6:]
    before, refs = (None, refs) if first else (refs[0], refs[1:])
    outputs, (slid, stacked, twisted) = refs[:-3], refs[-3:]
    count = masked.shape[0]
    core, chip = where_ref[0], where_ref[1]
    half, rows = ROWS // CORES, ROWS // QUAD

    rc, rs = rphase_ref.at[det, 0], rphase_ref.at[det, 1]
    cc, cs = cphase_ref[det, 0], cphase_ref[det, 1]
    for which, quarter in enumerate(quarter_refs):
        of_core, of_chip = (core if which < 2 else 1 - core), (chip if which % 2 == 0 else 1 - chip)
        part = pl.ds(pl.multiple_of(of_core * half + of_chip * rows, rows), rows)
        turn_re = rc[part] * cc - rs[part] * cs
        turn_im = rc[part] * cs + rs[part] * cc
        data_re, data_im = quarter[0].astype(jnp.float32), quarter[1].astype(jnp.float32)
        slid[0, part, :] = data_re * turn_re - data_im * turn_im
        slid[1, part, :] = data_re * turn_im + data_im * turn_re

    largest = []
    for tpl in range(count):
        for at in range(0, PART, ROW_STEP):
            for col_at in range(0, COLS, PART):
                cols = slice(col_at, col_at + PART)
                parts = []
                for quarter in range(RADIX):
                    spot = slice(quarter * PART + at, quarter * PART + at + ROW_STEP)
                    wave_re = masked[tpl, 0, spot, cols].astype(jnp.float32)
                    wave_im = masked[tpl, 1, spot, cols].astype(jnp.float32)
                    data_re, data_im = slid[0, spot, cols], slid[1, spot, cols]
                    parts.append((held(data_re * wave_re + data_im * wave_im), held(data_im * wave_re - data_re * wave_im)))
                for residue, (re, im) in enumerate(quarters(parts)):
                    stacked[tpl, residue, at : at + ROW_STEP, cols] = re.astype(jnp.bfloat16)
                    stacked[tpl, residue, PART + at : PART + at + ROW_STEP, cols] = im.astype(jnp.bfloat16)
        for residue in range(RADIX):
            section = jnp.dot(row_ref[residue], stacked[tpl, residue], preferred_element_type=jnp.float32)
            for at in range(0, PART, ROW_STEP):
                parts = []
                for quarter in range(RADIX):
                    cols = slice(quarter * PART, (quarter + 1) * PART)
                    re, im = section[at : at + ROW_STEP, cols], section[PART + at : PART + at + ROW_STEP, cols]
                    turn_re = twiddle_ref[residue, 0, at : at + ROW_STEP, cols]
                    turn_im = twiddle_ref[residue, 1, at : at + ROW_STEP, cols]
                    parts.append((held(re * turn_re - im * turn_im), held(re * turn_im + im * turn_re)))
                spot = slice(residue * PART + at, residue * PART + at + ROW_STEP)
                for other, (re, im) in enumerate(quarters(parts)):
                    twisted[tpl, other, spot, :PART] = re.astype(jnp.bfloat16)
                    twisted[tpl, other, spot, PART:] = im.astype(jnp.bfloat16)
        peak = jnp.zeros((8, PART), jnp.float32)
        for other in range(RADIX):
            series = jnp.dot(twisted[tpl, other], col_ref[other], preferred_element_type=jnp.float32)
            squares = series[:, :PART] * series[:, :PART] + series[:, PART:] * series[:, PART:]
            cols = slice(other * PART, (other + 1) * PART)
            if not first:
                squares = squares + before[tpl, :, cols]
            if last:
                peak = jnp.maximum(peak, jnp.max(squares.reshape(-1, 8, PART), axis=0))
            else:
                outputs[0][tpl, :, cols] = squares
        largest.append(peak)

    if last:
        for tpl in range(count):
            place = where_ref[3 + tpl]
            outputs[0][place] = jnp.max(largest[tpl]) / (2.0 * (sigma_ref[tpl] + eps_norm))
            outputs[1][place] = sigma_ref[tpl] / (ROWS * COLS)


smem = pl.BlockSpec(memory_space=pltpu.SMEM)
vmem = pl.BlockSpec(memory_space=pltpu.VMEM)


def prepare(cutoffs, lists, where, waves):
    count = len(waves)
    return pl.pallas_call(
        prepare_kernel,
        out_shape=(
            jax.ShapeDtypeStruct((count, 2, ROWS, COLS), jnp.bfloat16),
            jax.ShapeDtypeStruct((count,), jnp.float32),
        ),
        in_specs=[smem, smem, smem] + [vmem] * count,
        out_specs=(vmem, smem),
        compiler_params=pltpu.CompilerParams(vmem_limit_bytes=VMEM_LIMIT),
        cost_estimate=pl.CostEstimate(flops=2_000_000_000, bytes_accessed=6_000_000, transcendentals=0),
    )(cutoffs, lists, where, *waves)


def detector(det, where, sigma, found, masked, turns, before):
    count = masked.shape[0]
    last = det == DET - 1
    scalars = jax.ShapeDtypeStruct((count,), jnp.float32)
    operands = [*found, masked, *turns, *tables(), *before]
    return pl.pallas_call(
        functools.partial(detector_kernel, det),
        out_shape=(scalars, scalars) if last else (jax.ShapeDtypeStruct((count, ROWS, COLS), jnp.float32),),
        in_specs=[smem, smem] + [vmem] * len(operands),
        out_specs=(smem, smem) if last else (vmem,),
        scratch_shapes=[
            pltpu.VMEM((2, ROWS, COLS), jnp.float32),
            pltpu.VMEM((count, RADIX, 2 * PART, COLS), jnp.bfloat16),
            pltpu.VMEM((count, RADIX, ROWS, 2 * PART), jnp.bfloat16),
        ],
        compiler_params=pltpu.CompilerParams(vmem_limit_bytes=VMEM_LIMIT),
        cost_estimate=pl.CostEstimate(flops=5_000_000_000, bytes_accessed=10_000_000, transcendentals=0),
    )(where, sigma, *operands)


def body(strain_slots, templates, cutoffs, lists, owner, slides):
    me, owner = lax.axis_index("tpl"), owner[0]
    quarter = [None] * DET
    turns = slide_turns(slides)
    for det in range(DET):
        quarter[det] = quarter_of(strain_slots, det, owner)
        if det == 0:
            waves, places, quarter[0] = collect(templates, lists, quarter[0])
        strain_slots, quarter[det] = lax.optimization_barrier((strain_slots, quarter[det]))
        if det == 1:
            turns, quarter[1] = lax.optimization_barrier((turns, quarter[1]))
    found = [all_quarters(along_line(part, owner)) for part in quarter]
    where = jnp.stack([jnp.asarray(at, jnp.int32) for at in (me % CORES, me // CORES % PAIR, me, *places)])
    masked, sigma = prepare(cutoffs, lists, where, waves)
    result = ()
    for det in range(DET):
        result = detector(det, where, sigma, found[det], masked, turns, result)
    return result


def solution(mesh):
    in_specs = (
        P(("grp", "tpl"), None, None, None),
        P(None, None, "tpl"),
        P(),
        P(),
        P("grp"),
        P("grp"),
    )
    out_specs = (P(("grp", "tpl")), P(("grp", "tpl")))
    return jax.shard_map(body, mesh=mesh, in_specs=in_specs, out_specs=out_specs, check_vma=False)
```

```python
import functools

import jax
import jax.numpy as jnp
import numpy as np
from jax import lax
from jax.experimental import pallas as pl
from jax.experimental.pallas import tpu as pltpu
from jax.sharding import PartitionSpec as P

DET = 3
ROWS = 512
COLS = 512
RADIX = 4
PART = 128
ROW_STEP = 16
WAVE_ROWS = 32
SEND_ROWS = 16
CORES = 2
PAIR = 2
QUAD = CORES * PAIR
VMEM_LIMIT = 24 * 1024 * 1024


two_pi = 6.283185307179586
eps_norm = 1e-06


def turn_table(left_ids, right_ids, period):
    angles = (left_ids[:, None] * right_ids[None, :] % period).astype(np.float64) * (2 * np.pi / period)
    return np.cos(angles), np.sin(angles)


def tables():
    part_ids, col_ids = np.arange(PART), np.arange(COLS)
    row_tables, col_tables, turns = [], [], []
    for residue in range(RADIX):
        cos, sin = turn_table(RADIX * part_ids + residue, part_ids, ROWS)
        row_tables.append(np.block([[cos, -sin], [sin, cos]]))
        col_tables.append(np.block([[cos.T, sin.T], [-sin.T, cos.T]] * 2))
        turns.append(np.stack(turn_table(RADIX * part_ids + residue, col_ids, ROWS * COLS)))
    return (
        jnp.asarray(np.stack(row_tables), jnp.float32).astype(jnp.bfloat16),
        jnp.asarray(np.stack(col_tables), jnp.float32).astype(jnp.bfloat16),
        jnp.asarray(np.stack(turns), jnp.float32),
    )


def slide_turns(slides):
    total = ROWS * COLS
    row_turns = (jnp.arange(ROWS, dtype=jnp.int32)[None, :] * (COLS * slides % total)[:, None]) % total
    col_turns = (jnp.arange(COLS, dtype=jnp.int32)[None, :] * slides[:, None]) % total
    row_angles = row_turns.astype(jnp.float32) * (two_pi / total)
    col_angles = col_turns.astype(jnp.float32) * (two_pi / total)
    rows = jnp.concatenate([jnp.cos(row_angles)[:, None], jnp.sin(row_angles)[:, None]] * 4, 1)
    cols = jnp.concatenate([jnp.cos(col_angles)[:, None], jnp.sin(col_angles)[:, None]] * 4, 1)
    return rows, cols


def partner(flip):
    return [(at, at ^ flip) for at in range(lax.axis_size("tpl"))]


def swap(block, flip):
    return lax.ppermute(block, "tpl", partner(flip))


def quarter_of(strain_slots, det, owner):
    me = lax.axis_index("tpl")
    core, chip = me % CORES, me // CORES % PAIR
    half = ROWS * COLS // CORES
    bins = half // PAIR
    side = lambda which: lax.dynamic_slice(strain_slots, (0, det, 0, which * half), (1, 1, 2, half))[0, 0]
    got = swap(side(1 - core), 1)
    kept = jnp.where(core == owner % CORES, side(core), got)
    got = swap(jnp.where(chip == 0, kept[:, bins:], kept[:, :bins]), CORES)
    kept = jnp.where(chip == 0, kept[:, :bins], kept[:, bins:])
    return jnp.where(chip == owner // CORES % PAIR, kept, got).reshape(2, ROWS // QUAD, COLS)


def along_line(quarter, owner):
    lines = lax.axis_size("tpl") // QUAD
    line, from_line = lax.axis_index("tpl") // QUAD, owner // QUAD
    if lines == 1:
        return quarter
    odd = line % 2 == 1
    quarter = jnp.where(line % 2 == from_line % 2, quarter, swap(quarter, QUAD))
    if lines == 2:
        return quarter
    rows = quarter.shape[1] // 2
    piece = jnp.where(odd, quarter[:, rows:], quarter[:, :rows])
    bit = 2
    while bit < lines:
        piece = jnp.where(line // bit % 2 == from_line // bit % 2, piece, swap(piece, bit * QUAD))
        bit *= 2
    other = swap(piece, QUAD)
    return jnp.concatenate([jnp.where(odd, other, piece), jnp.where(odd, piece, other)], 1)


def all_quarters(quarter):
    beside = swap(quarter, CORES)
    return quarter, beside, swap(quarter, 1), swap(beside, 1)


def pick(templates, lists):
    devices, groups = lax.axis_size("tpl"), lax.axis_size("grp")
    own_group = lax.axis_index("grp")
    per_device = lists.shape[1]
    rows = templates.shape[2] // COLS
    pieces = per_device * 2
    if pieces % groups:
        groups, own_group = 1, jnp.int32(0)
    size = pieces // groups
    if size == 2 and rows == WAVE_ROWS:
        picked = templates[lax.dynamic_index_in_dim(lists, own_group, 1, keepdims=False)]
        picked = picked.reshape(devices, size, rows, COLS)
        parts = [picked[:, :, at : at + SEND_ROWS] for at in range(0, rows, SEND_ROWS)]
        return parts, [(own_group - turn) % groups for turn in range(groups)]
    picked = templates[lists.reshape(-1)].reshape(devices, pieces, rows, COLS)
    return [lax.dynamic_slice_in_dim(picked, own_group * size, size, 1)], None


def exchange(block):
    return lax.all_to_all(block, "tpl", split_axis=0, concat_axis=0, tiled=True)


def across(own):
    groups = lax.axis_size("grp")
    return [own] + [
        lax.ppermute(own, "grp", [(at, (at + turn) % groups) for at in range(groups)]) for turn in range(1, groups)
    ]


def assemble(own, per_device):
    groups = lax.axis_size("grp")
    found = jnp.stack(across(own) if per_device * 2 % groups == 0 else [own])
    found = found[(lax.axis_index("grp") - jnp.arange(found.shape[0])) % found.shape[0]]
    found = found.transpose(0, 2, 1, 3, 4).reshape(per_device, 2, ROWS // WAVE_ROWS, WAVE_ROWS, COLS)
    return [[found[at].transpose(1, 0, 2, 3)] for at in range(per_device)]


def held(values):
    scaled = values * 65537.0
    return scaled - (scaled - values)


def quarters(parts):
    (re0, im0), (re1, im1), (re2, im2), (re3, im3) = parts
    even_re, even_im, odd_re, odd_im = re0 + re2, im0 + im2, re1 + re3, im1 + im3
    left_re, left_im, right_re, right_im = re0 - re2, im0 - im2, re1 - re3, im1 - im3
    return (
        (even_re + odd_re, even_im + odd_im),
        (left_re - right_im, left_im + right_re),
        (even_re - odd_re, even_im - odd_im),
        (left_re + right_im, left_im - right_re),
    )


def prepare_kernel(count, cut_ref, list_ref, where_ref, *refs):
    piece_refs, (masked_ref, sigma_ref) = refs[:-2], refs[-2:]
    pieces = len(piece_refs) // count
    rows = WAVE_ROWS // pieces
    for tpl in range(count):
        cutoff = cut_ref[list_ref[where_ref[2] * count + where_ref[3 + tpl]]]
        total = jnp.zeros((8, COLS), jnp.float32)
        for piece in range(pieces):
            wave_ref = piece_refs[tpl * pieces + piece]
            for block in range(ROWS // WAVE_ROWS):
                start = block * WAVE_ROWS + piece * rows
                bins = (lax.broadcasted_iota(jnp.int32, (rows, COLS), 0) + start) * COLS
                inside = bins + lax.broadcasted_iota(jnp.int32, (rows, COLS), 1) < cutoff
                wave_re = jnp.where(inside, wave_ref[block, 0].astype(jnp.float32), 0.0)
                wave_im = jnp.where(inside, wave_ref[block, 1].astype(jnp.float32), 0.0)
                masked_ref[tpl, 0, start : start + rows, :] = wave_re.astype(jnp.bfloat16)
                masked_ref[tpl, 1, start : start + rows, :] = wave_im.astype(jnp.bfloat16)
                squares = wave_re * wave_re + wave_im * wave_im
                total = total + jnp.sum(squares.reshape(-1, 8, COLS), axis=0)
        sigma_ref[tpl] = jnp.sum(total)


def detector_kernel(det, where_ref, sigma_ref, *refs):
    first, last = det == 0, det == DET - 1
    quarter_refs, refs = refs[:QUAD], refs[QUAD:]
    masked, rphase_ref, cphase_ref, row_ref, col_ref, twiddle_ref = refs[:6]
    refs = refs[6:]
    before, refs = (None, refs) if first else (refs[0], refs[1:])
    outputs, (turned_ref, slid, stacked, twisted) = refs[:-4], refs[-4:]
    count = masked.shape[0]
    core, chip = where_ref[0], where_ref[1]
    half, rows = ROWS // CORES, ROWS // QUAD

    turned_ref[...] = rphase_ref[det].T
    cc, cs = cphase_ref[det, 0:1, :], cphase_ref[det, 1:2, :]
    for which, quarter in enumerate(quarter_refs):
        of_core, of_chip = (core if which < 2 else 1 - core), (chip if which % 2 == 0 else 1 - chip)
        part = pl.ds(pl.multiple_of(of_core * half + of_chip * rows, rows), rows)
        rc, rs = turned_ref[part, 0:1], turned_ref[part, 1:2]
        turn_re = rc * cc - rs * cs
        turn_im = rc * cs + rs * cc
        data_re, data_im = quarter[0].astype(jnp.float32), quarter[1].astype(jnp.float32)
        slid[0, part, :] = data_re * turn_re - data_im * turn_im
        slid[1, part, :] = data_re * turn_im + data_im * turn_re

    largest = []
    for tpl in range(count):
        for at in range(0, PART, ROW_STEP):
            for col_at in range(0, COLS, PART):
                cols = slice(col_at, col_at + PART)
                parts = []
                for quarter in range(RADIX):
                    spot = slice(quarter * PART + at, quarter * PART + at + ROW_STEP)
                    wave_re = masked[tpl, 0, spot, cols].astype(jnp.float32)
                    wave_im = masked[tpl, 1, spot, cols].astype(jnp.float32)
                    data_re, data_im = slid[0, spot, cols], slid[1, spot, cols]
                    parts.append((held(data_re * wave_re + data_im * wave_im), held(data_im * wave_re - data_re * wave_im)))
                for residue, (re, im) in enumerate(quarters(parts)):
                    stacked[tpl, residue, at : at + ROW_STEP, cols] = re.astype(jnp.bfloat16)
                    stacked[tpl, residue, PART + at : PART + at + ROW_STEP, cols] = im.astype(jnp.bfloat16)
        for residue in range(RADIX):
            section = jnp.dot(row_ref[residue], stacked[tpl, residue], preferred_element_type=jnp.float32)
            for at in range(0, PART, ROW_STEP):
                parts = []
                for quarter in range(RADIX):
                    cols = slice(quarter * PART, (quarter + 1) * PART)
                    re, im = section[at : at + ROW_STEP, cols], section[PART + at : PART + at + ROW_STEP, cols]
                    turn_re = twiddle_ref[residue, 0, at : at + ROW_STEP, cols]
                    turn_im = twiddle_ref[residue, 1, at : at + ROW_STEP, cols]
                    parts.append((held(re * turn_re - im * turn_im), held(re * turn_im + im * turn_re)))
                spot = slice(residue * PART + at, residue * PART + at + ROW_STEP)
                for other, sums in enumerate(quarters(parts)):
                    for which, value in enumerate(sums):
                        high = value.astype(jnp.bfloat16)
                        low = (value - high.astype(jnp.float32)).astype(jnp.bfloat16)
                        twisted[tpl, other, spot, which * PART : (which + 1) * PART] = high
                        twisted[tpl, other, spot, (which + 2) * PART : (which + 3) * PART] = low
        peak = jnp.zeros((8, PART), jnp.float32)
        for other in range(RADIX):
            series = jnp.dot(twisted[tpl, other], col_ref[other], preferred_element_type=jnp.float32)
            squares = series[:, :PART] * series[:, :PART] + series[:, PART:] * series[:, PART:]
            cols = slice(other * PART, (other + 1) * PART)
            if not first:
                squares = squares + before[tpl, :, cols]
            if last:
                peak = jnp.maximum(peak, jnp.max(squares.reshape(-1, 8, PART), axis=0))
            else:
                outputs[0][tpl, :, cols] = squares
        largest.append(peak)

    if last:
        for tpl in range(count):
            place = where_ref[3 + tpl]
            outputs[0][place] = jnp.max(largest[tpl]) / (2.0 * (sigma_ref[tpl] + eps_norm))
            outputs[1][place] = sigma_ref[tpl] / (ROWS * COLS)


smem = pl.BlockSpec(memory_space=pltpu.SMEM)
vmem = pl.BlockSpec(memory_space=pltpu.VMEM)


def prepare(cutoffs, lists, where, waves):
    count = len(waves)
    operands = [piece for wave in waves for piece in wave]
    return pl.pallas_call(
        functools.partial(prepare_kernel, count),
        out_shape=(
            jax.ShapeDtypeStruct((count, 2, ROWS, COLS), jnp.bfloat16),
            jax.ShapeDtypeStruct((count,), jnp.float32),
        ),
        in_specs=[smem, smem, smem] + [vmem] * len(operands),
        out_specs=(vmem, smem),
        compiler_params=pltpu.CompilerParams(vmem_limit_bytes=VMEM_LIMIT),
        cost_estimate=pl.CostEstimate(flops=2_000_000_000, bytes_accessed=6_000_000, transcendentals=0),
    )(cutoffs, lists, where, *operands)


def detector(det, where, sigma, found, masked, turns, before):
    count = masked.shape[0]
    last = det == DET - 1
    scalars = jax.ShapeDtypeStruct((count,), jnp.float32)
    operands = [*found, masked, *turns, *tables(), *before]
    return pl.pallas_call(
        functools.partial(detector_kernel, det),
        out_shape=(scalars, scalars) if last else (jax.ShapeDtypeStruct((count, ROWS, COLS), jnp.float32),),
        in_specs=[smem, smem] + [vmem] * len(operands),
        out_specs=(smem, smem) if last else (vmem,),
        scratch_shapes=[
            pltpu.VMEM((ROWS, 8), jnp.float32),
            pltpu.VMEM((2, ROWS, COLS), jnp.float32),
            pltpu.VMEM((count, RADIX, 2 * PART, COLS), jnp.bfloat16),
            pltpu.VMEM((count, RADIX, ROWS, 4 * PART), jnp.bfloat16),
        ],
        compiler_params=pltpu.CompilerParams(vmem_limit_bytes=VMEM_LIMIT),
        cost_estimate=pl.CostEstimate(flops=5_000_000_000, bytes_accessed=10_000_000, transcendentals=0),
    )(where, sigma, *operands)


def body(strain_slots, templates, cutoffs, lists, owner, slides):
    me, owner = lax.axis_index("tpl"), owner[0]
    per_device = lists.shape[1]
    parts, places = pick(templates, lists)
    (strain_slots, parts) = lax.optimization_barrier((strain_slots, parts))
    ids = list(range(per_device)) if places is None else places
    where = jnp.stack([jnp.asarray(at, jnp.int32) for at in (me % CORES, me // CORES % PAIR, me, *ids)])
    small = (*slide_turns(slides), where, lists.reshape(-1))

    quarter = [quarter_of(strain_slots, 0, owner)]
    arrived = [exchange(parts[0])]
    strain_slots, quarter[0], small, arrived[0] = lax.optimization_barrier((strain_slots, quarter[0], small, arrived[0]))
    arrived += [exchange(part) for part in parts[1:]]
    for det in range(1, DET):
        quarter.append(quarter_of(strain_slots, det, owner))
        strain_slots, quarter[det] = lax.optimization_barrier((strain_slots, quarter[det]))
    quarter[1:], arrived[1:] = lax.optimization_barrier((quarter[1:], arrived[1:]))
    *turns, where, flat_list = small

    found = [all_quarters(along_line(part, owner)) for part in quarter]
    if places is None:
        waves = assemble(arrived[0], per_device)
    else:
        waves = [list(wave) for wave in zip(*[across(own) for own in arrived])]
    masked, sigma = prepare(cutoffs, flat_list, where, waves)
    result = ()
    for det in range(DET):
        result = detector(det, where, sigma, found[det], masked, turns, result)
    return result


def solution(mesh):
    in_specs = (
        P(("grp", "tpl"), None, None, None),
        P(None, None, "tpl"),
        P(),
        P(),
        P("grp"),
        P("grp"),
    )
    out_specs = (P(("grp", "tpl")), P(("grp", "tpl")))
    return jax.shard_map(body, mesh=mesh, in_specs=in_specs, out_specs=out_specs, check_vma=False)
```

```python
import functools

import jax
import jax.numpy as jnp
import numpy as np
from jax import lax
from jax.experimental import pallas as pl
from jax.experimental.pallas import tpu as pltpu
from jax.sharding import PartitionSpec as P

DET = 3
ROWS = 512
COLS = 512
RADIX = 4
PART = 128
ROW_STEP = 16
WAVE_ROWS = 32
SEND_ROWS = 32
CORES = 2
HALF_CHUNKS = 2
LAG = 2
TEMPLATE_SLOT = 4
MASKED_SLOT = 12
VMEM_LIMIT = 24 * 1024 * 1024


two_pi = 6.283185307179586
eps_norm = 1e-06


def turn_table(left_ids, right_ids, period):
    angles = (left_ids[:, None] * right_ids[None, :] % period).astype(np.float64) * (2 * np.pi / period)
    return np.cos(angles), np.sin(angles)


def tables():
    part_ids, col_ids = np.arange(PART), np.arange(COLS)
    row_tables, col_tables, turns = [], [], []
    for residue in range(RADIX):
        cos, sin = turn_table(RADIX * part_ids + residue, part_ids, ROWS)
        row_tables.append(np.block([[cos, -sin], [sin, cos]]))
        col_tables.append(np.block([[cos.T, sin.T], [-sin.T, cos.T]] * 2))
        turns.append(np.stack(turn_table(RADIX * part_ids + residue, col_ids, ROWS * COLS)))
    return (
        jnp.asarray(np.stack(row_tables), jnp.float32).astype(jnp.bfloat16),
        jnp.asarray(np.stack(col_tables), jnp.float32).astype(jnp.bfloat16),
        jnp.asarray(np.stack(turns), jnp.float32),
    )


def slide_turns(slides):
    total = ROWS * COLS
    row_turns = (jnp.arange(ROWS, dtype=jnp.int32)[None, :] * (COLS * slides % total)[:, None]) % total
    col_turns = (jnp.arange(COLS, dtype=jnp.int32)[None, :] * slides[:, None]) % total
    row_angles = row_turns.astype(jnp.float32) * (two_pi / total)
    col_angles = col_turns.astype(jnp.float32) * (two_pi / total)
    rows = jnp.concatenate([jnp.cos(row_angles)[:, None], jnp.sin(row_angles)[:, None]] * 4, 1)
    cols = jnp.concatenate([jnp.cos(col_angles)[:, None], jnp.sin(col_angles)[:, None]] * 4, 1)
    return rows, cols


def ring_order(chips):
    return list(range(0, chips, 2)) + list(range(chips - 1 - chips % 2, 0, -2))


def to_partner():
    return [(i, i ^ 1) for i in range(lax.axis_size("tpl"))]


def half_chunks(strain_slots, det, owner):
    core = lax.axis_index("tpl") % CORES
    half = ROWS * COLS // CORES
    bins = half // HALF_CHUNKS
    side = lambda which: lax.dynamic_slice(strain_slots, (0, det, 0, which * half), (1, 1, 2, half))[0, 0]
    got = lax.ppermute(side(1 - core), "tpl", to_partner())
    first = jnp.where(core == owner % CORES, side(core), got)
    return [first[:, at : at + bins].reshape(2, bins // COLS, COLS) for at in range(0, half, bins)]


def spread(chunks, owner, hooks):
    devices = lax.axis_size("tpl")
    chips = devices // CORES
    order = ring_order(chips)
    chip, core = lax.axis_index("tpl") // CORES, lax.axis_index("tpl") % CORES
    on_owner_chip = chip == owner // CORES
    along = []
    for at in range(chips):
        along.append((order[at] * CORES, order[(at + 1) % chips] * CORES))
        along.append((order[(at + 1) % chips] * CORES + 1, order[at] * CORES + 1))
    sent, arrived = [], []
    count = len(chunks)
    for slot in range(count + LAG * (chips - 1)):
        if slot < LAG:
            here = chunks[slot]
        elif slot < count:
            here = jnp.where(on_owner_chip, chunks[slot], arrived[slot - LAG])
        else:
            here = arrived[slot - LAG]
        if slot in hooks:
            here = hooks[slot](here)
        sent.append(here)
        if slot < count + LAG * (chips - 2):
            arrived.append(lax.ppermute(here, "tpl", along))
    shared = [lax.ppermute(here, "tpl", to_partner()) for here in sent]
    return sent, shared


def distances(owner):
    chips = lax.axis_size("tpl") // CORES
    chip, core = lax.axis_index("tpl") // CORES, lax.axis_index("tpl") % CORES
    place = lambda at: jnp.where(at % 2 == 0, at // 2, chips - 1 - at // 2)
    forward = (place(chip) - place(owner // CORES)) % chips
    backward = (place(owner // CORES) - place(chip)) % chips
    return jnp.where(core == 0, forward, backward), jnp.where(core == 0, backward, forward)


def pick(templates, lists):
    devices, groups = lax.axis_size("tpl"), lax.axis_size("grp")
    own_group = lax.axis_index("grp")
    per_device = lists.shape[1]
    rows = templates.shape[2] // COLS
    pieces = per_device * 2
    if pieces % groups:
        groups, own_group = 1, jnp.int32(0)
    size = pieces // groups
    if size == 2 and rows == WAVE_ROWS:
        picked = templates[lax.dynamic_index_in_dim(lists, own_group, 1, keepdims=False)]
        picked = picked.reshape(devices, size, rows, COLS)
        parts = [picked[:, :, at : at + SEND_ROWS] for at in range(0, rows, SEND_ROWS)]
        return parts, [(own_group - turn) % groups for turn in range(groups)]
    picked = templates[lists.reshape(-1)].reshape(devices, pieces, rows, COLS)
    return [lax.dynamic_slice_in_dim(picked, own_group * size, size, 1)], None


def exchange(block):
    return lax.all_to_all(block, "tpl", split_axis=0, concat_axis=0, tiled=True)


def across(own):
    groups = lax.axis_size("grp")
    return [own] + [
        lax.ppermute(own, "grp", [(at, (at + turn) % groups) for at in range(groups)]) for turn in range(1, groups)
    ]


def assemble(own, per_device):
    groups = lax.axis_size("grp")
    found = jnp.stack(across(own) if per_device * 2 % groups == 0 else [own])
    found = found[(lax.axis_index("grp") - jnp.arange(found.shape[0])) % found.shape[0]]
    found = found.transpose(0, 2, 1, 3, 4).reshape(per_device, 2, ROWS // WAVE_ROWS, WAVE_ROWS, COLS)
    return [[found[at].transpose(1, 0, 2, 3)] for at in range(per_device)]


def quarters(parts):
    (re0, im0), (re1, im1), (re2, im2), (re3, im3) = parts
    even_re, even_im, odd_re, odd_im = re0 + re2, im0 + im2, re1 + re3, im1 + im3
    left_re, left_im, right_re, right_im = re0 - re2, im0 - im2, re1 - re3, im1 - im3
    return (
        (even_re + odd_re, even_im + odd_im),
        (left_re - right_im, left_im + right_re),
        (even_re - odd_re, even_im - odd_im),
        (left_re + right_im, left_im - right_re),
    )


def prepare_kernel(count, cut_ref, list_ref, where_ref, *refs):
    piece_refs, (masked_ref, sigma_ref) = refs[:-2], refs[-2:]
    pieces = len(piece_refs) // count
    rows = WAVE_ROWS // pieces
    for tpl in range(count):
        cutoff = cut_ref[list_ref[where_ref[2] * count + where_ref[4 + tpl]]]
        total = jnp.zeros((8, COLS), jnp.float32)
        for piece in range(pieces):
            wave_ref = piece_refs[tpl * pieces + piece]
            for block in range(ROWS // WAVE_ROWS):
                start = block * WAVE_ROWS + piece * rows
                bins = (lax.broadcasted_iota(jnp.int32, (rows, COLS), 0) + start) * COLS
                inside = bins + lax.broadcasted_iota(jnp.int32, (rows, COLS), 1) < cutoff
                wave_re = jnp.where(inside, wave_ref[block, 0].astype(jnp.float32), 0.0)
                wave_im = jnp.where(inside, wave_ref[block, 1].astype(jnp.float32), 0.0)
                masked_ref[tpl, 0, start : start + rows, :] = wave_re.astype(jnp.bfloat16)
                masked_ref[tpl, 1, start : start + rows, :] = wave_im.astype(jnp.bfloat16)
                squares = wave_re * wave_re + wave_im * wave_im
                total = total + jnp.sum(squares.reshape(-1, 8, COLS), axis=0)
        sigma_ref[tpl] = jnp.sum(total)


def detector_kernel(det, chips, where_ref, sigma_ref, *refs):
    first, last = det == 0, det == DET - 1
    slots = HALF_CHUNKS + LAG * (chips - 1)
    near_refs, far_refs, refs = refs[:slots], refs[slots : 2 * slots], refs[2 * slots :]
    masked, rphase_ref, cphase_ref, row_ref, col_ref, twiddle_ref = refs[:6]
    refs = refs[6:]
    before, refs = (None, refs) if first else (refs[0], refs[1:])
    outputs, (strain_ref, strain_sem, turned_ref, slid, stacked, twisted) = refs[:-6], refs[-6:]
    count = masked.shape[0]
    core, near, far = where_ref[0], where_ref[1], where_ref[3]
    half = ROWS // CORES
    rows = half // HALF_CHUNKS

    for slot_refs, distance, side in ((near_refs, near, core), (far_refs, far, 1 - core)):
        for away in range(chips):
            @pl.when(distance == away)
            def _():
                for at in range(HALF_CHUNKS):
                    into = pl.ds(pl.multiple_of(side * half + at * rows, rows), rows)
                    pltpu.make_async_copy(slot_refs[at + LAG * away], strain_ref.at[:, into, :], strain_sem).start()
    turned_ref[...] = rphase_ref[det].T
    cc, cs = cphase_ref[det, 0:1, :], cphase_ref[det, 1:2, :]
    pltpu.make_async_copy(strain_ref, strain_ref, strain_sem).wait()
    for at in range(0, ROWS, PART):
        part = slice(at, at + PART)
        rc, rs = turned_ref[part, 0:1], turned_ref[part, 1:2]
        turn_re = rc * cc - rs * cs
        turn_im = rc * cs + rs * cc
        data_re, data_im = strain_ref[0, part, :].astype(jnp.float32), strain_ref[1, part, :].astype(jnp.float32)
        slid[0, part, :] = data_re * turn_re - data_im * turn_im
        slid[1, part, :] = data_re * turn_im + data_im * turn_re

    largest = []
    for tpl in range(count):
        for at in range(0, PART, ROW_STEP):
            for col_at in range(0, COLS, PART):
                cols = slice(col_at, col_at + PART)
                parts = []
                for quarter in range(RADIX):
                    spot = slice(quarter * PART + at, quarter * PART + at + ROW_STEP)
                    wave_re = masked[tpl, 0, spot, cols].astype(jnp.float32)
                    wave_im = masked[tpl, 1, spot, cols].astype(jnp.float32)
                    data_re, data_im = slid[0, spot, cols], slid[1, spot, cols]
                    parts.append((data_re * wave_re + data_im * wave_im, data_im * wave_re - data_re * wave_im))
                for residue, (re, im) in enumerate(quarters(parts)):
                    stacked[tpl, residue, at : at + ROW_STEP, cols] = re.astype(jnp.bfloat16)
                    stacked[tpl, residue, PART + at : PART + at + ROW_STEP, cols] = im.astype(jnp.bfloat16)
        for residue in range(RADIX):
            section = jnp.dot(row_ref[residue], stacked[tpl, residue], preferred_element_type=jnp.float32)
            for at in range(0, PART, ROW_STEP):
                parts = []
                for quarter in range(RADIX):
                    cols = slice(quarter * PART, (quarter + 1) * PART)
                    re, im = section[at : at + ROW_STEP, cols], section[PART + at : PART + at + ROW_STEP, cols]
                    turn_re = twiddle_ref[residue, 0, at : at + ROW_STEP, cols]
                    turn_im = twiddle_ref[residue, 1, at : at + ROW_STEP, cols]
                    parts.append((re * turn_re - im * turn_im, re * turn_im + im * turn_re))
                spot = slice(residue * PART + at, residue * PART + at + ROW_STEP)
                for other, sums in enumerate(quarters(parts)):
                    for which, value in enumerate(sums):
                        high = value.astype(jnp.bfloat16)
                        low = (value - high.astype(jnp.float32)).astype(jnp.bfloat16)
                        twisted[tpl, other, spot, which * PART : (which + 1) * PART] = high
                        twisted[tpl, other, spot, (which + 2) * PART : (which + 3) * PART] = low
        peak = jnp.zeros((8, PART), jnp.float32)
        for other in range(RADIX):
            series = jnp.dot(twisted[tpl, other], col_ref[other], preferred_element_type=jnp.float32)
            squares = series[:, :PART] * series[:, :PART] + series[:, PART:] * series[:, PART:]
            cols = slice(other * PART, (other + 1) * PART)
            if not first:
                squares = squares + before[tpl, :, cols]
            if last:
                peak = jnp.maximum(peak, jnp.max(squares.reshape(-1, 8, PART), axis=0))
            else:
                outputs[0][tpl, :, cols] = squares
        largest.append(peak)

    if last:
        for tpl in range(count):
            place = where_ref[4 + tpl]
            outputs[0][place] = jnp.max(largest[tpl]) / (2.0 * (sigma_ref[tpl] + eps_norm))
            outputs[1][place] = sigma_ref[tpl] / (ROWS * COLS)


smem = pl.BlockSpec(memory_space=pltpu.SMEM)
vmem = pl.BlockSpec(memory_space=pltpu.VMEM)
anywhere = pl.BlockSpec(memory_space=pl.ANY)


def prepare(cutoffs, lists, where, waves):
    count = len(waves)
    operands = [piece for wave in waves for piece in wave]
    return pl.pallas_call(
        functools.partial(prepare_kernel, count),
        out_shape=(
            jax.ShapeDtypeStruct((count, 2, ROWS, COLS), jnp.bfloat16),
            jax.ShapeDtypeStruct((count,), jnp.float32),
        ),
        in_specs=[smem, smem, smem] + [vmem] * len(operands),
        out_specs=(vmem, smem),
        compiler_params=pltpu.CompilerParams(vmem_limit_bytes=VMEM_LIMIT),
        cost_estimate=pl.CostEstimate(flops=2_000_000_000, bytes_accessed=6_000_000, transcendentals=0),
    )(cutoffs, lists, where, *operands)


def detector(det, chips, where, sigma, sent, shared, masked, turns, before):
    count = masked.shape[0]
    slots = slice(det * HALF_CHUNKS, (det + 1) * HALF_CHUNKS + LAG * (chips - 1))
    found = [*sent[slots], *shared[slots]]
    last = det == DET - 1
    scalars = jax.ShapeDtypeStruct((count,), jnp.float32)
    operands = [masked, *turns, *tables(), *before]
    return pl.pallas_call(
        functools.partial(detector_kernel, det, chips),
        out_shape=(scalars, scalars) if last else (jax.ShapeDtypeStruct((count, ROWS, COLS), jnp.float32),),
        in_specs=[smem, smem] + [anywhere] * len(found) + [vmem] * len(operands),
        out_specs=(smem, smem) if last else (vmem,),
        scratch_shapes=[
            pltpu.VMEM((2, ROWS, COLS), jnp.bfloat16),
            pltpu.SemaphoreType.DMA,
            pltpu.VMEM((ROWS, 8), jnp.float32),
            pltpu.VMEM((2, ROWS, COLS), jnp.float32),
            pltpu.VMEM((count, RADIX, 2 * PART, COLS), jnp.bfloat16),
            pltpu.VMEM((count, RADIX, ROWS, 4 * PART), jnp.bfloat16),
        ],
        compiler_params=pltpu.CompilerParams(vmem_limit_bytes=VMEM_LIMIT),
        cost_estimate=pl.CostEstimate(flops=5_000_000_000, bytes_accessed=10_000_000, transcendentals=0),
    )(where, sigma, *found, *operands)


def body(strain_slots, templates, cutoffs, lists, owner, slides):
    me, owner = lax.axis_index("tpl"), owner[0]
    chips = lax.axis_size("tpl") // CORES
    per_device = lists.shape[1]
    chunks = half_chunks(strain_slots, 0, owner)
    strain_slots, templates, chunks = lax.optimization_barrier((strain_slots, templates, chunks))
    parts, places = pick(templates, lists)
    ids = list(range(per_device)) if places is None else places
    near, far = distances(owner)
    where = jnp.stack([jnp.asarray(at, jnp.int32) for at in (me % CORES, near, me, far, *ids)])
    for det in range(1, DET):
        more = half_chunks(strain_slots, det, owner)
        strain_slots, more = lax.optimization_barrier((strain_slots, more))
        chunks += more
    held = {"arrived": exchange(parts[0]), "small": (slide_turns(slides), where, lists.reshape(-1))}

    def templates_here(chunk):
        chunk, held["arrived"], held["small"] = lax.optimization_barrier((chunk, held["arrived"], held["small"]))
        if places is None:
            waves = assemble(held["arrived"], per_device)
        else:
            waves = [[wave] for wave in across(held["arrived"])]
        _, where, flat_list = held["small"]
        held["masked"] = prepare(cutoffs, flat_list, where, waves)
        return chunk

    def masked_here(chunk):
        chunk, held["masked"] = lax.optimization_barrier((chunk, held["masked"]))
        return chunk

    sent, shared = spread(chunks, owner, {TEMPLATE_SLOT: templates_here, MASKED_SLOT: masked_here})
    turns, where, _ = held["small"]
    masked, sigma = held["masked"]
    result = ()
    for det in range(DET):
        result = detector(det, chips, where, sigma, sent, shared, masked, turns, result)
    return result


def solution(mesh):
    in_specs = (
        P(("grp", "tpl"), None, None, None),
        P(None, None, "tpl"),
        P(),
        P(),
        P("grp"),
        P("grp"),
    )
    out_specs = (P(("grp", "tpl")), P(("grp", "tpl")))
    return jax.shard_map(body, mesh=mesh, in_specs=in_specs, out_specs=out_specs, check_vma=False)
```

```python
import functools

import jax
import jax.numpy as jnp
import numpy as np
from jax import lax
from jax.experimental import pallas as pl
from jax.experimental.pallas import tpu as pltpu
from jax.sharding import PartitionSpec as P

DET = 3
ROWS = 512
COLS = 512
RADIX = 4
PART = 128
ROW_STEP = 16
WAVE_ROWS = 32
CORES = 2
HALF_CHUNKS = 2
LAG = 2
LINES = 4
QUAD = 4
STAGE_SLOTS = (6, 9, 14)
VMEM_LIMIT = 24 * 1024 * 1024


two_pi = 6.283185307179586
eps_norm = 1e-06


def turn_table(left_ids, right_ids, period):
    angles = (left_ids[:, None] * right_ids[None, :] % period).astype(np.float64) * (2 * np.pi / period)
    return np.cos(angles), np.sin(angles)


def tables():
    part_ids, col_ids = np.arange(PART), np.arange(COLS)
    row_tables, col_tables, turns = [], [], []
    for residue in range(RADIX):
        cos, sin = turn_table(RADIX * part_ids + residue, part_ids, ROWS)
        row_tables.append(np.block([[cos, -sin], [sin, cos]]))
        col_tables.append(np.block([[cos.T, sin.T], [-sin.T, cos.T]] * 2))
        turns.append(np.stack(turn_table(RADIX * part_ids + residue, col_ids, ROWS * COLS)))
    return (
        jnp.asarray(np.stack(row_tables), jnp.float32).astype(jnp.bfloat16),
        jnp.asarray(np.stack(col_tables), jnp.float32).astype(jnp.bfloat16),
        jnp.asarray(np.stack(turns), jnp.float32),
    )


def slide_turns(slides):
    total = ROWS * COLS
    row_turns = (jnp.arange(ROWS, dtype=jnp.int32)[None, :] * (COLS * slides % total)[:, None]) % total
    col_turns = (jnp.arange(COLS, dtype=jnp.int32)[None, :] * slides[:, None]) % total
    row_angles = row_turns.astype(jnp.float32) * (two_pi / total)
    col_angles = col_turns.astype(jnp.float32) * (two_pi / total)
    rows = jnp.concatenate([jnp.cos(row_angles)[:, None], jnp.sin(row_angles)[:, None]] * 4, 1)
    cols = jnp.concatenate([jnp.cos(col_angles)[:, None], jnp.sin(col_angles)[:, None]] * 4, 1)
    return rows, cols


def ring_order(chips):
    return list(range(0, chips, 2)) + list(range(chips - 1 - chips % 2, 0, -2))


def swap(block, flip):
    return lax.ppermute(block, "tpl", [(at, at ^ flip) for at in range(lax.axis_size("tpl"))])


def half_chunks(strain_slots, det, owner):
    core = lax.axis_index("tpl") % CORES
    half = ROWS * COLS // CORES
    bins = half // HALF_CHUNKS
    side = lambda which: lax.dynamic_slice(strain_slots, (0, det, 0, which * half), (1, 1, 2, half))[0, 0]
    got = swap(side(1 - core), 1)
    first = jnp.where(core == owner % CORES, side(core), got)
    return [first[:, at : at + bins].reshape(2, bins // COLS, COLS) for at in range(0, half, bins)]


def spread(chunks, owner, hooks):
    devices = lax.axis_size("tpl")
    chips = devices // CORES
    order = ring_order(chips)
    chip, core = lax.axis_index("tpl") // CORES, lax.axis_index("tpl") % CORES
    on_owner_chip = chip == owner // CORES
    along = []
    for at in range(chips):
        along.append((order[at] * CORES, order[(at + 1) % chips] * CORES))
        along.append((order[(at + 1) % chips] * CORES + 1, order[at] * CORES + 1))
    sent, shared, arrived = [], [], []
    count = len(chunks)
    for slot in range(count + LAG * (chips - 1)):
        if slot < LAG:
            here = chunks[slot]
        elif slot < count:
            here = jnp.where(on_owner_chip, chunks[slot], arrived[slot - LAG])
        else:
            here = arrived[slot - LAG]
        if slot in hooks:
            here = hooks[slot](here, sent, shared)
        sent.append(here)
        shared.append(swap(here, 1))
        if slot < count + LAG * (chips - 2):
            arrived.append(lax.ppermute(here, "tpl", along))
    return sent, shared


def distances(owner):
    chips = lax.axis_size("tpl") // CORES
    chip, core = lax.axis_index("tpl") // CORES, lax.axis_index("tpl") % CORES
    place = lambda at: jnp.where(at % 2 == 0, at // 2, chips - 1 - at // 2)
    forward = (place(chip) - place(owner // CORES)) % chips
    backward = (place(owner // CORES) - place(chip)) % chips
    return jnp.where(core == 0, forward, backward), jnp.where(core == 0, backward, forward)


def pick_direct(templates, lists):
    me, group = lax.axis_index("tpl"), lax.axis_index("grp")
    ids = lax.dynamic_index_in_dim(lists, group, 1, keepdims=False)[me ^ jnp.arange(LINES * QUAD)]
    return templates[ids].reshape(LINES, QUAD, 2, WAVE_ROWS, COLS)


def between_lines(picked):
    return [picked[0]] + [swap(picked[flip], flip * QUAD) for flip in range(1, LINES)]


def inside_quad(lines):
    blocks = [jnp.stack([line[flip] for line in lines]) for flip in range(QUAD)]
    return [blocks[0]] + [swap(blocks[flip], flip) for flip in range(1, QUAD)]


def across(block, turn):
    groups = lax.axis_size("grp")
    return lax.ppermute(block, "grp", [(at, (at + turn) % groups) for at in range(groups)]) if turn else block


def collect_plain(templates, lists):
    devices, groups = lax.axis_size("tpl"), lax.axis_size("grp")
    own_group = lax.axis_index("grp")
    per_device = lists.shape[1]
    pieces = per_device * 2
    if pieces % groups:
        groups, own_group = 1, 0
    size = pieces // groups
    picked = templates[lists.reshape(-1)].reshape(devices, pieces, templates.shape[2] // COLS, COLS)
    picked = lax.dynamic_slice_in_dim(picked, own_group * size, size, 1)
    own = lax.all_to_all(picked, "tpl", split_axis=0, concat_axis=0, tiled=True)
    found = jnp.stack([across(own, turn) for turn in range(groups)])[(own_group - jnp.arange(groups)) % groups]
    found = found.transpose(0, 2, 1, 3, 4).reshape(per_device, 2, ROWS // WAVE_ROWS, WAVE_ROWS, COLS)
    return [found[at].transpose(1, 0, 2, 3) for at in range(per_device)]


def quarters(parts):
    (re0, im0), (re1, im1), (re2, im2), (re3, im3) = parts
    even_re, even_im, odd_re, odd_im = re0 + re2, im0 + im2, re1 + re3, im1 + im3
    left_re, left_im, right_re, right_im = re0 - re2, im0 - im2, re1 - re3, im1 - im3
    return (
        (even_re + odd_re, even_im + odd_im),
        (left_re - right_im, left_im + right_re),
        (even_re - odd_re, even_im - odd_im),
        (left_re + right_im, left_im - right_re),
    )


def prepare_kernel(count, cut_ref, list_ref, where_ref, *refs):
    piece_refs, (masked_ref, sigma_ref) = refs[:-2], refs[-2:]
    pieces = len(piece_refs) // count
    flips = where_ref[4]
    for tpl in range(count):
        cutoff = cut_ref[list_ref[where_ref[2] * count + where_ref[5 + tpl]]]
        total = jnp.zeros((8, COLS), jnp.float32)
        for piece in range(pieces):
            wave_ref = piece_refs[tpl * pieces + piece]
            for block in range(ROWS // WAVE_ROWS // pieces):
                start = pl.multiple_of((flips ^ (block * pieces + piece)) * WAVE_ROWS, WAVE_ROWS)
                bins = (lax.broadcasted_iota(jnp.int32, (WAVE_ROWS, COLS), 0) + start) * COLS
                inside = bins + lax.broadcasted_iota(jnp.int32, (WAVE_ROWS, COLS), 1) < cutoff
                wave_re = jnp.where(inside, wave_ref[block, 0].astype(jnp.float32), 0.0)
                wave_im = jnp.where(inside, wave_ref[block, 1].astype(jnp.float32), 0.0)
                masked_ref[tpl, 0, pl.ds(start, WAVE_ROWS), :] = wave_re.astype(jnp.bfloat16)
                masked_ref[tpl, 1, pl.ds(start, WAVE_ROWS), :] = wave_im.astype(jnp.bfloat16)
                squares = wave_re * wave_re + wave_im * wave_im
                total = total + jnp.sum(squares.reshape(-1, 8, COLS), axis=0)
        sigma_ref[tpl] = jnp.sum(total)


def detector_kernel(det, chips, where_ref, sigma_ref, *refs):
    first, last = det == 0, det == DET - 1
    slots = HALF_CHUNKS + LAG * (chips - 1)
    near_refs, far_refs, refs = refs[:slots], refs[slots : 2 * slots], refs[2 * slots :]
    masked, rphase_ref, cphase_ref, row_ref, col_ref, twiddle_ref = refs[:6]
    refs = refs[6:]
    before, refs = (None, refs) if first else (refs[0], refs[1:])
    outputs, (strain_ref, strain_sem, turned_ref, slid, stacked, twisted) = refs[:-6], refs[-6:]
    count = masked.shape[0]
    core, near, far = where_ref[0], where_ref[1], where_ref[3]
    half = ROWS // CORES
    rows = half // HALF_CHUNKS

    for slot_refs, distance, side in ((near_refs, near, core), (far_refs, far, 1 - core)):
        for away in range(chips):
            @pl.when(distance == away)
            def _():
                for at in range(HALF_CHUNKS):
                    into = pl.ds(pl.multiple_of(side * half + at * rows, rows), rows)
                    pltpu.make_async_copy(slot_refs[at + LAG * away], strain_ref.at[:, into, :], strain_sem).start()
    turned_ref[...] = rphase_ref[det].T
    cc, cs = cphase_ref[det, 0:1, :], cphase_ref[det, 1:2, :]
    pltpu.make_async_copy(strain_ref, strain_ref, strain_sem).wait()
    for at in range(0, ROWS, PART):
        part = slice(at, at + PART)
        rc, rs = turned_ref[part, 0:1], turned_ref[part, 1:2]
        turn_re = rc * cc - rs * cs
        turn_im = rc * cs + rs * cc
        data_re, data_im = strain_ref[0, part, :].astype(jnp.float32), strain_ref[1, part, :].astype(jnp.float32)
        slid[0, part, :] = data_re * turn_re - data_im * turn_im
        slid[1, part, :] = data_re * turn_im + data_im * turn_re

    largest = []
    for tpl in range(count):
        for at in range(0, PART, ROW_STEP):
            for col_at in range(0, COLS, PART):
                cols = slice(col_at, col_at + PART)
                parts = []
                for quarter in range(RADIX):
                    spot = slice(quarter * PART + at, quarter * PART + at + ROW_STEP)
                    wave_re = masked[tpl, 0, spot, cols].astype(jnp.float32)
                    wave_im = masked[tpl, 1, spot, cols].astype(jnp.float32)
                    data_re, data_im = slid[0, spot, cols], slid[1, spot, cols]
                    parts.append((data_re * wave_re + data_im * wave_im, data_im * wave_re - data_re * wave_im))
                for residue, (re, im) in enumerate(quarters(parts)):
                    stacked[tpl, residue, at : at + ROW_STEP, cols] = re.astype(jnp.bfloat16)
                    stacked[tpl, residue, PART + at : PART + at + ROW_STEP, cols] = im.astype(jnp.bfloat16)
        for residue in range(RADIX):
            section = jnp.dot(row_ref[residue], stacked[tpl, residue], preferred_element_type=jnp.float32)
            for at in range(0, PART, ROW_STEP):
                parts = []
                for quarter in range(RADIX):
                    cols = slice(quarter * PART, (quarter + 1) * PART)
                    re, im = section[at : at + ROW_STEP, cols], section[PART + at : PART + at + ROW_STEP, cols]
                    turn_re = twiddle_ref[residue, 0, at : at + ROW_STEP, cols]
                    turn_im = twiddle_ref[residue, 1, at : at + ROW_STEP, cols]
                    parts.append((re * turn_re - im * turn_im, re * turn_im + im * turn_re))
                spot = slice(residue * PART + at, residue * PART + at + ROW_STEP)
                for other, sums in enumerate(quarters(parts)):
                    for which, value in enumerate(sums):
                        high = value.astype(jnp.bfloat16)
                        low = (value - high.astype(jnp.float32)).astype(jnp.bfloat16)
                        twisted[tpl, other, spot, which * PART : (which + 1) * PART] = high
                        twisted[tpl, other, spot, (which + 2) * PART : (which + 3) * PART] = low
        peak = jnp.zeros((8, PART), jnp.float32)
        for other in range(RADIX):
            series = jnp.dot(twisted[tpl, other], col_ref[other], preferred_element_type=jnp.float32)
            squares = series[:, :PART] * series[:, :PART] + series[:, PART:] * series[:, PART:]
            cols = slice(other * PART, (other + 1) * PART)
            if not first:
                squares = squares + before[tpl, :, cols]
            if last:
                peak = jnp.maximum(peak, jnp.max(squares.reshape(-1, 8, PART), axis=0))
            else:
                outputs[0][tpl, :, cols] = squares
        largest.append(peak)

    if last:
        for tpl in range(count):
            place = where_ref[5 + tpl]
            outputs[0][place] = jnp.max(largest[tpl]) / (2.0 * (sigma_ref[tpl] + eps_norm))
            outputs[1][place] = sigma_ref[tpl] / (ROWS * COLS)


smem = pl.BlockSpec(memory_space=pltpu.SMEM)
vmem = pl.BlockSpec(memory_space=pltpu.VMEM)
anywhere = pl.BlockSpec(memory_space=pl.ANY)


def prepare(cutoffs, lists, where, waves):
    count = len(waves)
    operands = [piece for wave in waves for piece in wave]
    return pl.pallas_call(
        functools.partial(prepare_kernel, count),
        out_shape=(
            jax.ShapeDtypeStruct((count, 2, ROWS, COLS), jnp.bfloat16),
            jax.ShapeDtypeStruct((count,), jnp.float32),
        ),
        in_specs=[smem, smem, smem] + [vmem] * len(operands),
        out_specs=(vmem, smem),
        compiler_params=pltpu.CompilerParams(vmem_limit_bytes=VMEM_LIMIT),
        cost_estimate=pl.CostEstimate(flops=2_000_000_000, bytes_accessed=6_000_000, transcendentals=0),
    )(cutoffs, lists, where, *operands)


def detector(det, chips, where, sigma, sent, shared, masked, turns, before):
    count = masked.shape[0]
    slots = slice(det * HALF_CHUNKS, (det + 1) * HALF_CHUNKS + LAG * (chips - 1))
    found = [*sent[slots], *shared[slots]]
    last = det == DET - 1
    scalars = jax.ShapeDtypeStruct((count,), jnp.float32)
    operands = [masked, *turns, *tables(), *before]
    return pl.pallas_call(
        functools.partial(detector_kernel, det, chips),
        out_shape=(scalars, scalars) if last else (jax.ShapeDtypeStruct((count, ROWS, COLS), jnp.float32),),
        in_specs=[smem, smem] + [anywhere] * len(found) + [vmem] * len(operands),
        out_specs=(smem, smem) if last else (vmem,),
        scratch_shapes=[
            pltpu.VMEM((2, ROWS, COLS), jnp.bfloat16),
            pltpu.SemaphoreType.DMA,
            pltpu.VMEM((ROWS, 8), jnp.float32),
            pltpu.VMEM((2, ROWS, COLS), jnp.float32),
            pltpu.VMEM((count, RADIX, 2 * PART, COLS), jnp.bfloat16),
            pltpu.VMEM((count, RADIX, ROWS, 4 * PART), jnp.bfloat16),
        ],
        compiler_params=pltpu.CompilerParams(vmem_limit_bytes=VMEM_LIMIT),
        cost_estimate=pl.CostEstimate(flops=5_000_000_000, bytes_accessed=10_000_000, transcendentals=0),
    )(where, sigma, *found, *operands)


def body(strain_slots, templates, cutoffs, lists, owner, slides):
    me, owner = lax.axis_index("tpl"), owner[0]
    devices, groups = lax.axis_size("tpl"), lax.axis_size("grp")
    chips = devices // CORES
    per_device = lists.shape[1]
    direct = per_device == groups and devices == LINES * QUAD and templates.shape[2] == WAVE_ROWS * COLS
    places = [(lax.axis_index("grp") - turn) % groups if direct else turn for turn in range(per_device)]

    chunks = half_chunks(strain_slots, 0, owner)
    strain_slots, templates, chunks = lax.optimization_barrier((strain_slots, templates, chunks))
    picked = pick_direct(templates, lists) if direct else collect_plain(templates, lists)
    near, far = distances(owner)
    numbers = (me % CORES, near, me, far, me if direct else 0, *places)
    where = jnp.stack([jnp.asarray(at, jnp.int32) for at in numbers])
    small = (*slide_turns(slides), where, lists.reshape(-1))
    for det in range(1, DET):
        more = half_chunks(strain_slots, det, owner)
        strain_slots, more = lax.optimization_barrier((strain_slots, more))
        chunks += more

    held = {"small": small, "lines": between_lines(picked) if direct else picked, "result": ()}

    def tie(name, chunk):
        chunk, held[name] = lax.optimization_barrier((chunk, held[name]))
        return chunk

    def after_lines(chunk, sent, shared):
        chunk = tie("small", tie("lines", chunk))
        held["blocks"] = inside_quad(held["lines"]) if direct else held["lines"]
        return chunk

    def after_blocks(chunk, sent, shared):
        chunk = tie("blocks", chunk)
        waves = [[across(block, turn) for block in held["blocks"]] for turn in range(per_device)]
        if not direct:
            waves = [[block] for block in held["blocks"]]
        *_, where, flat_list = held["small"]
        held["masked"] = prepare(cutoffs, flat_list, where, waves)
        return chunk

    def after_masked(chunk, sent, shared):
        return tie("masked", chunk)

    def filtered(det, sent, shared):
        *turns, where, _ = held["small"]
        masked, sigma = held["masked"]
        held["result"] = detector(det, chips, where, sigma, sent, shared, masked, turns, held["result"])

    def after_detector(det):
        def hook(chunk, sent, shared):
            filtered(det, sent, shared)
            return tie("result", chunk)

        return hook

    hooks = dict(zip(STAGE_SLOTS, (after_lines, after_blocks, after_masked)))
    for det in range(DET - 1):
        hooks[(det + 1) * HALF_CHUNKS - 1 + LAG * chips] = after_detector(det)
    sent, shared = spread(chunks, owner, hooks)
    filtered(DET - 1, sent, shared)
    return tuple(held["result"])


def solution(mesh):
    in_specs = (
        P(("grp", "tpl"), None, None, None),
        P(None, None, "tpl"),
        P(),
        P(),
        P("grp"),
        P("grp"),
    )
    out_specs = (P(("grp", "tpl")), P(("grp", "tpl")))
    return jax.shard_map(body, mesh=mesh, in_specs=in_specs, out_specs=out_specs, check_vma=False)
```

```python
import functools

import jax
import jax.numpy as jnp
import numpy as np
from jax import lax
from jax.experimental import pallas as pl
from jax.experimental.pallas import tpu as pltpu
from jax.sharding import PartitionSpec as P

DET = 3
ROWS = 512
COLS = 512
RADIX = 4
PART = 128
ROW_STEP = 16
WAVE_ROWS = 32
CORES = 2
HALF_CHUNKS = 2
LAG = 2
TEMPLATE_SLOT = 4
MASKED_SLOT = 12
VMEM_LIMIT = 24 * 1024 * 1024


two_pi = 6.283185307179586
eps_norm = 1e-06


def turn_table(left_ids, right_ids, period):
    angles = (left_ids[:, None] * right_ids[None, :] % period).astype(np.float64) * (2 * np.pi / period)
    return np.cos(angles), np.sin(angles)


def tables():
    part_ids, col_ids = np.arange(PART), np.arange(COLS)
    row_tables, col_tables, turns = [], [], []
    for residue in range(RADIX):
        cos, sin = turn_table(RADIX * part_ids + residue, part_ids, ROWS)
        row_tables.append(np.block([[cos, -sin], [sin, cos]]))
        col_tables.append(np.block([[cos.T, sin.T], [-sin.T, cos.T]] * 2))
        turns.append(np.stack(turn_table(RADIX * part_ids + residue, col_ids, ROWS * COLS)))
    return (
        jnp.asarray(np.stack(row_tables), jnp.float32).astype(jnp.bfloat16),
        jnp.asarray(np.stack(col_tables), jnp.float32).astype(jnp.bfloat16),
        jnp.asarray(np.stack(turns), jnp.float32),
    )


def slide_turns(slides):
    total = ROWS * COLS
    row_turns = (jnp.arange(ROWS, dtype=jnp.int32)[None, :] * (COLS * slides % total)[:, None]) % total
    col_turns = (jnp.arange(COLS, dtype=jnp.int32)[None, :] * slides[:, None]) % total
    row_angles = row_turns.astype(jnp.float32) * (two_pi / total)
    col_angles = col_turns.astype(jnp.float32) * (two_pi / total)
    rows = jnp.concatenate([jnp.cos(row_angles)[:, None], jnp.sin(row_angles)[:, None]] * 4, 1)
    cols = jnp.concatenate([jnp.cos(col_angles)[:, None], jnp.sin(col_angles)[:, None]] * 4, 1)
    return rows, cols


def ring_order(chips):
    return list(range(0, chips, 2)) + list(range(chips - 1 - chips % 2, 0, -2))


def swap(block, flip):
    return lax.ppermute(block, "tpl", [(at, at ^ flip) for at in range(lax.axis_size("tpl"))])


def half_chunks(strain_slots, det, owner):
    core = lax.axis_index("tpl") % CORES
    half = ROWS * COLS // CORES
    bins = half // HALF_CHUNKS
    side = lambda which: lax.dynamic_slice(strain_slots, (0, det, 0, which * half), (1, 1, 2, half))[0, 0]
    got = swap(side(1 - core), 1)
    first = jnp.where(core == owner % CORES, side(core), got)
    return [first[:, at : at + bins].reshape(2, bins // COLS, COLS) for at in range(0, half, bins)]


def spread(chunks, owner, hooks):
    devices = lax.axis_size("tpl")
    chips = devices // CORES
    order = ring_order(chips)
    chip, core = lax.axis_index("tpl") // CORES, lax.axis_index("tpl") % CORES
    on_owner_chip = chip == owner // CORES
    along = []
    for at in range(chips):
        along.append((order[at] * CORES, order[(at + 1) % chips] * CORES))
        along.append((order[(at + 1) % chips] * CORES + 1, order[at] * CORES + 1))
    sent, shared, arrived = [], [], []
    count = len(chunks)
    for slot in range(count + LAG * (chips - 1)):
        if slot < LAG:
            here = chunks[slot]
        elif slot < count:
            here = jnp.where(on_owner_chip, chunks[slot], arrived[slot - LAG])
        else:
            here = arrived[slot - LAG]
        if slot in hooks:
            here = hooks[slot](here, sent, shared)
        sent.append(here)
        shared.append(swap(here, 1))
        if slot < count + LAG * (chips - 2):
            arrived.append(lax.ppermute(here, "tpl", along))
    return sent, shared


def distances(owner):
    chips = lax.axis_size("tpl") // CORES
    chip, core = lax.axis_index("tpl") // CORES, lax.axis_index("tpl") % CORES
    place = lambda at: jnp.where(at % 2 == 0, at // 2, chips - 1 - at // 2)
    forward = (place(chip) - place(owner // CORES)) % chips
    backward = (place(owner // CORES) - place(chip)) % chips
    return jnp.where(core == 0, forward, backward), jnp.where(core == 0, backward, forward)


def collect(templates, lists):
    ids = lax.dynamic_index_in_dim(lists, lax.axis_index("grp"), 1, keepdims=False)
    return templates[ids].reshape(lists.shape[0], 2, WAVE_ROWS, COLS)


def exchange(block):
    return lax.all_to_all(block, "tpl", split_axis=0, concat_axis=0, tiled=True)


def across(block, turn):
    groups = lax.axis_size("grp")
    return lax.ppermute(block, "grp", [(at, (at + turn) % groups) for at in range(groups)]) if turn else block


def collect_plain(templates, lists):
    devices, groups = lax.axis_size("tpl"), lax.axis_size("grp")
    own_group = lax.axis_index("grp")
    per_device = lists.shape[1]
    pieces = per_device * 2
    if pieces % groups:
        groups, own_group = 1, 0
    size = pieces // groups
    picked = templates[lists.reshape(-1)].reshape(devices, pieces, templates.shape[2] // COLS, COLS)
    picked = lax.dynamic_slice_in_dim(picked, own_group * size, size, 1)
    own = exchange(picked)
    found = jnp.stack([across(own, turn) for turn in range(groups)])[(own_group - jnp.arange(groups)) % groups]
    found = found.transpose(0, 2, 1, 3, 4).reshape(per_device, 2, ROWS // WAVE_ROWS, WAVE_ROWS, COLS)
    return [found[at].transpose(1, 0, 2, 3) for at in range(per_device)]


def quarters(parts):
    (re0, im0), (re1, im1), (re2, im2), (re3, im3) = parts
    even_re, even_im, odd_re, odd_im = re0 + re2, im0 + im2, re1 + re3, im1 + im3
    left_re, left_im, right_re, right_im = re0 - re2, im0 - im2, re1 - re3, im1 - im3
    return (
        (even_re + odd_re, even_im + odd_im),
        (left_re - right_im, left_im + right_re),
        (even_re - odd_re, even_im - odd_im),
        (left_re + right_im, left_im - right_re),
    )


def prepare_kernel(count, cut_ref, list_ref, where_ref, *refs):
    wave_refs, (masked_ref, sigma_ref) = refs[:-2], refs[-2:]
    for tpl in range(count):
        cutoff = cut_ref[list_ref[where_ref[2] * count + where_ref[4 + tpl]]]
        total = jnp.zeros((8, COLS), jnp.float32)
        for block in range(ROWS // WAVE_ROWS):
            part = slice(block * WAVE_ROWS, (block + 1) * WAVE_ROWS)
            bins = (lax.broadcasted_iota(jnp.int32, (WAVE_ROWS, COLS), 0) + part.start) * COLS
            inside = bins + lax.broadcasted_iota(jnp.int32, (WAVE_ROWS, COLS), 1) < cutoff
            wave_re = jnp.where(inside, wave_refs[tpl][block, 0].astype(jnp.float32), 0.0)
            wave_im = jnp.where(inside, wave_refs[tpl][block, 1].astype(jnp.float32), 0.0)
            masked_ref[tpl, 0, part, :] = wave_re.astype(jnp.bfloat16)
            masked_ref[tpl, 1, part, :] = wave_im.astype(jnp.bfloat16)
            squares = wave_re * wave_re + wave_im * wave_im
            total = total + jnp.sum(squares.reshape(-1, 8, COLS), axis=0)
        sigma_ref[tpl] = jnp.sum(total)


def detector_kernel(det, chips, where_ref, sigma_ref, *refs):
    first, last = det == 0, det == DET - 1
    slots = HALF_CHUNKS + LAG * (chips - 1)
    near_refs, far_refs, refs = refs[:slots], refs[slots : 2 * slots], refs[2 * slots :]
    masked, rphase_ref, cphase_ref, row_ref, col_ref, twiddle_ref = refs[:6]
    refs = refs[6:]
    before, refs = (None, refs) if first else (refs[0], refs[1:])
    outputs, (strain_ref, strain_sem, turned_ref, slid, stacked, twisted) = refs[:-6], refs[-6:]
    count = masked.shape[0]
    core, near, far = where_ref[0], where_ref[1], where_ref[3]
    half = ROWS // CORES
    rows = half // HALF_CHUNKS

    for slot_refs, distance, side in ((near_refs, near, core), (far_refs, far, 1 - core)):
        for away in range(chips):
            @pl.when(distance == away)
            def _():
                for at in range(HALF_CHUNKS):
                    into = pl.ds(pl.multiple_of(side * half + at * rows, rows), rows)
                    pltpu.make_async_copy(slot_refs[at + LAG * away], strain_ref.at[:, into, :], strain_sem).start()
    turned_ref[...] = rphase_ref[det].T
    cc, cs = cphase_ref[det, 0:1, :], cphase_ref[det, 1:2, :]
    pltpu.make_async_copy(strain_ref, strain_ref, strain_sem).wait()
    for at in range(0, ROWS, PART):
        part = slice(at, at + PART)
        rc, rs = turned_ref[part, 0:1], turned_ref[part, 1:2]
        turn_re = rc * cc - rs * cs
        turn_im = rc * cs + rs * cc
        data_re, data_im = strain_ref[0, part, :].astype(jnp.float32), strain_ref[1, part, :].astype(jnp.float32)
        slid[0, part, :] = data_re * turn_re - data_im * turn_im
        slid[1, part, :] = data_re * turn_im + data_im * turn_re

    largest = []
    for tpl in range(count):
        for at in range(0, PART, ROW_STEP):
            for col_at in range(0, COLS, PART):
                cols = slice(col_at, col_at + PART)
                parts = []
                for quarter in range(RADIX):
                    spot = slice(quarter * PART + at, quarter * PART + at + ROW_STEP)
                    wave_re = masked[tpl, 0, spot, cols].astype(jnp.float32)
                    wave_im = masked[tpl, 1, spot, cols].astype(jnp.float32)
                    data_re, data_im = slid[0, spot, cols], slid[1, spot, cols]
                    parts.append((data_re * wave_re + data_im * wave_im, data_im * wave_re - data_re * wave_im))
                for residue, (re, im) in enumerate(quarters(parts)):
                    stacked[tpl, residue, at : at + ROW_STEP, cols] = re.astype(jnp.bfloat16)
                    stacked[tpl, residue, PART + at : PART + at + ROW_STEP, cols] = im.astype(jnp.bfloat16)
        for residue in range(RADIX):
            section = jnp.dot(row_ref[residue], stacked[tpl, residue], preferred_element_type=jnp.float32)
            for at in range(0, PART, ROW_STEP):
                parts = []
                for quarter in range(RADIX):
                    cols = slice(quarter * PART, (quarter + 1) * PART)
                    re, im = section[at : at + ROW_STEP, cols], section[PART + at : PART + at + ROW_STEP, cols]
                    turn_re = twiddle_ref[residue, 0, at : at + ROW_STEP, cols]
                    turn_im = twiddle_ref[residue, 1, at : at + ROW_STEP, cols]
                    parts.append((re * turn_re - im * turn_im, re * turn_im + im * turn_re))
                spot = slice(residue * PART + at, residue * PART + at + ROW_STEP)
                for other, sums in enumerate(quarters(parts)):
                    for which, value in enumerate(sums):
                        high = value.astype(jnp.bfloat16)
                        low = (value - high.astype(jnp.float32)).astype(jnp.bfloat16)
                        twisted[tpl, other, spot, which * PART : (which + 1) * PART] = high
                        twisted[tpl, other, spot, (which + 2) * PART : (which + 3) * PART] = low
        peak = jnp.zeros((8, PART), jnp.float32)
        for other in range(RADIX):
            series = jnp.dot(twisted[tpl, other], col_ref[other], preferred_element_type=jnp.float32)
            squares = series[:, :PART] * series[:, :PART] + series[:, PART:] * series[:, PART:]
            cols = slice(other * PART, (other + 1) * PART)
            if not first:
                squares = squares + before[tpl, :, cols]
            if last:
                peak = jnp.maximum(peak, jnp.max(squares.reshape(-1, 8, PART), axis=0))
            else:
                outputs[0][tpl, :, cols] = squares
        largest.append(peak)

    if last:
        for tpl in range(count):
            place = where_ref[4 + tpl]
            outputs[0][place] = jnp.max(largest[tpl]) / (2.0 * (sigma_ref[tpl] + eps_norm))
            outputs[1][place] = sigma_ref[tpl] / (ROWS * COLS)


smem = pl.BlockSpec(memory_space=pltpu.SMEM)
vmem = pl.BlockSpec(memory_space=pltpu.VMEM)
anywhere = pl.BlockSpec(memory_space=pl.ANY)


def prepare(cutoffs, lists, where, waves):
    count = len(waves)
    return pl.pallas_call(
        functools.partial(prepare_kernel, count),
        out_shape=(
            jax.ShapeDtypeStruct((count, 2, ROWS, COLS), jnp.bfloat16),
            jax.ShapeDtypeStruct((count,), jnp.float32),
        ),
        in_specs=[smem, smem, smem] + [vmem] * count,
        out_specs=(vmem, smem),
        compiler_params=pltpu.CompilerParams(vmem_limit_bytes=VMEM_LIMIT),
        cost_estimate=pl.CostEstimate(flops=2_000_000_000, bytes_accessed=6_000_000, transcendentals=0),
    )(cutoffs, lists, where, *waves)


def detector(det, chips, where, sigma, sent, shared, masked, turns, before):
    count = masked.shape[0]
    slots = slice(det * HALF_CHUNKS, (det + 1) * HALF_CHUNKS + LAG * (chips - 1))
    found = [*sent[slots], *shared[slots]]
    last = det == DET - 1
    scalars = jax.ShapeDtypeStruct((count,), jnp.float32)
    operands = [masked, *turns, *tables(), *before]
    return pl.pallas_call(
        functools.partial(detector_kernel, det, chips),
        out_shape=(scalars, scalars) if last else (jax.ShapeDtypeStruct((count, ROWS, COLS), jnp.float32),),
        in_specs=[smem, smem] + [anywhere] * len(found) + [vmem] * len(operands),
        out_specs=(smem, smem) if last else (vmem,),
        scratch_shapes=[
            pltpu.VMEM((2, ROWS, COLS), jnp.bfloat16),
            pltpu.SemaphoreType.DMA,
            pltpu.VMEM((ROWS, 8), jnp.float32),
            pltpu.VMEM((2, ROWS, COLS), jnp.float32),
            pltpu.VMEM((count, RADIX, 2 * PART, COLS), jnp.bfloat16),
            pltpu.VMEM((count, RADIX, ROWS, 4 * PART), jnp.bfloat16),
        ],
        compiler_params=pltpu.CompilerParams(vmem_limit_bytes=VMEM_LIMIT),
        cost_estimate=pl.CostEstimate(flops=5_000_000_000, bytes_accessed=10_000_000, transcendentals=0),
    )(where, sigma, *found, *operands)


def body(strain_slots, templates, cutoffs, lists, owner, slides):
    me, owner = lax.axis_index("tpl"), owner[0]
    devices, groups = lax.axis_size("tpl"), lax.axis_size("grp")
    chips = devices // CORES
    per_device = lists.shape[1]
    direct = per_device == groups and templates.shape[2] == WAVE_ROWS * COLS
    places = [(lax.axis_index("grp") - turn) % groups if direct else turn for turn in range(per_device)]

    picked = collect(templates, lists) if direct else collect_plain(templates, lists)
    strain_slots, picked = lax.optimization_barrier((strain_slots, picked))
    chunks = []
    for det in range(DET):
        more = half_chunks(strain_slots, det, owner)
        strain_slots, more = lax.optimization_barrier((strain_slots, more))
        chunks += more
    near, far = distances(owner)
    where = jnp.stack([jnp.asarray(at, jnp.int32) for at in (me % CORES, near, me, far, *places)])
    small = (*slide_turns(slides), where, lists.reshape(-1))

    held = {"small": small, "arrived": exchange(picked) if direct else picked, "result": ()}

    def tie(name, chunk):
        chunk, held[name] = lax.optimization_barrier((chunk, held[name]))
        return chunk

    def after_arrived(chunk, sent, shared):
        chunk = tie("small", tie("arrived", chunk))
        waves = held["arrived"]
        if direct:
            waves = [across(waves, turn) for turn in range(per_device)]
        *_, where, flat_list = held["small"]
        held["masked"] = prepare(cutoffs, flat_list, where, waves)
        return chunk

    def after_masked(chunk, sent, shared):
        return tie("masked", chunk)

    def filtered(det, sent, shared):
        *turns, where, _ = held["small"]
        masked, sigma = held["masked"]
        held["result"] = detector(det, chips, where, sigma, sent, shared, masked, turns, held["result"])

    def after_detector(det):
        def hook(chunk, sent, shared):
            filtered(det, sent, shared)
            return tie("result", chunk)

        return hook

    hooks = {TEMPLATE_SLOT: after_arrived, MASKED_SLOT: after_masked}
    for det in range(DET - 1):
        hooks[(det + 1) * HALF_CHUNKS - 1 + LAG * chips] = after_detector(det)
    sent, shared = spread(chunks, owner, hooks)
    filtered(DET - 1, sent, shared)
    return tuple(held["result"])


def solution(mesh):
    in_specs = (
        P(("grp", "tpl"), None, None, None),
        P(None, None, "tpl"),
        P(),
        P(),
        P("grp"),
        P("grp"),
    )
    out_specs = (P(("grp", "tpl")), P(("grp", "tpl")))
    return jax.shard_map(body, mesh=mesh, in_specs=in_specs, out_specs=out_specs, check_vma=False)
```

```python
import functools

import jax
import jax.numpy as jnp
import numpy as np
from jax import lax
from jax.experimental import pallas as pl
from jax.experimental.pallas import tpu as pltpu
from jax.sharding import PartitionSpec as P

DET = 3
ROWS = 512
COLS = 512
RADIX = 4
PART = 128
ROW_STEP = 16
WAVE_ROWS = 32
CORES = 2
PAIR = 2
QUAD = CORES * PAIR
VMEM_LIMIT = 24 * 1024 * 1024


two_pi = 6.283185307179586
eps_norm = 1e-06


def turn_table(left_ids, right_ids, period):
    angles = (left_ids[:, None] * right_ids[None, :] % period).astype(np.float64) * (2 * np.pi / period)
    return np.cos(angles), np.sin(angles)


def tables():
    part_ids, col_ids = np.arange(PART), np.arange(COLS)
    row_tables, col_tables, turns = [], [], []
    for residue in range(RADIX):
        cos, sin = turn_table(RADIX * part_ids + residue, part_ids, ROWS)
        row_tables.append(np.block([[cos, -sin], [sin, cos]]))
        col_tables.append(np.block([[cos.T, sin.T], [-sin.T, cos.T]] * 2))
        turns.append(np.stack(turn_table(RADIX * part_ids + residue, col_ids, ROWS * COLS)))
    return (
        jnp.asarray(np.stack(row_tables), jnp.float32).astype(jnp.bfloat16),
        jnp.asarray(np.stack(col_tables), jnp.float32).astype(jnp.bfloat16),
        jnp.asarray(np.stack(turns), jnp.float32),
    )


def slide_turns(slides):
    total = ROWS * COLS
    row_turns = (jnp.arange(ROWS, dtype=jnp.int32)[None, :] * (COLS * slides % total)[:, None]) % total
    col_turns = (jnp.arange(COLS, dtype=jnp.int32)[None, :] * slides[:, None]) % total
    row_angles = row_turns.astype(jnp.float32) * (two_pi / total)
    col_angles = col_turns.astype(jnp.float32) * (two_pi / total)
    rows = jnp.concatenate([jnp.cos(row_angles)[:, None], jnp.sin(row_angles)[:, None]] * 4, 1)
    cols = jnp.concatenate([jnp.cos(col_angles)[:, None], jnp.sin(col_angles)[:, None]] * 4, 1)
    return rows, cols


def partner(flip):
    return [(at, at ^ flip) for at in range(lax.axis_size("tpl"))]


def swap(block, flip):
    return lax.ppermute(block, "tpl", partner(flip))


def quarter_of(strain_slots, det, owner):
    me = lax.axis_index("tpl")
    core, chip = me % CORES, me // CORES % PAIR
    half = ROWS * COLS // CORES
    bins = half // PAIR
    side = lambda which: lax.dynamic_slice(strain_slots, (0, det, 0, which * half), (1, 1, 2, half))[0, 0]
    got = swap(side(1 - core), 1)
    kept = jnp.where(core == owner % CORES, side(core), got)
    got = swap(jnp.where(chip == 0, kept[:, bins:], kept[:, :bins]), CORES)
    kept = jnp.where(chip == 0, kept[:, :bins], kept[:, bins:])
    return jnp.where(chip == owner // CORES % PAIR, kept, got).reshape(2, ROWS // QUAD, COLS)


def along_line(quarter, owner):
    lines = lax.axis_size("tpl") // QUAD
    line, from_line = lax.axis_index("tpl") // QUAD, owner // QUAD
    if lines == 1:
        return quarter
    odd = line % 2 == 1
    quarter = jnp.where(line % 2 == from_line % 2, quarter, swap(quarter, QUAD))
    if lines == 2:
        return quarter
    rows = quarter.shape[1] // 2
    piece = jnp.where(odd, quarter[:, rows:], quarter[:, :rows])
    bit = 2
    while bit < lines:
        piece = jnp.where(line // bit % 2 == from_line // bit % 2, piece, swap(piece, bit * QUAD))
        bit *= 2
    other = swap(piece, QUAD)
    return jnp.concatenate([jnp.where(odd, other, piece), jnp.where(odd, piece, other)], 1)


def all_quarters(quarter):
    beside = swap(quarter, CORES)
    return quarter, beside, swap(quarter, 1), swap(beside, 1)


def collect(templates, lists):
    ids = lax.dynamic_index_in_dim(lists, lax.axis_index("grp"), 1, keepdims=False)
    return templates[ids].reshape(lists.shape[0], 2, WAVE_ROWS, COLS)


def exchange(block):
    return lax.all_to_all(block, "tpl", split_axis=0, concat_axis=0, tiled=True)


def across(block, turn):
    groups = lax.axis_size("grp")
    return lax.ppermute(block, "grp", [(at, (at + turn) % groups) for at in range(groups)]) if turn else block


def collect_plain(templates, lists):
    devices, groups = lax.axis_size("tpl"), lax.axis_size("grp")
    own_group = lax.axis_index("grp")
    per_device = lists.shape[1]
    pieces = per_device * 2
    if pieces % groups:
        groups, own_group = 1, 0
    size = pieces // groups
    picked = templates[lists.reshape(-1)].reshape(devices, pieces, templates.shape[2] // COLS, COLS)
    picked = lax.dynamic_slice_in_dim(picked, own_group * size, size, 1)
    own = exchange(picked)
    found = jnp.stack([across(own, turn) for turn in range(groups)])[(own_group - jnp.arange(groups)) % groups]
    found = found.transpose(0, 2, 1, 3, 4).reshape(per_device, 2, ROWS // WAVE_ROWS, WAVE_ROWS, COLS)
    return [found[at].transpose(1, 0, 2, 3) for at in range(per_device)]


def quarters(parts):
    (re0, im0), (re1, im1), (re2, im2), (re3, im3) = parts
    even_re, even_im, odd_re, odd_im = re0 + re2, im0 + im2, re1 + re3, im1 + im3
    left_re, left_im, right_re, right_im = re0 - re2, im0 - im2, re1 - re3, im1 - im3
    return (
        (even_re + odd_re, even_im + odd_im),
        (left_re - right_im, left_im + right_re),
        (even_re - odd_re, even_im - odd_im),
        (left_re + right_im, left_im - right_re),
    )


def prepare_kernel(count, cut_ref, list_ref, where_ref, *refs):
    wave_refs, (masked_ref, sigma_ref) = refs[:-2], refs[-2:]
    for tpl in range(count):
        cutoff = cut_ref[list_ref[where_ref[2] * count + where_ref[3 + tpl]]]
        total = jnp.zeros((8, COLS), jnp.float32)
        for block in range(ROWS // WAVE_ROWS):
            part = slice(block * WAVE_ROWS, (block + 1) * WAVE_ROWS)
            bins = (lax.broadcasted_iota(jnp.int32, (WAVE_ROWS, COLS), 0) + part.start) * COLS
            inside = bins + lax.broadcasted_iota(jnp.int32, (WAVE_ROWS, COLS), 1) < cutoff
            wave_re = jnp.where(inside, wave_refs[tpl][block, 0].astype(jnp.float32), 0.0)
            wave_im = jnp.where(inside, wave_refs[tpl][block, 1].astype(jnp.float32), 0.0)
            masked_ref[tpl, 0, part, :] = wave_re.astype(jnp.bfloat16)
            masked_ref[tpl, 1, part, :] = wave_im.astype(jnp.bfloat16)
            squares = wave_re * wave_re + wave_im * wave_im
            total = total + jnp.sum(squares.reshape(-1, 8, COLS), axis=0)
        sigma_ref[tpl] = jnp.sum(total)


def detector_kernel(det, where_ref, sigma_ref, *refs):
    first, last = det == 0, det == DET - 1
    quarter_refs, refs = refs[:QUAD], refs[QUAD:]
    masked, rphase_ref, cphase_ref, row_ref, col_ref, twiddle_ref = refs[:6]
    refs = refs[6:]
    before, refs = (None, refs) if first else (refs[0], refs[1:])
    outputs, (turned_ref, slid, stacked, twisted) = refs[:-4], refs[-4:]
    count = masked.shape[0]
    core, chip = where_ref[0], where_ref[1]
    half, rows = ROWS // CORES, ROWS // QUAD

    turned_ref[...] = rphase_ref[det].T
    cc, cs = cphase_ref[det, 0:1, :], cphase_ref[det, 1:2, :]
    for which, quarter in enumerate(quarter_refs):
        of_core, of_chip = (core if which < 2 else 1 - core), (chip if which % 2 == 0 else 1 - chip)
        part = pl.ds(pl.multiple_of(of_core * half + of_chip * rows, rows), rows)
        rc, rs = turned_ref[part, 0:1], turned_ref[part, 1:2]
        turn_re = rc * cc - rs * cs
        turn_im = rc * cs + rs * cc
        data_re, data_im = quarter[0].astype(jnp.float32), quarter[1].astype(jnp.float32)
        slid[0, part, :] = data_re * turn_re - data_im * turn_im
        slid[1, part, :] = data_re * turn_im + data_im * turn_re

    largest = []
    for tpl in range(count):
        for at in range(0, PART, ROW_STEP):
            for col_at in range(0, COLS, PART):
                cols = slice(col_at, col_at + PART)
                parts = []
                for quarter in range(RADIX):
                    spot = slice(quarter * PART + at, quarter * PART + at + ROW_STEP)
                    wave_re = masked[tpl, 0, spot, cols].astype(jnp.float32)
                    wave_im = masked[tpl, 1, spot, cols].astype(jnp.float32)
                    data_re, data_im = slid[0, spot, cols], slid[1, spot, cols]
                    parts.append((data_re * wave_re + data_im * wave_im, data_im * wave_re - data_re * wave_im))
                for residue, (re, im) in enumerate(quarters(parts)):
                    stacked[tpl, residue, at : at + ROW_STEP, cols] = re.astype(jnp.bfloat16)
                    stacked[tpl, residue, PART + at : PART + at + ROW_STEP, cols] = im.astype(jnp.bfloat16)
        for residue in range(RADIX):
            section = jnp.dot(row_ref[residue], stacked[tpl, residue], preferred_element_type=jnp.float32)
            for at in range(0, PART, ROW_STEP):
                parts = []
                for quarter in range(RADIX):
                    cols = slice(quarter * PART, (quarter + 1) * PART)
                    re, im = section[at : at + ROW_STEP, cols], section[PART + at : PART + at + ROW_STEP, cols]
                    turn_re = twiddle_ref[residue, 0, at : at + ROW_STEP, cols]
                    turn_im = twiddle_ref[residue, 1, at : at + ROW_STEP, cols]
                    parts.append((re * turn_re - im * turn_im, re * turn_im + im * turn_re))
                spot = slice(residue * PART + at, residue * PART + at + ROW_STEP)
                for other, sums in enumerate(quarters(parts)):
                    for which, value in enumerate(sums):
                        high = value.astype(jnp.bfloat16)
                        low = (value - high.astype(jnp.float32)).astype(jnp.bfloat16)
                        twisted[tpl, other, spot, which * PART : (which + 1) * PART] = high
                        twisted[tpl, other, spot, (which + 2) * PART : (which + 3) * PART] = low
        peak = jnp.zeros((8, PART), jnp.float32)
        for other in range(RADIX):
            series = jnp.dot(twisted[tpl, other], col_ref[other], preferred_element_type=jnp.float32)
            squares = series[:, :PART] * series[:, :PART] + series[:, PART:] * series[:, PART:]
            cols = slice(other * PART, (other + 1) * PART)
            if not first:
                squares = squares + before[tpl, :, cols]
            if last:
                peak = jnp.maximum(peak, jnp.max(squares.reshape(-1, 8, PART), axis=0))
            else:
                outputs[0][tpl, :, cols] = squares
        largest.append(peak)

    if last:
        for tpl in range(count):
            place = where_ref[3 + tpl]
            outputs[0][place] = jnp.max(largest[tpl]) / (2.0 * (sigma_ref[tpl] + eps_norm))
            outputs[1][place] = sigma_ref[tpl] / (ROWS * COLS)


smem = pl.BlockSpec(memory_space=pltpu.SMEM)
vmem = pl.BlockSpec(memory_space=pltpu.VMEM)


def prepare(cutoffs, lists, where, waves):
    count = len(waves)
    return pl.pallas_call(
        functools.partial(prepare_kernel, count),
        out_shape=(
            jax.ShapeDtypeStruct((count, 2, ROWS, COLS), jnp.bfloat16),
            jax.ShapeDtypeStruct((count,), jnp.float32),
        ),
        in_specs=[smem, smem, smem] + [vmem] * count,
        out_specs=(vmem, smem),
        compiler_params=pltpu.CompilerParams(vmem_limit_bytes=VMEM_LIMIT),
        cost_estimate=pl.CostEstimate(flops=2_000_000_000, bytes_accessed=6_000_000, transcendentals=0),
    )(cutoffs, lists, where, *waves)


def detector(det, where, sigma, found, masked, turns, before):
    count = masked.shape[0]
    last = det == DET - 1
    scalars = jax.ShapeDtypeStruct((count,), jnp.float32)
    operands = [*found, masked, *turns, *tables(), *before]
    return pl.pallas_call(
        functools.partial(detector_kernel, det),
        out_shape=(scalars, scalars) if last else (jax.ShapeDtypeStruct((count, ROWS, COLS), jnp.float32),),
        in_specs=[smem, smem] + [vmem] * len(operands),
        out_specs=(smem, smem) if last else (vmem,),
        scratch_shapes=[
            pltpu.VMEM((ROWS, 8), jnp.float32),
            pltpu.VMEM((2, ROWS, COLS), jnp.float32),
            pltpu.VMEM((count, RADIX, 2 * PART, COLS), jnp.bfloat16),
            pltpu.VMEM((count, RADIX, ROWS, 4 * PART), jnp.bfloat16),
        ],
        compiler_params=pltpu.CompilerParams(vmem_limit_bytes=VMEM_LIMIT),
        cost_estimate=pl.CostEstimate(flops=5_000_000_000, bytes_accessed=10_000_000, transcendentals=0),
    )(where, sigma, *operands)


def body(strain_slots, templates, cutoffs, lists, owner, slides):
    me, owner = lax.axis_index("tpl"), owner[0]
    groups = lax.axis_size("grp")
    per_device = lists.shape[1]
    direct = per_device == groups and templates.shape[2] == WAVE_ROWS * COLS
    places = [(lax.axis_index("grp") - turn) % groups if direct else turn for turn in range(per_device)]

    picked = collect(templates, lists) if direct else collect_plain(templates, lists)
    strain_slots, picked = lax.optimization_barrier((strain_slots, picked))
    arrived = exchange(picked) if direct else picked
    where = jnp.stack([jnp.asarray(at, jnp.int32) for at in (me % CORES, me // CORES % PAIR, me, *places)])
    small = (*slide_turns(slides), where, lists.reshape(-1))
    quarter = []
    for det in range(DET):
        quarter.append(quarter_of(strain_slots, det, owner))
        strain_slots, quarter[det] = lax.optimization_barrier((strain_slots, quarter[det]))
    quarter[-1], arrived, small = lax.optimization_barrier((quarter[-1], arrived, small))
    *turns, where, flat_list = small

    found = [all_quarters(along_line(part, owner)) for part in quarter]
    waves = [across(arrived, turn) for turn in range(per_device)] if direct else arrived
    masked, sigma = prepare(cutoffs, flat_list, where, waves)
    result = ()
    for det in range(DET):
        result = detector(det, where, sigma, found[det], masked, turns, result)
    return result


def solution(mesh):
    in_specs = (
        P(("grp", "tpl"), None, None, None),
        P(None, None, "tpl"),
        P(),
        P(),
        P("grp"),
        P("grp"),
    )
    out_specs = (P(("grp", "tpl")), P(("grp", "tpl")))
    return jax.shard_map(body, mesh=mesh, in_specs=in_specs, out_specs=out_specs, check_vma=False)
```

```python
import functools

import jax
import jax.numpy as jnp
import numpy as np
from jax import lax
from jax.experimental import pallas as pl
from jax.experimental.pallas import tpu as pltpu
from jax.sharding import PartitionSpec as P

DET = 3
ROWS = 512
COLS = 512
RADIX = 4
PART = 128
ROW_STEP = 16
WAVE_ROWS = 32
CORES = 2
HALF_CHUNKS = 2
LAG = 2
TEMPLATE_SLOT = 2
MASKED_SLOT = 13
VMEM_LIMIT = 24 * 1024 * 1024


two_pi = 6.283185307179586
eps_norm = 1e-06


def turn_table(left_ids, right_ids, period):
    angles = (left_ids[:, None] * right_ids[None, :] % period).astype(np.float64) * (2 * np.pi / period)
    return np.cos(angles), np.sin(angles)


def tables():
    part_ids, col_ids = np.arange(PART), np.arange(COLS)
    row_tables, col_tables, turns = [], [], []
    for residue in range(RADIX):
        cos, sin = turn_table(RADIX * part_ids + residue, part_ids, ROWS)
        row_tables.append(np.block([[cos, -sin], [sin, cos]]))
        col_tables.append(np.block([[cos.T, sin.T], [-sin.T, cos.T]] * 2))
        turns.append(np.stack(turn_table(RADIX * part_ids + residue, col_ids, ROWS * COLS)))
    return (
        jnp.asarray(np.stack(row_tables), jnp.float32).astype(jnp.bfloat16),
        jnp.asarray(np.stack(col_tables), jnp.float32).astype(jnp.bfloat16),
        jnp.asarray(np.stack(turns), jnp.float32),
    )


def slide_turns(slides):
    total = ROWS * COLS
    row_turns = (jnp.arange(ROWS, dtype=jnp.int32)[None, :] * (COLS * slides % total)[:, None]) % total
    col_turns = (jnp.arange(COLS, dtype=jnp.int32)[None, :] * slides[:, None]) % total
    row_angles = row_turns.astype(jnp.float32) * (two_pi / total)
    col_angles = col_turns.astype(jnp.float32) * (two_pi / total)
    rows = jnp.concatenate([jnp.cos(row_angles)[:, None], jnp.sin(row_angles)[:, None]] * 4, 1)
    cols = jnp.concatenate([jnp.cos(col_angles)[:, None], jnp.sin(col_angles)[:, None]] * 4, 1)
    return rows, cols


def ring_order(chips):
    return list(range(0, chips, 2)) + list(range(chips - 1 - chips % 2, 0, -2))


def swap(block, flip):
    return lax.ppermute(block, "tpl", [(at, at ^ flip) for at in range(lax.axis_size("tpl"))])


def half_chunks(strain_slots, det, owner):
    core = lax.axis_index("tpl") % CORES
    half = ROWS * COLS // CORES
    bins = half // HALF_CHUNKS
    side = lambda which: lax.dynamic_slice(strain_slots, (0, det, 0, which * half), (1, 1, 2, half))[0, 0]
    got = swap(side(1 - core), 1)
    first = jnp.where(core == owner % CORES, side(core), got)
    return [first[:, at : at + bins].reshape(2, bins // COLS, COLS) for at in range(0, half, bins)]


def spread(chunks, owner, hooks):
    devices = lax.axis_size("tpl")
    chips = devices // CORES
    order = ring_order(chips)
    chip, core = lax.axis_index("tpl") // CORES, lax.axis_index("tpl") % CORES
    on_owner_chip = chip == owner // CORES
    along = []
    for at in range(chips):
        along.append((order[at] * CORES, order[(at + 1) % chips] * CORES))
        along.append((order[(at + 1) % chips] * CORES + 1, order[at] * CORES + 1))
    sent, shared, arrived = [], [], []
    count = len(chunks)
    last = count + LAG * (chips - 1)
    for slot in range(last):
        if slot < LAG:
            here = chunks[slot]
        elif slot < count:
            here = jnp.where(on_owner_chip, chunks[slot], arrived[slot - LAG])
        else:
            here = arrived[slot - LAG]
        if slot in hooks:
            here = hooks[slot](here, sent, shared)
        sent.append(here)
        shared.append(swap(hooks[last](here, sent, shared) if slot >= last - LAG else here, 1))
        if slot < count + LAG * (chips - 2):
            arrived.append(lax.ppermute(here, "tpl", along))
    return sent, shared


def distances(owner):
    chips = lax.axis_size("tpl") // CORES
    chip, core = lax.axis_index("tpl") // CORES, lax.axis_index("tpl") % CORES
    place = lambda at: jnp.where(at % 2 == 0, at // 2, chips - 1 - at // 2)
    forward = (place(chip) - place(owner // CORES)) % chips
    backward = (place(owner // CORES) - place(chip)) % chips
    return jnp.where(core == 0, forward, backward), jnp.where(core == 0, backward, forward)


def collect(templates, lists):
    ids = lax.dynamic_index_in_dim(lists, lax.axis_index("grp"), 1, keepdims=False)
    return templates[ids].reshape(lists.shape[0], 2, WAVE_ROWS, COLS)


def exchange(block):
    return lax.all_to_all(block, "tpl", split_axis=0, concat_axis=0, tiled=True)


def across(block, turn):
    groups = lax.axis_size("grp")
    return lax.ppermute(block, "grp", [(at, (at + turn) % groups) for at in range(groups)]) if turn else block


def collect_plain(templates, lists):
    devices, groups = lax.axis_size("tpl"), lax.axis_size("grp")
    own_group = lax.axis_index("grp")
    per_device = lists.shape[1]
    pieces = per_device * 2
    if pieces % groups:
        groups, own_group = 1, 0
    size = pieces // groups
    picked = templates[lists.reshape(-1)].reshape(devices, pieces, templates.shape[2] // COLS, COLS)
    picked = lax.dynamic_slice_in_dim(picked, own_group * size, size, 1)
    own = exchange(picked)
    found = jnp.stack([across(own, turn) for turn in range(groups)])[(own_group - jnp.arange(groups)) % groups]
    found = found.transpose(0, 2, 1, 3, 4).reshape(per_device, 2, ROWS // WAVE_ROWS, WAVE_ROWS, COLS)
    return [found[at].transpose(1, 0, 2, 3) for at in range(per_device)]


def quarters(parts):
    (re0, im0), (re1, im1), (re2, im2), (re3, im3) = parts
    even_re, even_im, odd_re, odd_im = re0 + re2, im0 + im2, re1 + re3, im1 + im3
    left_re, left_im, right_re, right_im = re0 - re2, im0 - im2, re1 - re3, im1 - im3
    return (
        (even_re + odd_re, even_im + odd_im),
        (left_re - right_im, left_im + right_re),
        (even_re - odd_re, even_im - odd_im),
        (left_re + right_im, left_im - right_re),
    )


def prepare_kernel(count, cut_ref, list_ref, where_ref, *refs):
    wave_refs, (masked_ref, sigma_ref) = refs[:-2], refs[-2:]
    for tpl in range(count):
        cutoff = cut_ref[list_ref[where_ref[2] * count + where_ref[4 + tpl]]]
        total = jnp.zeros((8, COLS), jnp.float32)
        for block in range(ROWS // WAVE_ROWS):
            part = slice(block * WAVE_ROWS, (block + 1) * WAVE_ROWS)
            bins = (lax.broadcasted_iota(jnp.int32, (WAVE_ROWS, COLS), 0) + part.start) * COLS
            inside = bins + lax.broadcasted_iota(jnp.int32, (WAVE_ROWS, COLS), 1) < cutoff
            wave_re = jnp.where(inside, wave_refs[tpl][block, 0].astype(jnp.float32), 0.0)
            wave_im = jnp.where(inside, wave_refs[tpl][block, 1].astype(jnp.float32), 0.0)
            masked_ref[tpl, 0, part, :] = wave_re.astype(jnp.bfloat16)
            masked_ref[tpl, 1, part, :] = wave_im.astype(jnp.bfloat16)
            squares = wave_re * wave_re + wave_im * wave_im
            total = total + jnp.sum(squares.reshape(-1, 8, COLS), axis=0)
        sigma_ref[tpl] = jnp.sum(total)


def detector_kernel(det, chips, where_ref, sigma_ref, *refs):
    first, last = det == 0, det == DET - 1
    slots = HALF_CHUNKS + LAG * (chips - 1)
    near_refs, far_refs, refs = refs[:slots], refs[slots : 2 * slots], refs[2 * slots :]
    masked, rphase_ref, cphase_ref, row_ref, col_ref, twiddle_ref = refs[:6]
    refs = refs[6:]
    before, refs = (None, refs) if first else (refs[0], refs[1:])
    outputs, (strain_ref, strain_sem, turned_ref, slid, stacked, twisted) = refs[:-6], refs[-6:]
    count = masked.shape[0]
    core, near, far = where_ref[0], where_ref[1], where_ref[3]
    half = ROWS // CORES
    rows = half // HALF_CHUNKS

    for slot_refs, distance, side in ((near_refs, near, core), (far_refs, far, 1 - core)):
        for away in range(chips):
            @pl.when(distance == away)
            def _():
                for at in range(HALF_CHUNKS):
                    into = pl.ds(pl.multiple_of(side * half + at * rows, rows), rows)
                    pltpu.make_async_copy(slot_refs[at + LAG * away], strain_ref.at[:, into, :], strain_sem).start()
    turned_ref[...] = rphase_ref[det].T
    cc, cs = cphase_ref[det, 0:1, :], cphase_ref[det, 1:2, :]
    pltpu.make_async_copy(strain_ref, strain_ref, strain_sem).wait()
    for at in range(0, ROWS, PART):
        part = slice(at, at + PART)
        rc, rs = turned_ref[part, 0:1], turned_ref[part, 1:2]
        turn_re = rc * cc - rs * cs
        turn_im = rc * cs + rs * cc
        data_re, data_im = strain_ref[0, part, :].astype(jnp.float32), strain_ref[1, part, :].astype(jnp.float32)
        slid[0, part, :] = data_re * turn_re - data_im * turn_im
        slid[1, part, :] = data_re * turn_im + data_im * turn_re

    largest = []
    for tpl in range(count):
        for at in range(0, PART, ROW_STEP):
            for col_at in range(0, COLS, PART):
                cols = slice(col_at, col_at + PART)
                parts = []
                for quarter in range(RADIX):
                    spot = slice(quarter * PART + at, quarter * PART + at + ROW_STEP)
                    wave_re = masked[tpl, 0, spot, cols].astype(jnp.float32)
                    wave_im = masked[tpl, 1, spot, cols].astype(jnp.float32)
                    data_re, data_im = slid[0, spot, cols], slid[1, spot, cols]
                    parts.append((data_re * wave_re + data_im * wave_im, data_im * wave_re - data_re * wave_im))
                for residue, (re, im) in enumerate(quarters(parts)):
                    stacked[tpl, residue, at : at + ROW_STEP, cols] = re.astype(jnp.bfloat16)
                    stacked[tpl, residue, PART + at : PART + at + ROW_STEP, cols] = im.astype(jnp.bfloat16)
        for residue in range(RADIX):
            section = jnp.dot(row_ref[residue], stacked[tpl, residue], preferred_element_type=jnp.float32)
            for at in range(0, PART, ROW_STEP):
                parts = []
                for quarter in range(RADIX):
                    cols = slice(quarter * PART, (quarter + 1) * PART)
                    re, im = section[at : at + ROW_STEP, cols], section[PART + at : PART + at + ROW_STEP, cols]
                    turn_re = twiddle_ref[residue, 0, at : at + ROW_STEP, cols]
                    turn_im = twiddle_ref[residue, 1, at : at + ROW_STEP, cols]
                    parts.append((re * turn_re - im * turn_im, re * turn_im + im * turn_re))
                spot = slice(residue * PART + at, residue * PART + at + ROW_STEP)
                for other, sums in enumerate(quarters(parts)):
                    for which, value in enumerate(sums):
                        high = value.astype(jnp.bfloat16)
                        low = (value - high.astype(jnp.float32)).astype(jnp.bfloat16)
                        twisted[tpl, other, spot, which * PART : (which + 1) * PART] = high
                        twisted[tpl, other, spot, (which + 2) * PART : (which + 3) * PART] = low
        peak = jnp.zeros((8, PART), jnp.float32)
        for other in range(RADIX):
            series = jnp.dot(twisted[tpl, other], col_ref[other], preferred_element_type=jnp.float32)
            squares = series[:, :PART] * series[:, :PART] + series[:, PART:] * series[:, PART:]
            cols = slice(other * PART, (other + 1) * PART)
            if not first:
                squares = squares + before[tpl, :, cols]
            if last:
                peak = jnp.maximum(peak, jnp.max(squares.reshape(-1, 8, PART), axis=0))
            else:
                outputs[0][tpl, :, cols] = squares
        largest.append(peak)

    if not last:
        outputs[1][0] = jnp.int32(0)

    if last:
        for tpl in range(count):
            place = where_ref[4 + tpl]
            outputs[0][place] = jnp.max(largest[tpl]) / (2.0 * (sigma_ref[tpl] + eps_norm))
            outputs[1][place] = sigma_ref[tpl] / (ROWS * COLS)


smem = pl.BlockSpec(memory_space=pltpu.SMEM)
vmem = pl.BlockSpec(memory_space=pltpu.VMEM)
anywhere = pl.BlockSpec(memory_space=pl.ANY)


def prepare(cutoffs, lists, where, waves):
    count = len(waves)
    return pl.pallas_call(
        functools.partial(prepare_kernel, count),
        out_shape=(
            jax.ShapeDtypeStruct((count, 2, ROWS, COLS), jnp.bfloat16),
            jax.ShapeDtypeStruct((count,), jnp.float32),
        ),
        in_specs=[smem, smem, smem] + [vmem] * count,
        out_specs=(vmem, smem),
        compiler_params=pltpu.CompilerParams(vmem_limit_bytes=VMEM_LIMIT),
        cost_estimate=pl.CostEstimate(flops=2_000_000_000, bytes_accessed=6_000_000, transcendentals=0),
    )(cutoffs, lists, where, *waves)


def detector(det, chips, where, sigma, sent, shared, masked, turns, before):
    count = masked.shape[0]
    slots = slice(det * HALF_CHUNKS, (det + 1) * HALF_CHUNKS + LAG * (chips - 1))
    found = [*sent[slots], *shared[slots]]
    last = det == DET - 1
    scalars = jax.ShapeDtypeStruct((count,), jnp.float32)
    operands = [masked, *turns, *tables(), *before[:1]]
    return pl.pallas_call(
        functools.partial(detector_kernel, det, chips),
        out_shape=(scalars, scalars)
        if last
        else (jax.ShapeDtypeStruct((count, ROWS, COLS), jnp.float32), jax.ShapeDtypeStruct((1,), jnp.int32)),
        in_specs=[smem, smem] + [anywhere] * len(found) + [vmem] * len(operands),
        out_specs=(smem, smem) if last else (vmem, smem),
        scratch_shapes=[
            pltpu.VMEM((2, ROWS, COLS), jnp.bfloat16),
            pltpu.SemaphoreType.DMA,
            pltpu.VMEM((ROWS, 8), jnp.float32),
            pltpu.VMEM((2, ROWS, COLS), jnp.float32),
            pltpu.VMEM((count, RADIX, 2 * PART, COLS), jnp.bfloat16),
            pltpu.VMEM((count, RADIX, ROWS, 4 * PART), jnp.bfloat16),
        ],
        compiler_params=pltpu.CompilerParams(vmem_limit_bytes=VMEM_LIMIT),
        cost_estimate=pl.CostEstimate(flops=5_000_000_000, bytes_accessed=10_000_000, transcendentals=0),
    )(where, sigma, *found, *operands)


def body(strain_slots, templates, cutoffs, lists, owner, slides):
    me, owner = lax.axis_index("tpl"), owner[0]
    devices, groups = lax.axis_size("tpl"), lax.axis_size("grp")
    chips = devices // CORES
    per_device = lists.shape[1]
    direct = per_device == groups and templates.shape[2] == WAVE_ROWS * COLS
    places = [(lax.axis_index("grp") - turn) % groups if direct else turn for turn in range(per_device)]

    picked = collect(templates, lists) if direct else collect_plain(templates, lists)
    strain_slots, picked = lax.optimization_barrier((strain_slots, picked))
    chunks = []
    for det in range(DET):
        more = half_chunks(strain_slots, det, owner)
        strain_slots, more = lax.optimization_barrier((strain_slots, more))
        chunks += more
    near, far = distances(owner)
    where = jnp.stack([jnp.asarray(at, jnp.int32) for at in (me % CORES, near, me, far, *places)])
    small = (*slide_turns(slides), where, lists.reshape(-1))

    arrived = exchange(picked) if direct else picked
    waves = [across(arrived, turn) for turn in range(per_device)] if direct else arrived
    *turns, where, flat_list = small
    masked, sigma = prepare(cutoffs, flat_list, where, waves)
    results = [()]

    def once(ready, chunk):
        return jnp.where(ready, chunk, jnp.zeros_like(chunk))

    def after_arrived(chunk, sent, shared):
        block = arrived if direct else arrived[0]
        return once(block[(0,) * block.ndim].astype(jnp.float32) < 1e3, chunk)

    def after_masked(chunk, sent, shared):
        return once(sigma[0] >= 0.0, chunk)

    def after_detector(det):
        def hook(chunk, sent, shared):
            if len(results) == det + 1:
                results.append(detector(det, chips, where, sigma, sent, shared, masked, turns, results[-1]))
            return once(results[-1][1][0] == 0, chunk)

        return hook

    hooks = {TEMPLATE_SLOT: after_arrived, MASKED_SLOT: after_masked}
    for det in range(DET - 1):
        hooks[(det + 1) * HALF_CHUNKS + LAG * chips - (1 if det < DET - 2 else 0)] = after_detector(det)
    sent, shared = spread(chunks, owner, hooks)
    return tuple(detector(DET - 1, chips, where, sigma, sent, shared, masked, turns, results[-1]))


def solution(mesh):
    in_specs = (
        P(("grp", "tpl"), None, None, None),
        P(None, None, "tpl"),
        P(),
        P(),
        P("grp"),
        P("grp"),
    )
    out_specs = (P(("grp", "tpl")), P(("grp", "tpl")))
    return jax.shard_map(body, mesh=mesh, in_specs=in_specs, out_specs=out_specs, check_vma=False)
```

```python
import functools

import jax
import jax.numpy as jnp
import numpy as np
from jax import lax
from jax.experimental import pallas as pl
from jax.experimental.pallas import tpu as pltpu
from jax.sharding import PartitionSpec as P

DET = 3
ROWS = 512
COLS = 512
RADIX = 4
PART = 128
ROW_STEP = 16
WAVE_ROWS = 32
CORES = 2
VMEM_LIMIT = 24 * 1024 * 1024


two_pi = 6.283185307179586
eps_norm = 1e-06


def turn_table(left_ids, right_ids, period):
    angles = (left_ids[:, None] * right_ids[None, :] % period).astype(np.float64) * (2 * np.pi / period)
    return np.cos(angles), np.sin(angles)


def tables():
    part_ids, col_ids = np.arange(PART), np.arange(COLS)
    row_tables, col_tables, turns = [], [], []
    for residue in range(RADIX):
        cos, sin = turn_table(RADIX * part_ids + residue, part_ids, ROWS)
        row_tables.append(np.block([[cos, -sin], [sin, cos]]))
        col_tables.append(np.block([[cos.T, sin.T], [-sin.T, cos.T]] * 2))
        turns.append(np.stack(turn_table(RADIX * part_ids + residue, col_ids, ROWS * COLS)))
    return (
        jnp.asarray(np.stack(row_tables), jnp.float32).astype(jnp.bfloat16),
        jnp.asarray(np.stack(col_tables), jnp.float32).astype(jnp.bfloat16),
        jnp.asarray(np.stack(turns), jnp.float32),
    )


def slide_turns(slides):
    total = ROWS * COLS
    row_turns = (jnp.arange(ROWS, dtype=jnp.int32)[None, :] * (COLS * slides % total)[:, None]) % total
    col_turns = (jnp.arange(COLS, dtype=jnp.int32)[None, :] * slides[:, None]) % total
    row_angles = row_turns.astype(jnp.float32) * (two_pi / total)
    col_angles = col_turns.astype(jnp.float32) * (two_pi / total)
    rows = jnp.concatenate([jnp.cos(row_angles)[:, None], jnp.sin(row_angles)[:, None]] * 4, 1)
    cols = jnp.concatenate([jnp.cos(col_angles)[:, None], jnp.sin(col_angles)[:, None]] * 4, 1)
    return rows, cols


def swap(block):
    return lax.ppermute(block, "tpl", [(at, at ^ 1) for at in range(lax.axis_size("tpl"))])


def spread(strain_slots, det, owner):
    devices = lax.axis_size("tpl")
    me = lax.axis_index("tpl")
    core = me % CORES
    half = ROWS * COLS // CORES
    side = lambda which: lax.dynamic_slice(strain_slots, (0, det, 0, which * half), (1, 1, 2, half))[0, 0]
    got = swap(side(1 - core))
    kept = jnp.where(core == owner % CORES, side(core), got).reshape(2, ROWS // CORES, COLS)
    kept = jnp.where(me // CORES == owner // CORES, kept, jnp.zeros_like(kept))
    same_core = [list(range(first, devices, CORES)) for first in range(CORES)]
    near = lax.psum(kept, "tpl", axis_index_groups=same_core)
    return near, swap(near)


def collect(templates, lists):
    ids = lax.dynamic_index_in_dim(lists, lax.axis_index("grp"), 1, keepdims=False)
    return templates[ids].reshape(lists.shape[0], 2, WAVE_ROWS, COLS)


def exchange(block):
    return lax.all_to_all(block, "tpl", split_axis=0, concat_axis=0, tiled=True)


def across(block, turn):
    groups = lax.axis_size("grp")
    return lax.ppermute(block, "grp", [(at, (at + turn) % groups) for at in range(groups)]) if turn else block


def collect_plain(templates, lists):
    devices, groups = lax.axis_size("tpl"), lax.axis_size("grp")
    own_group = lax.axis_index("grp")
    per_device = lists.shape[1]
    pieces = per_device * 2
    if pieces % groups:
        groups, own_group = 1, 0
    size = pieces // groups
    picked = templates[lists.reshape(-1)].reshape(devices, pieces, templates.shape[2] // COLS, COLS)
    picked = lax.dynamic_slice_in_dim(picked, own_group * size, size, 1)
    own = exchange(picked)
    found = jnp.stack([across(own, turn) for turn in range(groups)])[(own_group - jnp.arange(groups)) % groups]
    found = found.transpose(0, 2, 1, 3, 4).reshape(per_device, 2, ROWS // WAVE_ROWS, WAVE_ROWS, COLS)
    return [found[at].transpose(1, 0, 2, 3) for at in range(per_device)]


def quarters(parts):
    (re0, im0), (re1, im1), (re2, im2), (re3, im3) = parts
    even_re, even_im, odd_re, odd_im = re0 + re2, im0 + im2, re1 + re3, im1 + im3
    left_re, left_im, right_re, right_im = re0 - re2, im0 - im2, re1 - re3, im1 - im3
    return (
        (even_re + odd_re, even_im + odd_im),
        (left_re - right_im, left_im + right_re),
        (even_re - odd_re, even_im - odd_im),
        (left_re + right_im, left_im - right_re),
    )


def prepare_kernel(count, cut_ref, list_ref, where_ref, *refs):
    wave_refs, (masked_ref, sigma_ref) = refs[:-2], refs[-2:]
    for tpl in range(count):
        cutoff = cut_ref[list_ref[where_ref[1] * count + where_ref[2 + tpl]]]
        total = jnp.zeros((8, COLS), jnp.float32)
        for block in range(ROWS // WAVE_ROWS):
            part = slice(block * WAVE_ROWS, (block + 1) * WAVE_ROWS)
            bins = (lax.broadcasted_iota(jnp.int32, (WAVE_ROWS, COLS), 0) + part.start) * COLS
            inside = bins + lax.broadcasted_iota(jnp.int32, (WAVE_ROWS, COLS), 1) < cutoff
            wave_re = jnp.where(inside, wave_refs[tpl][block, 0].astype(jnp.float32), 0.0)
            wave_im = jnp.where(inside, wave_refs[tpl][block, 1].astype(jnp.float32), 0.0)
            masked_ref[tpl, 0, part, :] = wave_re.astype(jnp.bfloat16)
            masked_ref[tpl, 1, part, :] = wave_im.astype(jnp.bfloat16)
            squares = wave_re * wave_re + wave_im * wave_im
            total = total + jnp.sum(squares.reshape(-1, 8, COLS), axis=0)
        sigma_ref[tpl] = jnp.sum(total)


def detector_kernel(det, where_ref, sigma_ref, *refs):
    first, last = det == 0, det == DET - 1
    half_refs, refs = refs[:CORES], refs[CORES:]
    masked, rphase_ref, cphase_ref, row_ref, col_ref, twiddle_ref = refs[:6]
    refs = refs[6:]
    before, refs = (None, refs) if first else (refs[0], refs[1:])
    outputs, (turned_ref, slid, stacked, twisted) = refs[:-4], refs[-4:]
    count = masked.shape[0]
    core, half = where_ref[0], ROWS // CORES

    turned_ref[...] = rphase_ref[det].T
    cc, cs = cphase_ref[det, 0:1, :], cphase_ref[det, 1:2, :]
    for which, half_ref in enumerate(half_refs):
        of_core = core if which == 0 else 1 - core
        for at in range(0, half, PART):
            part = pl.ds(pl.multiple_of(of_core * half + at, PART), PART)
            rc, rs = turned_ref[part, 0:1], turned_ref[part, 1:2]
            turn_re = rc * cc - rs * cs
            turn_im = rc * cs + rs * cc
            data_re = half_ref[0, at : at + PART].astype(jnp.float32)
            data_im = half_ref[1, at : at + PART].astype(jnp.float32)
            slid[0, part, :] = data_re * turn_re - data_im * turn_im
            slid[1, part, :] = data_re * turn_im + data_im * turn_re

    largest = []
    for tpl in range(count):
        for at in range(0, PART, ROW_STEP):
            for col_at in range(0, COLS, PART):
                cols = slice(col_at, col_at + PART)
                parts = []
                for quarter in range(RADIX):
                    spot = slice(quarter * PART + at, quarter * PART + at + ROW_STEP)
                    wave_re = masked[tpl, 0, spot, cols].astype(jnp.float32)
                    wave_im = masked[tpl, 1, spot, cols].astype(jnp.float32)
                    data_re, data_im = slid[0, spot, cols], slid[1, spot, cols]
                    parts.append((data_re * wave_re + data_im * wave_im, data_im * wave_re - data_re * wave_im))
                for residue, (re, im) in enumerate(quarters(parts)):
                    stacked[tpl, residue, at : at + ROW_STEP, cols] = re.astype(jnp.bfloat16)
                    stacked[tpl, residue, PART + at : PART + at + ROW_STEP, cols] = im.astype(jnp.bfloat16)
        for residue in range(RADIX):
            section = jnp.dot(row_ref[residue], stacked[tpl, residue], preferred_element_type=jnp.float32)
            for at in range(0, PART, ROW_STEP):
                parts = []
                for quarter in range(RADIX):
                    cols = slice(quarter * PART, (quarter + 1) * PART)
                    re, im = section[at : at + ROW_STEP, cols], section[PART + at : PART + at + ROW_STEP, cols]
                    turn_re = twiddle_ref[residue, 0, at : at + ROW_STEP, cols]
                    turn_im = twiddle_ref[residue, 1, at : at + ROW_STEP, cols]
                    parts.append((re * turn_re - im * turn_im, re * turn_im + im * turn_re))
                spot = slice(residue * PART + at, residue * PART + at + ROW_STEP)
                for other, sums in enumerate(quarters(parts)):
                    for which, value in enumerate(sums):
                        high = value.astype(jnp.bfloat16)
                        low = (value - high.astype(jnp.float32)).astype(jnp.bfloat16)
                        twisted[tpl, other, spot, which * PART : (which + 1) * PART] = high
                        twisted[tpl, other, spot, (which + 2) * PART : (which + 3) * PART] = low
        peak = jnp.zeros((8, PART), jnp.float32)
        for other in range(RADIX):
            series = jnp.dot(twisted[tpl, other], col_ref[other], preferred_element_type=jnp.float32)
            squares = series[:, :PART] * series[:, :PART] + series[:, PART:] * series[:, PART:]
            cols = slice(other * PART, (other + 1) * PART)
            if not first:
                squares = squares + before[tpl, :, cols]
            if last:
                peak = jnp.maximum(peak, jnp.max(squares.reshape(-1, 8, PART), axis=0))
            else:
                outputs[0][tpl, :, cols] = squares
        largest.append(peak)

    if last:
        for tpl in range(count):
            place = where_ref[2 + tpl]
            outputs[0][place] = jnp.max(largest[tpl]) / (2.0 * (sigma_ref[tpl] + eps_norm))
            outputs[1][place] = sigma_ref[tpl] / (ROWS * COLS)


smem = pl.BlockSpec(memory_space=pltpu.SMEM)
vmem = pl.BlockSpec(memory_space=pltpu.VMEM)


def prepare(cutoffs, lists, where, waves):
    count = len(waves)
    return pl.pallas_call(
        functools.partial(prepare_kernel, count),
        out_shape=(
            jax.ShapeDtypeStruct((count, 2, ROWS, COLS), jnp.bfloat16),
            jax.ShapeDtypeStruct((count,), jnp.float32),
        ),
        in_specs=[smem, smem, smem] + [vmem] * count,
        out_specs=(vmem, smem),
        compiler_params=pltpu.CompilerParams(vmem_limit_bytes=VMEM_LIMIT),
        cost_estimate=pl.CostEstimate(flops=2_000_000_000, bytes_accessed=6_000_000, transcendentals=0),
    )(cutoffs, lists, where, *waves)


def detector(det, where, sigma, found, masked, turns, before):
    count = masked.shape[0]
    last = det == DET - 1
    scalars = jax.ShapeDtypeStruct((count,), jnp.float32)
    operands = [*found, masked, *turns, *tables(), *before]
    return pl.pallas_call(
        functools.partial(detector_kernel, det),
        out_shape=(scalars, scalars) if last else (jax.ShapeDtypeStruct((count, ROWS, COLS), jnp.float32),),
        in_specs=[smem, smem] + [vmem] * len(operands),
        out_specs=(smem, smem) if last else (vmem,),
        scratch_shapes=[
            pltpu.VMEM((ROWS, 8), jnp.float32),
            pltpu.VMEM((2, ROWS, COLS), jnp.float32),
            pltpu.VMEM((count, RADIX, 2 * PART, COLS), jnp.bfloat16),
            pltpu.VMEM((count, RADIX, ROWS, 4 * PART), jnp.bfloat16),
        ],
        compiler_params=pltpu.CompilerParams(vmem_limit_bytes=VMEM_LIMIT),
        cost_estimate=pl.CostEstimate(flops=5_000_000_000, bytes_accessed=10_000_000, transcendentals=0),
    )(where, sigma, *operands)


def body(strain_slots, templates, cutoffs, lists, owner, slides):
    me, owner = lax.axis_index("tpl"), owner[0]
    groups = lax.axis_size("grp")
    per_device = lists.shape[1]
    direct = per_device == groups and templates.shape[2] == WAVE_ROWS * COLS
    places = [(lax.axis_index("grp") - turn) % groups if direct else turn for turn in range(per_device)]

    picked = collect(templates, lists) if direct else collect_plain(templates, lists)
    strain_slots, picked = lax.optimization_barrier((strain_slots, picked))
    arrived = exchange(picked) if direct else picked
    where = jnp.stack([jnp.asarray(at, jnp.int32) for at in (me % CORES, me, *places)])
    found = []
    for det in range(DET):
        found.append(spread(strain_slots, det, owner))
    turns = slide_turns(slides)
    waves = [across(arrived, turn) for turn in range(per_device)] if direct else arrived
    masked, sigma = prepare(cutoffs, lists.reshape(-1), where, waves)
    result = ()
    for det in range(DET):
        result = detector(det, where, sigma, found[det], masked, turns, result)
    return result


def solution(mesh):
    in_specs = (
        P(("grp", "tpl"), None, None, None),
        P(None, None, "tpl"),
        P(),
        P(),
        P("grp"),
        P("grp"),
    )
    out_specs = (P(("grp", "tpl")), P(("grp", "tpl")))
    return jax.shard_map(body, mesh=mesh, in_specs=in_specs, out_specs=out_specs, check_vma=False)
```

```python
import functools

import jax
import jax.numpy as jnp
import numpy as np
from jax import lax
from jax.experimental import pallas as pl
from jax.experimental.pallas import tpu as pltpu
from jax.sharding import PartitionSpec as P

DET = 3
ROWS = 512
COLS = 512
RADIX = 4
PART = 128
ROW_STEP = 16
WAVE_ROWS = 32
SEND_ROWS = 32
CORES = 2
HALF_CHUNKS = 2
LAG = 2
VMEM_CHIPS = 8
VMEM_LIMIT = 32 * 1024 * 1024


two_pi = 6.283185307179586
eps_norm = 1e-06


def turn_table(left_ids, right_ids, period):
    angles = (left_ids[:, None] * right_ids[None, :] % period).astype(np.float64) * (2 * np.pi / period)
    return np.cos(angles), np.sin(angles)


def tables():
    part_ids, col_ids = np.arange(PART), np.arange(COLS)
    row_tables, col_tables, turns = [], [], []
    for residue in range(RADIX):
        cos, sin = turn_table(RADIX * part_ids + residue, part_ids, ROWS)
        row_tables.append(np.block([[cos, -sin], [sin, cos]]))
        col_tables.append(np.block([[cos.T, sin.T], [-sin.T, cos.T]] * 2))
        turns.append(np.stack(turn_table(RADIX * part_ids + residue, col_ids, ROWS * COLS)))
    return (
        jnp.asarray(np.stack(row_tables), jnp.float32).astype(jnp.bfloat16),
        jnp.asarray(np.stack(col_tables), jnp.float32).astype(jnp.bfloat16),
        jnp.asarray(np.stack(turns), jnp.float32),
    )


def slide_turns(slides):
    total = ROWS * COLS
    row_turns = (jnp.arange(ROWS, dtype=jnp.int32)[None, :] * (COLS * slides % total)[:, None]) % total
    col_turns = (jnp.arange(COLS, dtype=jnp.int32)[None, :] * slides[:, None]) % total
    row_angles = row_turns.astype(jnp.float32) * (two_pi / total)
    col_angles = col_turns.astype(jnp.float32) * (two_pi / total)
    rows = jnp.concatenate([jnp.cos(row_angles)[:, None], jnp.sin(row_angles)[:, None]] * 4, 1)
    cols = jnp.concatenate([jnp.cos(col_angles)[:, None], jnp.sin(col_angles)[:, None]] * 4, 1)
    return rows, cols


def ring_order(chips):
    return list(range(0, chips, 2)) + list(range(chips - 1 - chips % 2, 0, -2))


def to_partner():
    return [(i, i ^ 1) for i in range(lax.axis_size("tpl"))]


def half_chunks(strain_slots, det, owner):
    core = lax.axis_index("tpl") % CORES
    half = ROWS * COLS // CORES
    bins = half // HALF_CHUNKS
    side = lambda which: lax.dynamic_slice(strain_slots, (0, det, 0, which * half), (1, 1, 2, half))[0, 0]
    got = lax.ppermute(side(1 - core), "tpl", to_partner())
    first = jnp.where(core == owner % CORES, side(core), got)
    return [first[:, at : at + bins].reshape(2, bins // COLS, COLS) for at in range(0, half, bins)]


def spread(chunks, owner, hooks):
    devices = lax.axis_size("tpl")
    chips = devices // CORES
    order = ring_order(chips)
    chip, core = lax.axis_index("tpl") // CORES, lax.axis_index("tpl") % CORES
    on_owner_chip = chip == owner // CORES
    along = []
    for at in range(chips):
        along.append((order[at] * CORES, order[(at + 1) % chips] * CORES))
        along.append((order[(at + 1) % chips] * CORES + 1, order[at] * CORES + 1))
    sent, shared, arrived = [], [], []
    count = len(chunks)
    for slot in range(count + LAG * (chips - 1)):
        if slot < LAG:
            here = chunks[slot]
        elif slot < count:
            here = jnp.where(on_owner_chip, chunks[slot], arrived[slot - LAG])
        else:
            here = arrived[slot - LAG]
        if slot in hooks:
            here = hooks[slot](here, sent, shared)
        sent.append(here)
        shared.append(lax.ppermute(here, "tpl", to_partner()))
        if slot < count + LAG * (chips - 2):
            arrived.append(lax.ppermute(here, "tpl", along))
    return sent, shared


def distances(owner):
    chips = lax.axis_size("tpl") // CORES
    chip, core = lax.axis_index("tpl") // CORES, lax.axis_index("tpl") % CORES
    place = lambda at: jnp.where(at % 2 == 0, at // 2, chips - 1 - at // 2)
    forward = (place(chip) - place(owner // CORES)) % chips
    backward = (place(owner // CORES) - place(chip)) % chips
    return jnp.where(core == 0, forward, backward), jnp.where(core == 0, backward, forward)


def pick(templates, lists):
    devices, groups = lax.axis_size("tpl"), lax.axis_size("grp")
    own_group = lax.axis_index("grp")
    per_device = lists.shape[1]
    rows = templates.shape[2] // COLS
    pieces = per_device * 2
    if pieces % groups:
        groups, own_group = 1, jnp.int32(0)
    size = pieces // groups
    if size == 2 and rows == WAVE_ROWS:
        picked = templates[lax.dynamic_index_in_dim(lists, own_group, 1, keepdims=False)]
        picked = picked.reshape(devices, size, rows, COLS)
        parts = [picked[:, :, at : at + SEND_ROWS] for at in range(0, rows, SEND_ROWS)]
        return parts, [(own_group - turn) % groups for turn in range(groups)]
    picked = templates[lists.reshape(-1)].reshape(devices, pieces, rows, COLS)
    return [lax.dynamic_slice_in_dim(picked, own_group * size, size, 1)], None


def exchange(block):
    return lax.all_to_all(block, "tpl", split_axis=0, concat_axis=0, tiled=True)


def across(own):
    groups = lax.axis_size("grp")
    return [own] + [
        lax.ppermute(own, "grp", [(at, (at + turn) % groups) for at in range(groups)]) for turn in range(1, groups)
    ]


def assemble(own, per_device):
    groups = lax.axis_size("grp")
    found = jnp.stack(across(own) if per_device * 2 % groups == 0 else [own])
    found = found[(lax.axis_index("grp") - jnp.arange(found.shape[0])) % found.shape[0]]
    found = found.transpose(0, 2, 1, 3, 4).reshape(per_device, 2, ROWS // WAVE_ROWS, WAVE_ROWS, COLS)
    return [[found[at].transpose(1, 0, 2, 3)] for at in range(per_device)]


def quarters(parts):
    (re0, im0), (re1, im1), (re2, im2), (re3, im3) = parts
    even_re, even_im, odd_re, odd_im = re0 + re2, im0 + im2, re1 + re3, im1 + im3
    left_re, left_im, right_re, right_im = re0 - re2, im0 - im2, re1 - re3, im1 - im3
    return (
        (even_re + odd_re, even_im + odd_im),
        (left_re - right_im, left_im + right_re),
        (even_re - odd_re, even_im - odd_im),
        (left_re + right_im, left_im - right_re),
    )


def prepare_kernel(count, cut_ref, list_ref, where_ref, *refs):
    piece_refs, (masked_ref, sigma_ref) = refs[:-2], refs[-2:]
    pieces = len(piece_refs) // count
    rows = WAVE_ROWS // pieces
    for tpl in range(count):
        cutoff = cut_ref[list_ref[where_ref[2] * count + where_ref[4 + tpl]]]
        total = jnp.zeros((8, COLS), jnp.float32)
        for piece in range(pieces):
            wave_ref = piece_refs[tpl * pieces + piece]
            for block in range(ROWS // WAVE_ROWS):
                start = block * WAVE_ROWS + piece * rows
                bins = (lax.broadcasted_iota(jnp.int32, (rows, COLS), 0) + start) * COLS
                inside = bins + lax.broadcasted_iota(jnp.int32, (rows, COLS), 1) < cutoff
                wave_re = jnp.where(inside, wave_ref[block, 0].astype(jnp.float32), 0.0)
                wave_im = jnp.where(inside, wave_ref[block, 1].astype(jnp.float32), 0.0)
                masked_ref[tpl, 0, start : start + rows, :] = wave_re.astype(jnp.bfloat16)
                masked_ref[tpl, 1, start : start + rows, :] = wave_im.astype(jnp.bfloat16)
                squares = wave_re * wave_re + wave_im * wave_im
                total = total + jnp.sum(squares.reshape(-1, 8, COLS), axis=0)
        sigma_ref[tpl] = jnp.sum(total)


def detector_kernel(det, chips, where_ref, sigma_ref, *refs):
    first, last = det == 0, det == DET - 1
    slots = HALF_CHUNKS + LAG * (chips - 1)
    near_refs, far_refs, refs = refs[:slots], refs[slots : 2 * slots], refs[2 * slots :]
    masked, rphase_ref, cphase_ref, row_ref, col_ref, twiddle_ref = refs[:6]
    refs = refs[6:]
    before, refs = (None, refs) if first else (refs[0], refs[1:])
    outputs, (strain_ref, strain_sem, turned_ref, slid, stacked, twisted) = refs[:-6], refs[-6:]
    count = masked.shape[0]
    core, near, far = where_ref[0], where_ref[1], where_ref[3]
    half = ROWS // CORES
    rows = half // HALF_CHUNKS

    for slot_refs, distance, side in ((near_refs, near, core), (far_refs, far, 1 - core)):
        for away in range(chips):
            @pl.when(distance == away)
            def _():
                for at in range(HALF_CHUNKS):
                    into = pl.ds(pl.multiple_of(side * half + at * rows, rows), rows)
                    pltpu.make_async_copy(slot_refs[at + LAG * away], strain_ref.at[:, into, :], strain_sem).start()
    turned_ref[...] = rphase_ref[det].T
    cc, cs = cphase_ref[det, 0:1, :], cphase_ref[det, 1:2, :]
    pltpu.make_async_copy(strain_ref, strain_ref, strain_sem).wait()
    for at in range(0, ROWS, PART):
        part = slice(at, at + PART)
        rc, rs = turned_ref[part, 0:1], turned_ref[part, 1:2]
        turn_re = rc * cc - rs * cs
        turn_im = rc * cs + rs * cc
        data_re, data_im = strain_ref[0, part, :].astype(jnp.float32), strain_ref[1, part, :].astype(jnp.float32)
        slid[0, part, :] = data_re * turn_re - data_im * turn_im
        slid[1, part, :] = data_re * turn_im + data_im * turn_re

    largest = []
    for tpl in range(count):
        for at in range(0, PART, ROW_STEP):
            for col_at in range(0, COLS, PART):
                cols = slice(col_at, col_at + PART)
                parts = []
                for quarter in range(RADIX):
                    spot = slice(quarter * PART + at, quarter * PART + at + ROW_STEP)
                    wave_re = masked[tpl, 0, spot, cols].astype(jnp.float32)
                    wave_im = masked[tpl, 1, spot, cols].astype(jnp.float32)
                    data_re, data_im = slid[0, spot, cols], slid[1, spot, cols]
                    parts.append((data_re * wave_re + data_im * wave_im, data_im * wave_re - data_re * wave_im))
                for residue, (re, im) in enumerate(quarters(parts)):
                    stacked[tpl, residue, at : at + ROW_STEP, cols] = re.astype(jnp.bfloat16)
                    stacked[tpl, residue, PART + at : PART + at + ROW_STEP, cols] = im.astype(jnp.bfloat16)
        for residue in range(RADIX):
            section = jnp.dot(row_ref[residue], stacked[tpl, residue], preferred_element_type=jnp.float32)
            for at in range(0, PART, ROW_STEP):
                parts = []
                for quarter in range(RADIX):
                    cols = slice(quarter * PART, (quarter + 1) * PART)
                    re, im = section[at : at + ROW_STEP, cols], section[PART + at : PART + at + ROW_STEP, cols]
                    turn_re = twiddle_ref[residue, 0, at : at + ROW_STEP, cols]
                    turn_im = twiddle_ref[residue, 1, at : at + ROW_STEP, cols]
                    parts.append((re * turn_re - im * turn_im, re * turn_im + im * turn_re))
                spot = slice(residue * PART + at, residue * PART + at + ROW_STEP)
                for other, sums in enumerate(quarters(parts)):
                    for which, value in enumerate(sums):
                        high = value.astype(jnp.bfloat16)
                        low = (value - high.astype(jnp.float32)).astype(jnp.bfloat16)
                        twisted[tpl, other, spot, which * PART : (which + 1) * PART] = high
                        twisted[tpl, other, spot, (which + 2) * PART : (which + 3) * PART] = low
        peak = jnp.zeros((8, PART), jnp.float32)
        for other in range(RADIX):
            series = jnp.dot(twisted[tpl, other], col_ref[other], preferred_element_type=jnp.float32)
            squares = series[:, :PART] * series[:, :PART] + series[:, PART:] * series[:, PART:]
            cols = slice(other * PART, (other + 1) * PART)
            if not first:
                squares = squares + before[tpl, :, cols]
            if last:
                peak = jnp.maximum(peak, jnp.max(squares.reshape(-1, 8, PART), axis=0))
            else:
                outputs[0][tpl, :, cols] = squares
        largest.append(peak)

    if not last:
        outputs[1][0] = jnp.int32(0)
    if last:
        for tpl in range(count):
            place = where_ref[4 + tpl]
            outputs[0][place] = jnp.max(largest[tpl]) / (2.0 * (sigma_ref[tpl] + eps_norm))
            outputs[1][place] = sigma_ref[tpl] / (ROWS * COLS)


smem = pl.BlockSpec(memory_space=pltpu.SMEM)
vmem = pl.BlockSpec(memory_space=pltpu.VMEM)
anywhere = pl.BlockSpec(memory_space=pl.ANY)


def prepare(cutoffs, lists, where, waves):
    count = len(waves)
    operands = [piece for wave in waves for piece in wave]
    return pl.pallas_call(
        functools.partial(prepare_kernel, count),
        out_shape=(
            jax.ShapeDtypeStruct((count, 2, ROWS, COLS), jnp.bfloat16),
            jax.ShapeDtypeStruct((count,), jnp.float32),
        ),
        in_specs=[smem, smem, smem] + [vmem] * len(operands),
        out_specs=(vmem, smem),
        compiler_params=pltpu.CompilerParams(vmem_limit_bytes=VMEM_LIMIT),
        cost_estimate=pl.CostEstimate(flops=2_000_000_000, bytes_accessed=6_000_000, transcendentals=0),
    )(cutoffs, lists, where, *operands)


def detector(det, chips, where, sigma, sent, shared, masked, turns, before):
    count = masked.shape[0]
    slots = slice(det * HALF_CHUNKS, (det + 1) * HALF_CHUNKS + LAG * (chips - 1))
    found = [*sent[slots], *shared[slots]]
    last = det == DET - 1
    scalars = jax.ShapeDtypeStruct((count,), jnp.float32)
    operands = [masked, *turns, *tables(), *before[:1]]
    return pl.pallas_call(
        functools.partial(detector_kernel, det, chips),
        out_shape=(scalars, scalars)
        if last
        else (jax.ShapeDtypeStruct((count, ROWS, COLS), jnp.float32), jax.ShapeDtypeStruct((1,), jnp.int32)),
        in_specs=[smem, smem] + [vmem if chips <= VMEM_CHIPS else anywhere] * len(found) + [vmem] * len(operands),
        out_specs=(smem, smem) if last else (vmem, smem),
        scratch_shapes=[
            pltpu.VMEM((2, ROWS, COLS), jnp.bfloat16),
            pltpu.SemaphoreType.DMA,
            pltpu.VMEM((ROWS, 8), jnp.float32),
            pltpu.VMEM((2, ROWS, COLS), jnp.float32),
            pltpu.VMEM((count, RADIX, 2 * PART, COLS), jnp.bfloat16),
            pltpu.VMEM((count, RADIX, ROWS, 4 * PART), jnp.bfloat16),
        ],
        compiler_params=pltpu.CompilerParams(vmem_limit_bytes=VMEM_LIMIT),
        cost_estimate=pl.CostEstimate(flops=5_000_000_000, bytes_accessed=10_000_000, transcendentals=0),
    )(where, sigma, *found, *operands)


def body(strain_slots, templates, cutoffs, lists, owner, slides):
    me, owner = lax.axis_index("tpl"), owner[0]
    chips = lax.axis_size("tpl") // CORES
    per_device = lists.shape[1]
    chunks = [chunk for det in range(DET) for chunk in half_chunks(strain_slots, det, owner)]
    parts, places = pick(templates, lists)
    ids = list(range(per_device)) if places is None else places
    near, far = distances(owner)
    where = jnp.stack([jnp.asarray(at, jnp.int32) for at in (me % CORES, near, me, far, *ids)])
    arrived = exchange(parts[0])
    if places is None:
        waves = assemble(arrived, per_device)
    else:
        waves = [[wave] for wave in across(arrived)]
    turns = slide_turns(slides)
    masked, sigma = prepare(cutoffs, lists.reshape(-1), where, waves)
    results = [()]

    def filtered(det, sent, shared):
        results.append(detector(det, chips, where, sigma, sent, shared, masked, turns, results[-1]))

    def after_first(chunk, sent, shared):
        filtered(0, sent, shared)
        return jnp.where(results[-1][1][0] == 0, chunk, jnp.zeros_like(chunk))

    sent, shared = spread(chunks, owner, {HALF_CHUNKS - 1 + LAG * chips: after_first})
    for det in range(1, DET):
        filtered(det, sent, shared)
    return results[-1]


def solution(mesh):
    in_specs = (
        P(("grp", "tpl"), None, None, None),
        P(None, None, "tpl"),
        P(),
        P(),
        P("grp"),
        P("grp"),
    )
    out_specs = (P(("grp", "tpl")), P(("grp", "tpl")))
    return jax.shard_map(body, mesh=mesh, in_specs=in_specs, out_specs=out_specs, check_vma=False)
```

```python
import functools

import jax
import jax.numpy as jnp
import numpy as np
from jax import lax
from jax.experimental import pallas as pl
from jax.experimental.pallas import tpu as pltpu
from jax.sharding import PartitionSpec as P

DET = 3
ROWS = 512
COLS = 512
RADIX = 4
PART = 128
ROW_STEP = 16
WAVE_ROWS = 32
SEND_ROWS = 32
CORES = 2
HALF_CHUNKS = 2
LAG = 2
VMEM_LIMIT = 24 * 1024 * 1024


two_pi = 6.283185307179586
eps_norm = 1e-06


def turn_table(left_ids, right_ids, period):
    angles = (left_ids[:, None] * right_ids[None, :] % period).astype(np.float64) * (2 * np.pi / period)
    return np.cos(angles), np.sin(angles)


def tables():
    part_ids, col_ids = np.arange(PART), np.arange(COLS)
    row_tables, col_tables, turns = [], [], []
    for residue in range(RADIX):
        cos, sin = turn_table(RADIX * part_ids + residue, part_ids, ROWS)
        row_tables.append(np.block([[cos, -sin], [sin, cos]]))
        col_tables.append(np.block([[cos.T, sin.T], [-sin.T, cos.T]] * 2))
        turns.append(np.stack(turn_table(RADIX * part_ids + residue, col_ids, ROWS * COLS)))
    return (
        jnp.asarray(np.stack(row_tables), jnp.float32).astype(jnp.bfloat16),
        jnp.asarray(np.stack(col_tables), jnp.float32).astype(jnp.bfloat16),
        jnp.asarray(np.stack(turns), jnp.float32),
    )


def slide_turns(slides):
    total = ROWS * COLS
    row_turns = (jnp.arange(ROWS, dtype=jnp.int32)[None, :] * (COLS * slides % total)[:, None]) % total
    col_turns = (jnp.arange(COLS, dtype=jnp.int32)[None, :] * slides[:, None]) % total
    row_angles = row_turns.astype(jnp.float32) * (two_pi / total)
    col_angles = col_turns.astype(jnp.float32) * (two_pi / total)
    rows = jnp.concatenate([jnp.cos(row_angles)[:, None], jnp.sin(row_angles)[:, None]] * 4, 1)
    cols = jnp.concatenate([jnp.cos(col_angles)[:, None], jnp.sin(col_angles)[:, None]] * 4, 1)
    return rows, cols


def ring_order(chips):
    return list(range(0, chips, 2)) + list(range(chips - 1 - chips % 2, 0, -2))


def to_partner():
    return [(i, i ^ 1) for i in range(lax.axis_size("tpl"))]


def half_chunks(strain_slots, det, owner):
    core = lax.axis_index("tpl") % CORES
    half = ROWS * COLS // CORES
    bins = half // HALF_CHUNKS
    side = lambda which: lax.dynamic_slice(strain_slots, (0, det, 0, which * half), (1, 1, 2, half))[0, 0]
    got = lax.ppermute(side(1 - core), "tpl", to_partner())
    first = jnp.where(core == owner % CORES, side(core), got)
    return [first[:, at : at + bins].reshape(2, bins // COLS, COLS) for at in range(0, half, bins)]


def spread(chunks, owner):
    devices = lax.axis_size("tpl")
    chips = devices // CORES
    order = ring_order(chips)
    chip, core = lax.axis_index("tpl") // CORES, lax.axis_index("tpl") % CORES
    on_owner_chip = chip == owner // CORES
    along = []
    for at in range(chips):
        along.append((order[at] * CORES, order[(at + 1) % chips] * CORES))
        along.append((order[(at + 1) % chips] * CORES + 1, order[at] * CORES + 1))
    sent, shared, arrived = [], [], []
    count = len(chunks)
    for slot in range(count + LAG * (chips - 1)):
        if slot < LAG:
            here = chunks[slot]
        elif slot < count:
            here = jnp.where(on_owner_chip, chunks[slot], arrived[slot - LAG])
        else:
            here = arrived[slot - LAG]
        sent.append(here)
        shared.append(lax.ppermute(here, "tpl", to_partner()))
        if slot < count + LAG * (chips - 2):
            arrived.append(lax.ppermute(here, "tpl", along))
    return sent, shared


def distances(owner):
    chips = lax.axis_size("tpl") // CORES
    chip, core = lax.axis_index("tpl") // CORES, lax.axis_index("tpl") % CORES
    place = lambda at: jnp.where(at % 2 == 0, at // 2, chips - 1 - at // 2)
    forward = (place(chip) - place(owner // CORES)) % chips
    backward = (place(owner // CORES) - place(chip)) % chips
    return jnp.where(core == 0, forward, backward), jnp.where(core == 0, backward, forward)


def pick(templates, lists):
    devices, groups = lax.axis_size("tpl"), lax.axis_size("grp")
    own_group = lax.axis_index("grp")
    per_device = lists.shape[1]
    rows = templates.shape[2] // COLS
    pieces = per_device * 2
    if pieces % groups:
        groups, own_group = 1, jnp.int32(0)
    size = pieces // groups
    if size == 2 and rows == WAVE_ROWS:
        picked = templates[lax.dynamic_index_in_dim(lists, own_group, 1, keepdims=False)]
        picked = picked.reshape(devices, size, rows, COLS)
        parts = [picked[:, :, at : at + SEND_ROWS] for at in range(0, rows, SEND_ROWS)]
        return parts, [(own_group - turn) % groups for turn in range(groups)]
    picked = templates[lists.reshape(-1)].reshape(devices, pieces, rows, COLS)
    return [lax.dynamic_slice_in_dim(picked, own_group * size, size, 1)], None


def exchange(block):
    return lax.all_to_all(block, "tpl", split_axis=0, concat_axis=0, tiled=True)


def across(own):
    groups = lax.axis_size("grp")
    return [own] + [
        lax.ppermute(own, "grp", [(at, (at + turn) % groups) for at in range(groups)]) for turn in range(1, groups)
    ]


def assemble(own, per_device):
    groups = lax.axis_size("grp")
    found = jnp.stack(across(own) if per_device * 2 % groups == 0 else [own])
    found = found[(lax.axis_index("grp") - jnp.arange(found.shape[0])) % found.shape[0]]
    found = found.transpose(0, 2, 1, 3, 4).reshape(per_device, 2, ROWS // WAVE_ROWS, WAVE_ROWS, COLS)
    return [[found[at].transpose(1, 0, 2, 3)] for at in range(per_device)]


def quarters(parts):
    (re0, im0), (re1, im1), (re2, im2), (re3, im3) = parts
    even_re, even_im, odd_re, odd_im = re0 + re2, im0 + im2, re1 + re3, im1 + im3
    left_re, left_im, right_re, right_im = re0 - re2, im0 - im2, re1 - re3, im1 - im3
    return (
        (even_re + odd_re, even_im + odd_im),
        (left_re - right_im, left_im + right_re),
        (even_re - odd_re, even_im - odd_im),
        (left_re + right_im, left_im - right_re),
    )


def prepare_kernel(count, cut_ref, list_ref, where_ref, *refs):
    piece_refs, (masked_ref, sigma_ref) = refs[:-2], refs[-2:]
    pieces = len(piece_refs) // count
    rows = WAVE_ROWS // pieces
    for tpl in range(count):
        cutoff = cut_ref[list_ref[where_ref[2] * count + where_ref[4 + tpl]]]
        total = jnp.zeros((8, COLS), jnp.float32)
        for piece in range(pieces):
            wave_ref = piece_refs[tpl * pieces + piece]
            for block in range(ROWS // WAVE_ROWS):
                start = block * WAVE_ROWS + piece * rows
                bins = (lax.broadcasted_iota(jnp.int32, (rows, COLS), 0) + start) * COLS
                inside = bins + lax.broadcasted_iota(jnp.int32, (rows, COLS), 1) < cutoff
                wave_re = jnp.where(inside, wave_ref[block, 0].astype(jnp.float32), 0.0)
                wave_im = jnp.where(inside, wave_ref[block, 1].astype(jnp.float32), 0.0)
                masked_ref[tpl, 0, start : start + rows, :] = wave_re.astype(jnp.bfloat16)
                masked_ref[tpl, 1, start : start + rows, :] = wave_im.astype(jnp.bfloat16)
                squares = wave_re * wave_re + wave_im * wave_im
                total = total + jnp.sum(squares.reshape(-1, 8, COLS), axis=0)
        sigma_ref[tpl] = jnp.sum(total)


def detector_kernel(det, chips, where_ref, sigma_ref, *refs):
    first, last = det == 0, det == DET - 1
    slots = HALF_CHUNKS + LAG * (chips - 1)
    near_refs, far_refs, refs = refs[:slots], refs[slots : 2 * slots], refs[2 * slots :]
    masked, rphase_ref, cphase_ref, row_ref, col_ref, twiddle_ref = refs[:6]
    refs = refs[6:]
    before, refs = (None, refs) if first else (refs[0], refs[1:])
    outputs, (strain_ref, strain_sem, turned_ref, slid, stacked, twisted) = refs[:-6], refs[-6:]
    count = masked.shape[0]
    core, near, far = where_ref[0], where_ref[1], where_ref[3]
    half = ROWS // CORES
    rows = half // HALF_CHUNKS

    for slot_refs, distance, side in ((near_refs, near, core), (far_refs, far, 1 - core)):
        for away in range(chips):
            @pl.when(distance == away)
            def _():
                for at in range(HALF_CHUNKS):
                    into = pl.ds(pl.multiple_of(side * half + at * rows, rows), rows)
                    pltpu.make_async_copy(slot_refs[at + LAG * away], strain_ref.at[:, into, :], strain_sem).start()
    turned_ref[...] = rphase_ref[det].T
    cc, cs = cphase_ref[det, 0:1, :], cphase_ref[det, 1:2, :]
    pltpu.make_async_copy(strain_ref, strain_ref, strain_sem).wait()
    for at in range(0, ROWS, PART):
        part = slice(at, at + PART)
        rc, rs = turned_ref[part, 0:1], turned_ref[part, 1:2]
        turn_re = rc * cc - rs * cs
        turn_im = rc * cs + rs * cc
        data_re, data_im = strain_ref[0, part, :].astype(jnp.float32), strain_ref[1, part, :].astype(jnp.float32)
        slid[0, part, :] = data_re * turn_re - data_im * turn_im
        slid[1, part, :] = data_re * turn_im + data_im * turn_re

    largest = []
    for tpl in range(count):
        for at in range(0, PART, ROW_STEP):
            for col_at in range(0, COLS, PART):
                cols = slice(col_at, col_at + PART)
                parts = []
                for quarter in range(RADIX):
                    spot = slice(quarter * PART + at, quarter * PART + at + ROW_STEP)
                    wave_re = masked[tpl, 0, spot, cols].astype(jnp.float32)
                    wave_im = masked[tpl, 1, spot, cols].astype(jnp.float32)
                    data_re, data_im = slid[0, spot, cols], slid[1, spot, cols]
                    parts.append((data_re * wave_re + data_im * wave_im, data_im * wave_re - data_re * wave_im))
                for residue, (re, im) in enumerate(quarters(parts)):
                    stacked[tpl, residue, at : at + ROW_STEP, cols] = re.astype(jnp.bfloat16)
                    stacked[tpl, residue, PART + at : PART + at + ROW_STEP, cols] = im.astype(jnp.bfloat16)
        for residue in range(RADIX):
            section = jnp.dot(row_ref[residue], stacked[tpl, residue], preferred_element_type=jnp.float32)
            for at in range(0, PART, ROW_STEP):
                parts = []
                for quarter in range(RADIX):
                    cols = slice(quarter * PART, (quarter + 1) * PART)
                    re, im = section[at : at + ROW_STEP, cols], section[PART + at : PART + at + ROW_STEP, cols]
                    turn_re = twiddle_ref[residue, 0, at : at + ROW_STEP, cols]
                    turn_im = twiddle_ref[residue, 1, at : at + ROW_STEP, cols]
                    parts.append((re * turn_re - im * turn_im, re * turn_im + im * turn_re))
                spot = slice(residue * PART + at, residue * PART + at + ROW_STEP)
                for other, sums in enumerate(quarters(parts)):
                    for which, value in enumerate(sums):
                        high = value.astype(jnp.bfloat16)
                        low = (value - high.astype(jnp.float32)).astype(jnp.bfloat16)
                        twisted[tpl, other, spot, which * PART : (which + 1) * PART] = high
                        twisted[tpl, other, spot, (which + 2) * PART : (which + 3) * PART] = low
        peak = jnp.zeros((8, PART), jnp.float32)
        for other in range(RADIX):
            series = jnp.dot(twisted[tpl, other], col_ref[other], preferred_element_type=jnp.float32)
            squares = series[:, :PART] * series[:, :PART] + series[:, PART:] * series[:, PART:]
            cols = slice(other * PART, (other + 1) * PART)
            if not first:
                squares = squares + before[tpl, :, cols]
            if last:
                peak = jnp.maximum(peak, jnp.max(squares.reshape(-1, 8, PART), axis=0))
            else:
                outputs[0][tpl, :, cols] = squares
        largest.append(peak)

    if last:
        for tpl in range(count):
            place = where_ref[4 + tpl]
            outputs[0][place] = jnp.max(largest[tpl]) / (2.0 * (sigma_ref[tpl] + eps_norm))
            outputs[1][place] = sigma_ref[tpl] / (ROWS * COLS)


smem = pl.BlockSpec(memory_space=pltpu.SMEM)
vmem = pl.BlockSpec(memory_space=pltpu.VMEM)
anywhere = pl.BlockSpec(memory_space=pl.ANY)


def prepare(cutoffs, lists, where, waves):
    count = len(waves)
    operands = [piece for wave in waves for piece in wave]
    return pl.pallas_call(
        functools.partial(prepare_kernel, count),
        out_shape=(
            jax.ShapeDtypeStruct((count, 2, ROWS, COLS), jnp.bfloat16),
            jax.ShapeDtypeStruct((count,), jnp.float32),
        ),
        in_specs=[smem, smem, smem] + [vmem] * len(operands),
        out_specs=(vmem, smem),
        compiler_params=pltpu.CompilerParams(vmem_limit_bytes=VMEM_LIMIT),
        cost_estimate=pl.CostEstimate(flops=2_000_000_000, bytes_accessed=6_000_000, transcendentals=0),
    )(cutoffs, lists, where, *operands)


def detector(det, chips, where, sigma, sent, shared, masked, turns, before):
    count = masked.shape[0]
    slots = slice(det * HALF_CHUNKS, (det + 1) * HALF_CHUNKS + LAG * (chips - 1))
    found = [*sent[slots], *shared[slots]]
    last = det == DET - 1
    scalars = jax.ShapeDtypeStruct((count,), jnp.float32)
    operands = [masked, *turns, *tables(), *before]
    return pl.pallas_call(
        functools.partial(detector_kernel, det, chips),
        out_shape=(scalars, scalars) if last else (jax.ShapeDtypeStruct((count, ROWS, COLS), jnp.float32),),
        in_specs=[smem, smem] + [anywhere] * len(found) + [vmem] * len(operands),
        out_specs=(smem, smem) if last else (vmem,),
        scratch_shapes=[
            pltpu.VMEM((2, ROWS, COLS), jnp.bfloat16),
            pltpu.SemaphoreType.DMA,
            pltpu.VMEM((ROWS, 8), jnp.float32),
            pltpu.VMEM((2, ROWS, COLS), jnp.float32),
            pltpu.VMEM((count, RADIX, 2 * PART, COLS), jnp.bfloat16),
            pltpu.VMEM((count, RADIX, ROWS, 4 * PART), jnp.bfloat16),
        ],
        compiler_params=pltpu.CompilerParams(vmem_limit_bytes=VMEM_LIMIT),
        cost_estimate=pl.CostEstimate(flops=5_000_000_000, bytes_accessed=10_000_000, transcendentals=0),
    )(where, sigma, *found, *operands)


def body(strain_slots, templates, cutoffs, lists, owner, slides):
    me, owner = lax.axis_index("tpl"), owner[0]
    chips = lax.axis_size("tpl") // CORES
    per_device = lists.shape[1]
    chunks = [chunk for det in range(DET) for chunk in half_chunks(strain_slots, det, owner)]
    parts, places = pick(templates, lists)
    ids = list(range(per_device)) if places is None else places
    near, far = distances(owner)
    where = jnp.stack([jnp.asarray(at, jnp.int32) for at in (me % CORES, near, me, far, *ids)])
    arrived = exchange(parts[0])
    if places is None:
        waves = assemble(arrived, per_device)
    else:
        waves = [[wave] for wave in across(arrived)]
    turns = slide_turns(slides)
    masked, sigma = prepare(cutoffs, lists.reshape(-1), where, waves)
    sent, shared = spread(chunks, owner)
    result = ()
    for det in range(DET):
        result = detector(det, chips, where, sigma, sent, shared, masked, turns, result)
    return result


def solution(mesh):
    in_specs = (
        P(("grp", "tpl"), None, None, None),
        P(None, None, "tpl"),
        P(),
        P(),
        P("grp"),
        P("grp"),
    )
    out_specs = (P(("grp", "tpl")), P(("grp", "tpl")))
    return jax.shard_map(body, mesh=mesh, in_specs=in_specs, out_specs=out_specs, check_vma=False)
```

```python
import functools

import jax
import jax.numpy as jnp
import numpy as np
from jax import lax
from jax.experimental import pallas as pl
from jax.experimental.pallas import tpu as pltpu
from jax.sharding import PartitionSpec as P

DET = 3
ROWS = 512
COLS = 512
RADIX = 4
PART = 128
ROW_STEP = 16
WAVE_ROWS = 32
SEND_ROWS = 32
CORES = 2
HALF_CHUNKS = 2
LAG = 2
TEMPLATE_SLOT = 4
MASKED_SLOT = 12
VMEM_LIMIT = 24 * 1024 * 1024


two_pi = 6.283185307179586
eps_norm = 1e-06


def turn_table(left_ids, right_ids, period):
    angles = (left_ids[:, None] * right_ids[None, :] % period).astype(np.float64) * (2 * np.pi / period)
    return np.cos(angles), np.sin(angles)


def tables():
    part_ids, col_ids = np.arange(PART), np.arange(COLS)
    row_tables, col_tables, turns = [], [], []
    for residue in range(RADIX):
        cos, sin = turn_table(RADIX * part_ids + residue, part_ids, ROWS)
        row_tables.append(np.block([[cos, -sin], [sin, cos]]))
        col_tables.append(np.block([[cos.T, sin.T], [-sin.T, cos.T]] * 2))
        turns.append(np.stack(turn_table(RADIX * part_ids + residue, col_ids, ROWS * COLS)))
    return (
        jnp.asarray(np.stack(row_tables), jnp.float32).astype(jnp.bfloat16),
        jnp.asarray(np.stack(col_tables), jnp.float32).astype(jnp.bfloat16),
        jnp.asarray(np.stack(turns), jnp.float32),
    )


def slide_turns(slides):
    total = ROWS * COLS
    row_turns = (jnp.arange(ROWS, dtype=jnp.int32)[None, :] * (COLS * slides % total)[:, None]) % total
    col_turns = (jnp.arange(COLS, dtype=jnp.int32)[None, :] * slides[:, None]) % total
    row_angles = row_turns.astype(jnp.float32) * (two_pi / total)
    col_angles = col_turns.astype(jnp.float32) * (two_pi / total)
    rows = jnp.concatenate([jnp.cos(row_angles)[:, None], jnp.sin(row_angles)[:, None]] * 4, 1)
    cols = jnp.concatenate([jnp.cos(col_angles)[:, None], jnp.sin(col_angles)[:, None]] * 4, 1)
    return rows, cols


def ring_order(chips):
    return list(range(0, chips, 2)) + list(range(chips - 1 - chips % 2, 0, -2))


def to_partner():
    return [(i, i ^ 1) for i in range(lax.axis_size("tpl"))]


def half_chunks(strain_slots, det, owner):
    core = lax.axis_index("tpl") % CORES
    half = ROWS * COLS // CORES
    bins = half // HALF_CHUNKS
    side = lambda which: lax.dynamic_slice(strain_slots, (0, det, 0, which * half), (1, 1, 2, half))[0, 0]
    got = lax.ppermute(side(1 - core), "tpl", to_partner())
    first = jnp.where(core == owner % CORES, side(core), got)
    return [first[:, at : at + bins].reshape(2, bins // COLS, COLS) for at in range(0, half, bins)]


def spread(chunks, owner, hooks):
    devices = lax.axis_size("tpl")
    chips = devices // CORES
    order = ring_order(chips)
    chip, core = lax.axis_index("tpl") // CORES, lax.axis_index("tpl") % CORES
    on_owner_chip = chip == owner // CORES
    along = []
    for at in range(chips):
        along.append((order[at] * CORES, order[(at + 1) % chips] * CORES))
        along.append((order[(at + 1) % chips] * CORES + 1, order[at] * CORES + 1))
    sent, arrived = [], []
    count = len(chunks)
    for slot in range(count + LAG * (chips - 1)):
        if slot < LAG:
            here = chunks[slot]
        elif slot < count:
            here = jnp.where(on_owner_chip, chunks[slot], arrived[slot - LAG])
        else:
            here = arrived[slot - LAG]
        if slot in hooks:
            here = hooks[slot](here)
        sent.append(here)
        if slot < count + LAG * (chips - 2):
            arrived.append(lax.ppermute(here, "tpl", along))
    shared = [lax.ppermute(here, "tpl", to_partner()) for here in sent]
    return sent, shared


def distances(owner):
    chips = lax.axis_size("tpl") // CORES
    chip, core = lax.axis_index("tpl") // CORES, lax.axis_index("tpl") % CORES
    place = lambda at: jnp.where(at % 2 == 0, at // 2, chips - 1 - at // 2)
    forward = (place(chip) - place(owner // CORES)) % chips
    backward = (place(owner // CORES) - place(chip)) % chips
    return jnp.where(core == 0, forward, backward), jnp.where(core == 0, backward, forward)


def pick(templates, lists):
    devices, groups = lax.axis_size("tpl"), lax.axis_size("grp")
    own_group = lax.axis_index("grp")
    per_device = lists.shape[1]
    rows = templates.shape[2] // COLS
    pieces = per_device * 2
    if pieces % groups:
        groups, own_group = 1, jnp.int32(0)
    size = pieces // groups
    if size == 2 and rows == WAVE_ROWS:
        picked = templates[lax.dynamic_index_in_dim(lists, own_group, 1, keepdims=False)]
        picked = picked.reshape(devices, size, rows, COLS)
        parts = [picked[:, :, at : at + SEND_ROWS] for at in range(0, rows, SEND_ROWS)]
        return parts, [(own_group - turn) % groups for turn in range(groups)]
    picked = templates[lists.reshape(-1)].reshape(devices, pieces, rows, COLS)
    return [lax.dynamic_slice_in_dim(picked, own_group * size, size, 1)], None


def exchange(block):
    return lax.all_to_all(block, "tpl", split_axis=0, concat_axis=0, tiled=True)


def across(own):
    groups = lax.axis_size("grp")
    return [own] + [
        lax.ppermute(own, "grp", [(at, (at + turn) % groups) for at in range(groups)]) for turn in range(1, groups)
    ]


def assemble(own, per_device):
    groups = lax.axis_size("grp")
    found = jnp.stack(across(own) if per_device * 2 % groups == 0 else [own])
    found = found[(lax.axis_index("grp") - jnp.arange(found.shape[0])) % found.shape[0]]
    found = found.transpose(0, 2, 1, 3, 4).reshape(per_device, 2, ROWS // WAVE_ROWS, WAVE_ROWS, COLS)
    return [[found[at].transpose(1, 0, 2, 3)] for at in range(per_device)]


def quarters(parts):
    (re0, im0), (re1, im1), (re2, im2), (re3, im3) = parts
    even_re, even_im, odd_re, odd_im = re0 + re2, im0 + im2, re1 + re3, im1 + im3
    left_re, left_im, right_re, right_im = re0 - re2, im0 - im2, re1 - re3, im1 - im3
    return (
        (even_re + odd_re, even_im + odd_im),
        (left_re - right_im, left_im + right_re),
        (even_re - odd_re, even_im - odd_im),
        (left_re + right_im, left_im - right_re),
    )


def prepare_kernel(count, cut_ref, list_ref, where_ref, *refs):
    piece_refs, (masked_ref, sigma_ref) = refs[:-2], refs[-2:]
    pieces = len(piece_refs) // count
    rows = WAVE_ROWS // pieces
    for tpl in range(count):
        cutoff = cut_ref[list_ref[where_ref[2] * count + where_ref[4 + tpl]]]
        total = jnp.zeros((8, COLS), jnp.float32)
        for piece in range(pieces):
            wave_ref = piece_refs[tpl * pieces + piece]
            for block in range(ROWS // WAVE_ROWS):
                start = block * WAVE_ROWS + piece * rows
                bins = (lax.broadcasted_iota(jnp.int32, (rows, COLS), 0) + start) * COLS
                inside = bins + lax.broadcasted_iota(jnp.int32, (rows, COLS), 1) < cutoff
                wave_re = jnp.where(inside, wave_ref[block, 0].astype(jnp.float32), 0.0)
                wave_im = jnp.where(inside, wave_ref[block, 1].astype(jnp.float32), 0.0)
                masked_ref[tpl, 0, start : start + rows, :] = wave_re.astype(jnp.bfloat16)
                masked_ref[tpl, 1, start : start + rows, :] = wave_im.astype(jnp.bfloat16)
                squares = wave_re * wave_re + wave_im * wave_im
                total = total + jnp.sum(squares.reshape(-1, 8, COLS), axis=0)
        sigma_ref[tpl] = jnp.sum(total)


def detector_kernel(det, chips, where_ref, sigma_ref, *refs):
    first, last = det == 0, det == DET - 1
    slots = HALF_CHUNKS + LAG * (chips - 1)
    near_refs, far_refs, refs = refs[:slots], refs[slots : 2 * slots], refs[2 * slots :]
    masked, rphase_ref, cphase_ref, row_ref, col_ref, twiddle_ref = refs[:6]
    refs = refs[6:]
    before, refs = (None, refs) if first else (refs[0], refs[1:])
    outputs, (strain_ref, strain_sem, turned_ref, slid, stacked, twisted) = refs[:-6], refs[-6:]
    count = masked.shape[0]
    core, near, far = where_ref[0], where_ref[1], where_ref[3]
    half = ROWS // CORES
    rows = half // HALF_CHUNKS

    for slot_refs, distance, side in ((near_refs, near, core), (far_refs, far, 1 - core)):
        for away in range(chips):
            @pl.when(distance == away)
            def _():
                for at in range(HALF_CHUNKS):
                    into = pl.ds(pl.multiple_of(side * half + at * rows, rows), rows)
                    pltpu.make_async_copy(slot_refs[at + LAG * away], strain_ref.at[:, into, :], strain_sem).start()
    turned_ref[...] = rphase_ref[det].T
    cc, cs = cphase_ref[det, 0:1, :], cphase_ref[det, 1:2, :]
    pltpu.make_async_copy(strain_ref, strain_ref, strain_sem).wait()
    for at in range(0, ROWS, PART):
        part = slice(at, at + PART)
        rc, rs = turned_ref[part, 0:1], turned_ref[part, 1:2]
        turn_re = rc * cc - rs * cs
        turn_im = rc * cs + rs * cc
        data_re, data_im = strain_ref[0, part, :].astype(jnp.float32), strain_ref[1, part, :].astype(jnp.float32)
        slid[0, part, :] = data_re * turn_re - data_im * turn_im
        slid[1, part, :] = data_re * turn_im + data_im * turn_re

    largest = []
    for tpl in range(count):
        for at in range(0, PART, ROW_STEP):
            for col_at in range(0, COLS, PART):
                cols = slice(col_at, col_at + PART)
                parts = []
                for quarter in range(RADIX):
                    spot = slice(quarter * PART + at, quarter * PART + at + ROW_STEP)
                    wave_re = masked[tpl, 0, spot, cols].astype(jnp.float32)
                    wave_im = masked[tpl, 1, spot, cols].astype(jnp.float32)
                    data_re, data_im = slid[0, spot, cols], slid[1, spot, cols]
                    parts.append((data_re * wave_re + data_im * wave_im, data_im * wave_re - data_re * wave_im))
                for residue, (re, im) in enumerate(quarters(parts)):
                    stacked[tpl, residue, at : at + ROW_STEP, cols] = re.astype(jnp.bfloat16)
                    stacked[tpl, residue, PART + at : PART + at + ROW_STEP, cols] = im.astype(jnp.bfloat16)
        for residue in range(RADIX):
            section = jnp.dot(row_ref[residue], stacked[tpl, residue], preferred_element_type=jnp.float32)
            for at in range(0, PART, ROW_STEP):
                parts = []
                for quarter in range(RADIX):
                    cols = slice(quarter * PART, (quarter + 1) * PART)
                    re, im = section[at : at + ROW_STEP, cols], section[PART + at : PART + at + ROW_STEP, cols]
                    turn_re = twiddle_ref[residue, 0, at : at + ROW_STEP, cols]
                    turn_im = twiddle_ref[residue, 1, at : at + ROW_STEP, cols]
                    parts.append((re * turn_re - im * turn_im, re * turn_im + im * turn_re))
                spot = slice(residue * PART + at, residue * PART + at + ROW_STEP)
                for other, sums in enumerate(quarters(parts)):
                    for which, value in enumerate(sums):
                        high = value.astype(jnp.bfloat16)
                        low = (value - high.astype(jnp.float32)).astype(jnp.bfloat16)
                        twisted[tpl, other, spot, which * PART : (which + 1) * PART] = high
                        twisted[tpl, other, spot, (which + 2) * PART : (which + 3) * PART] = low
        peak = jnp.zeros((8, PART), jnp.float32)
        for other in range(RADIX):
            series = jnp.dot(twisted[tpl, other], col_ref[other], preferred_element_type=jnp.float32)
            squares = series[:, :PART] * series[:, :PART] + series[:, PART:] * series[:, PART:]
            cols = slice(other * PART, (other + 1) * PART)
            if not first:
                squares = squares + before[tpl, :, cols]
            if last:
                peak = jnp.maximum(peak, jnp.max(squares.reshape(-1, 8, PART), axis=0))
            else:
                outputs[0][tpl, :, cols] = squares
        largest.append(peak)

    if last:
        for tpl in range(count):
            place = where_ref[4 + tpl]
            outputs[0][place] = jnp.max(largest[tpl]) / (2.0 * (sigma_ref[tpl] + eps_norm))
            outputs[1][place] = sigma_ref[tpl] / (ROWS * COLS)


smem = pl.BlockSpec(memory_space=pltpu.SMEM)
vmem = pl.BlockSpec(memory_space=pltpu.VMEM)
anywhere = pl.BlockSpec(memory_space=pl.ANY)


def prepare(cutoffs, lists, where, waves):
    count = len(waves)
    operands = [piece for wave in waves for piece in wave]
    return pl.pallas_call(
        functools.partial(prepare_kernel, count),
        out_shape=(
            jax.ShapeDtypeStruct((count, 2, ROWS, COLS), jnp.bfloat16),
            jax.ShapeDtypeStruct((count,), jnp.float32),
        ),
        in_specs=[smem, smem, smem] + [vmem] * len(operands),
        out_specs=(vmem, smem),
        compiler_params=pltpu.CompilerParams(vmem_limit_bytes=VMEM_LIMIT),
        cost_estimate=pl.CostEstimate(flops=2_000_000_000, bytes_accessed=6_000_000, transcendentals=0),
    )(cutoffs, lists, where, *operands)


def detector(det, chips, where, sigma, sent, shared, masked, turns, before):
    count = masked.shape[0]
    slots = slice(det * HALF_CHUNKS, (det + 1) * HALF_CHUNKS + LAG * (chips - 1))
    found = [*sent[slots], *shared[slots]]
    last = det == DET - 1
    scalars = jax.ShapeDtypeStruct((count,), jnp.float32)
    operands = [masked, *turns, *tables(), *before]
    return pl.pallas_call(
        functools.partial(detector_kernel, det, chips),
        out_shape=(scalars, scalars) if last else (jax.ShapeDtypeStruct((count, ROWS, COLS), jnp.float32),),
        in_specs=[smem, smem] + [anywhere] * len(found) + [vmem] * len(operands),
        out_specs=(smem, smem) if last else (vmem,),
        scratch_shapes=[
            pltpu.VMEM((2, ROWS, COLS), jnp.bfloat16),
            pltpu.SemaphoreType.DMA,
            pltpu.VMEM((ROWS, 8), jnp.float32),
            pltpu.VMEM((2, ROWS, COLS), jnp.float32),
            pltpu.VMEM((count, RADIX, 2 * PART, COLS), jnp.bfloat16),
            pltpu.VMEM((count, RADIX, ROWS, 4 * PART), jnp.bfloat16),
        ],
        compiler_params=pltpu.CompilerParams(vmem_limit_bytes=VMEM_LIMIT),
        cost_estimate=pl.CostEstimate(flops=5_000_000_000, bytes_accessed=10_000_000, transcendentals=0),
    )(where, sigma, *found, *operands)


def body(strain_slots, templates, cutoffs, lists, owner, slides):
    me, owner = lax.axis_index("tpl"), owner[0]
    chips = lax.axis_size("tpl") // CORES
    per_device = lists.shape[1]
    chunks = [chunk for det in range(DET) for chunk in half_chunks(strain_slots, det, owner)]
    parts, places = pick(templates, lists)
    ids = list(range(per_device)) if places is None else places
    near, far = distances(owner)
    where = jnp.stack([jnp.asarray(at, jnp.int32) for at in (me % CORES, near, me, far, *ids)])
    held = {"arrived": exchange(parts[0]), "small": (slide_turns(slides), where, lists.reshape(-1))}

    def templates_here(chunk):
        chunk, held["arrived"], held["small"] = lax.optimization_barrier((chunk, held["arrived"], held["small"]))
        if places is None:
            waves = assemble(held["arrived"], per_device)
        else:
            waves = [[wave] for wave in across(held["arrived"])]
        _, where, flat_list = held["small"]
        held["masked"] = prepare(cutoffs, flat_list, where, waves)
        return chunk

    def masked_here(chunk):
        chunk, held["masked"] = lax.optimization_barrier((chunk, held["masked"]))
        return chunk

    sent, shared = spread(chunks, owner, {TEMPLATE_SLOT: templates_here, MASKED_SLOT: masked_here})
    turns, where, _ = held["small"]
    masked, sigma = held["masked"]
    result = ()
    for det in range(DET):
        result = detector(det, chips, where, sigma, sent, shared, masked, turns, result)
    return result


def solution(mesh):
    in_specs = (
        P(("grp", "tpl"), None, None, None),
        P(None, None, "tpl"),
        P(),
        P(),
        P("grp"),
        P("grp"),
    )
    out_specs = (P(("grp", "tpl")), P(("grp", "tpl")))
    return jax.shard_map(body, mesh=mesh, in_specs=in_specs, out_specs=out_specs, check_vma=False)
```

```python
import functools

import jax
import jax.numpy as jnp
import numpy as np
from jax import lax
from jax.experimental import pallas as pl
from jax.experimental.pallas import tpu as pltpu
from jax.sharding import PartitionSpec as P

DET = 3
ROWS = 512
COLS = 512
RADIX = 4
PART = 128
ROW_STEP = 16
WAVE_ROWS = 32
SEND_ROWS = 32
CORES = 2
HALF_CHUNKS = 2
LAG = 2
TEMPLATE_SLOT = 4
MASKED_SLOT = 12
VMEM_LIMIT = 16 * 1024 * 1024


two_pi = 6.283185307179586
eps_norm = 1e-06


def turn_table(left_ids, right_ids, period):
    angles = (left_ids[:, None] * right_ids[None, :] % period).astype(np.float64) * (2 * np.pi / period)
    return np.cos(angles), np.sin(angles)


def tables():
    part_ids, col_ids = np.arange(PART), np.arange(COLS)
    row_tables, col_tables, turns = [], [], []
    for residue in range(RADIX):
        cos, sin = turn_table(RADIX * part_ids + residue, part_ids, ROWS)
        row_tables.append(np.block([[cos, -sin], [sin, cos]]))
        col_tables.append(np.block([[cos.T, sin.T], [-sin.T, cos.T]] * 2))
        turns.append(np.stack(turn_table(RADIX * part_ids + residue, col_ids, ROWS * COLS)))
    return (
        jnp.asarray(np.stack(row_tables), jnp.float32).astype(jnp.bfloat16),
        jnp.asarray(np.stack(col_tables), jnp.float32).astype(jnp.bfloat16),
        jnp.asarray(np.stack(turns), jnp.float32),
    )


def slide_turns(slides):
    total = ROWS * COLS
    row_turns = (jnp.arange(ROWS, dtype=jnp.int32)[None, :] * (COLS * slides % total)[:, None]) % total
    col_turns = (jnp.arange(COLS, dtype=jnp.int32)[None, :] * slides[:, None]) % total
    row_angles = row_turns.astype(jnp.float32) * (two_pi / total)
    col_angles = col_turns.astype(jnp.float32) * (two_pi / total)
    rows = jnp.concatenate([jnp.cos(row_angles)[:, None], jnp.sin(row_angles)[:, None]] * 4, 1)
    cols = jnp.concatenate([jnp.cos(col_angles)[:, None], jnp.sin(col_angles)[:, None]] * 4, 1)
    return rows, cols


def ring_order(chips):
    return list(range(0, chips, 2)) + list(range(chips - 1 - chips % 2, 0, -2))


def to_partner():
    return [(i, i ^ 1) for i in range(lax.axis_size("tpl"))]


def half_chunks(strain_slots, det, owner):
    core = lax.axis_index("tpl") % CORES
    half = ROWS * COLS // CORES
    bins = half // HALF_CHUNKS
    side = lambda which: lax.dynamic_slice(strain_slots, (0, det, 0, which * half), (1, 1, 2, half))[0, 0]
    got = lax.ppermute(side(1 - core), "tpl", to_partner())
    first = jnp.where(core == owner % CORES, side(core), got)
    return [first[:, at : at + bins].reshape(2, bins // COLS, COLS) for at in range(0, half, bins)]


def spread(chunks, owner, hooks):
    devices = lax.axis_size("tpl")
    chips = devices // CORES
    order = ring_order(chips)
    chip, core = lax.axis_index("tpl") // CORES, lax.axis_index("tpl") % CORES
    on_owner_chip = chip == owner // CORES
    along = []
    for at in range(chips):
        along.append((order[at] * CORES, order[(at + 1) % chips] * CORES))
        along.append((order[(at + 1) % chips] * CORES + 1, order[at] * CORES + 1))
    sent, arrived = [], []
    count = len(chunks)
    for slot in range(count + LAG * (chips - 1)):
        if slot < LAG:
            here = chunks[slot]
        elif slot < count:
            here = jnp.where(on_owner_chip, chunks[slot], arrived[slot - LAG])
        else:
            here = arrived[slot - LAG]
        if slot in hooks:
            here = hooks[slot](here)
        sent.append(here)
        if slot < count + LAG * (chips - 2):
            arrived.append(lax.ppermute(here, "tpl", along))
    shared = [lax.ppermute(here, "tpl", to_partner()) for here in sent]
    return sent, shared


def distances(owner):
    chips = lax.axis_size("tpl") // CORES
    chip, core = lax.axis_index("tpl") // CORES, lax.axis_index("tpl") % CORES
    place = lambda at: jnp.where(at % 2 == 0, at // 2, chips - 1 - at // 2)
    forward = (place(chip) - place(owner // CORES)) % chips
    backward = (place(owner // CORES) - place(chip)) % chips
    return jnp.where(core == 0, forward, backward), jnp.where(core == 0, backward, forward)


def pick(templates, lists):
    devices, groups = lax.axis_size("tpl"), lax.axis_size("grp")
    own_group = lax.axis_index("grp")
    per_device = lists.shape[1]
    rows = templates.shape[2] // COLS
    pieces = per_device * 2
    if pieces % groups:
        groups, own_group = 1, jnp.int32(0)
    size = pieces // groups
    if size == 2 and rows == WAVE_ROWS:
        picked = templates[lax.dynamic_index_in_dim(lists, own_group, 1, keepdims=False)]
        picked = picked.reshape(devices, size, rows, COLS)
        parts = [picked[:, :, at : at + SEND_ROWS] for at in range(0, rows, SEND_ROWS)]
        return parts, [(own_group - turn) % groups for turn in range(groups)]
    picked = templates[lists.reshape(-1)].reshape(devices, pieces, rows, COLS)
    return [lax.dynamic_slice_in_dim(picked, own_group * size, size, 1)], None


def exchange(block):
    return lax.all_to_all(block, "tpl", split_axis=0, concat_axis=0, tiled=True)


def across(own):
    groups = lax.axis_size("grp")
    return [own] + [
        lax.ppermute(own, "grp", [(at, (at + turn) % groups) for at in range(groups)]) for turn in range(1, groups)
    ]


def assemble(own, per_device):
    groups = lax.axis_size("grp")
    found = jnp.stack(across(own) if per_device * 2 % groups == 0 else [own])
    found = found[(lax.axis_index("grp") - jnp.arange(found.shape[0])) % found.shape[0]]
    found = found.transpose(0, 2, 1, 3, 4).reshape(per_device, 2, ROWS // WAVE_ROWS, WAVE_ROWS, COLS)
    return [[found[at].transpose(1, 0, 2, 3)] for at in range(per_device)]


def quarters(parts):
    (re0, im0), (re1, im1), (re2, im2), (re3, im3) = parts
    even_re, even_im, odd_re, odd_im = re0 + re2, im0 + im2, re1 + re3, im1 + im3
    left_re, left_im, right_re, right_im = re0 - re2, im0 - im2, re1 - re3, im1 - im3
    return (
        (even_re + odd_re, even_im + odd_im),
        (left_re - right_im, left_im + right_re),
        (even_re - odd_re, even_im - odd_im),
        (left_re + right_im, left_im - right_re),
    )


def prepare_kernel(count, cut_ref, list_ref, where_ref, *refs):
    piece_refs, (masked_ref, sigma_ref) = refs[:-2], refs[-2:]
    pieces = len(piece_refs) // count
    rows = WAVE_ROWS // pieces
    for tpl in range(count):
        cutoff = cut_ref[list_ref[where_ref[2] * count + where_ref[4 + tpl]]]
        total = jnp.zeros((8, COLS), jnp.float32)
        for piece in range(pieces):
            wave_ref = piece_refs[tpl * pieces + piece]
            for block in range(ROWS // WAVE_ROWS):
                start = block * WAVE_ROWS + piece * rows
                bins = (lax.broadcasted_iota(jnp.int32, (rows, COLS), 0) + start) * COLS
                inside = bins + lax.broadcasted_iota(jnp.int32, (rows, COLS), 1) < cutoff
                wave_re = jnp.where(inside, wave_ref[block, 0].astype(jnp.float32), 0.0)
                wave_im = jnp.where(inside, wave_ref[block, 1].astype(jnp.float32), 0.0)
                masked_ref[tpl, 0, start : start + rows, :] = wave_re.astype(jnp.bfloat16)
                masked_ref[tpl, 1, start : start + rows, :] = wave_im.astype(jnp.bfloat16)
                squares = wave_re * wave_re + wave_im * wave_im
                total = total + jnp.sum(squares.reshape(-1, 8, COLS), axis=0)
        sigma_ref[tpl] = jnp.sum(total)


def detector_kernel(det, chips, where_ref, sigma_ref, *refs):
    first, last = det == 0, det == DET - 1
    slots = HALF_CHUNKS + LAG * (chips - 1)
    near_refs, far_refs, refs = refs[:slots], refs[slots : 2 * slots], refs[2 * slots :]
    masked, rphase_ref, cphase_ref, row_ref, col_ref, twiddle_ref = refs[:6]
    refs = refs[6:]
    before, refs = (None, refs) if first else (refs[0], refs[1:])
    outputs, (strain_ref, strain_sem, turned_ref, slid, stacked, twisted) = refs[:-6], refs[-6:]
    count = masked.shape[0]
    core, near, far = where_ref[0], where_ref[1], where_ref[3]
    half = ROWS // CORES
    rows = half // HALF_CHUNKS

    for slot_refs, distance, side in ((near_refs, near, core), (far_refs, far, 1 - core)):
        for away in range(chips):
            @pl.when(distance == away)
            def _():
                for at in range(HALF_CHUNKS):
                    into = pl.ds(pl.multiple_of(side * half + at * rows, rows), rows)
                    pltpu.make_async_copy(slot_refs[at + LAG * away], strain_ref.at[:, into, :], strain_sem).start()
    turned_ref[...] = rphase_ref[det].T
    cc, cs = cphase_ref[det, 0:1, :], cphase_ref[det, 1:2, :]
    pltpu.make_async_copy(strain_ref, strain_ref, strain_sem).wait()
    for at in range(0, ROWS, PART):
        part = slice(at, at + PART)
        rc, rs = turned_ref[part, 0:1], turned_ref[part, 1:2]
        turn_re = rc * cc - rs * cs
        turn_im = rc * cs + rs * cc
        data_re, data_im = strain_ref[0, part, :].astype(jnp.float32), strain_ref[1, part, :].astype(jnp.float32)
        slid[0, part, :] = data_re * turn_re - data_im * turn_im
        slid[1, part, :] = data_re * turn_im + data_im * turn_re

    largest = []
    for tpl in range(count):
        for at in range(0, PART, ROW_STEP):
            for col_at in range(0, COLS, PART):
                cols = slice(col_at, col_at + PART)
                parts = []
                for quarter in range(RADIX):
                    spot = slice(quarter * PART + at, quarter * PART + at + ROW_STEP)
                    wave_re = masked[tpl, 0, spot, cols].astype(jnp.float32)
                    wave_im = masked[tpl, 1, spot, cols].astype(jnp.float32)
                    data_re, data_im = slid[0, spot, cols], slid[1, spot, cols]
                    parts.append((data_re * wave_re + data_im * wave_im, data_im * wave_re - data_re * wave_im))
                for residue, (re, im) in enumerate(quarters(parts)):
                    stacked[tpl, residue, at : at + ROW_STEP, cols] = re.astype(jnp.bfloat16)
                    stacked[tpl, residue, PART + at : PART + at + ROW_STEP, cols] = im.astype(jnp.bfloat16)
        for residue in range(RADIX):
            section = jnp.dot(row_ref[residue], stacked[tpl, residue], preferred_element_type=jnp.float32)
            for at in range(0, PART, ROW_STEP):
                parts = []
                for quarter in range(RADIX):
                    cols = slice(quarter * PART, (quarter + 1) * PART)
                    re, im = section[at : at + ROW_STEP, cols], section[PART + at : PART + at + ROW_STEP, cols]
                    turn_re = twiddle_ref[residue, 0, at : at + ROW_STEP, cols]
                    turn_im = twiddle_ref[residue, 1, at : at + ROW_STEP, cols]
                    parts.append((re * turn_re - im * turn_im, re * turn_im + im * turn_re))
                spot = slice(residue * PART + at, residue * PART + at + ROW_STEP)
                for other, sums in enumerate(quarters(parts)):
                    for which, value in enumerate(sums):
                        high = value.astype(jnp.bfloat16)
                        low = (value - high.astype(jnp.float32)).astype(jnp.bfloat16)
                        twisted[tpl, other, spot, which * PART : (which + 1) * PART] = high
                        twisted[tpl, other, spot, (which + 2) * PART : (which + 3) * PART] = low
        peak = jnp.zeros((8, PART), jnp.float32)
        for other in range(RADIX):
            series = jnp.dot(twisted[tpl, other], col_ref[other], preferred_element_type=jnp.float32)
            squares = series[:, :PART] * series[:, :PART] + series[:, PART:] * series[:, PART:]
            cols = slice(other * PART, (other + 1) * PART)
            if not first:
                squares = squares + before[tpl, :, cols]
            if last:
                peak = jnp.maximum(peak, jnp.max(squares.reshape(-1, 8, PART), axis=0))
            else:
                outputs[0][tpl, :, cols] = squares
        largest.append(peak)

    if last:
        for tpl in range(count):
            place = where_ref[4 + tpl]
            outputs[0][place] = jnp.max(largest[tpl]) / (2.0 * (sigma_ref[tpl] + eps_norm))
            outputs[1][place] = sigma_ref[tpl] / (ROWS * COLS)


smem = pl.BlockSpec(memory_space=pltpu.SMEM)
vmem = pl.BlockSpec(memory_space=pltpu.VMEM)
anywhere = pl.BlockSpec(memory_space=pl.ANY)


def prepare(cutoffs, lists, where, waves):
    count = len(waves)
    operands = [piece for wave in waves for piece in wave]
    return pl.pallas_call(
        functools.partial(prepare_kernel, count),
        out_shape=(
            jax.ShapeDtypeStruct((count, 2, ROWS, COLS), jnp.bfloat16),
            jax.ShapeDtypeStruct((count,), jnp.float32),
        ),
        in_specs=[smem, smem, smem] + [vmem] * len(operands),
        out_specs=(vmem, smem),
        compiler_params=pltpu.CompilerParams(vmem_limit_bytes=VMEM_LIMIT),
        cost_estimate=pl.CostEstimate(flops=2_000_000_000, bytes_accessed=6_000_000, transcendentals=0),
    )(cutoffs, lists, where, *operands)


def detector(det, chips, where, sigma, sent, shared, masked, turns, before):
    count = masked.shape[0]
    slots = slice(det * HALF_CHUNKS, (det + 1) * HALF_CHUNKS + LAG * (chips - 1))
    found = [*sent[slots], *shared[slots]]
    last = det == DET - 1
    scalars = jax.ShapeDtypeStruct((count,), jnp.float32)
    operands = [masked, *turns, *tables(), *before]
    return pl.pallas_call(
        functools.partial(detector_kernel, det, chips),
        out_shape=(scalars, scalars) if last else (jax.ShapeDtypeStruct((count, ROWS, COLS), jnp.float32),),
        in_specs=[smem, smem] + [anywhere] * len(found) + [vmem] * len(operands),
        out_specs=(smem, smem) if last else (vmem,),
        scratch_shapes=[
            pltpu.VMEM((2, ROWS, COLS), jnp.bfloat16),
            pltpu.SemaphoreType.DMA,
            pltpu.VMEM((ROWS, 8), jnp.float32),
            pltpu.VMEM((2, ROWS, COLS), jnp.float32),
            pltpu.VMEM((count, RADIX, 2 * PART, COLS), jnp.bfloat16),
            pltpu.VMEM((count, RADIX, ROWS, 4 * PART), jnp.bfloat16),
        ],
        compiler_params=pltpu.CompilerParams(vmem_limit_bytes=VMEM_LIMIT),
        cost_estimate=pl.CostEstimate(flops=5_000_000_000, bytes_accessed=10_000_000, transcendentals=0),
    )(where, sigma, *found, *operands)


def body(strain_slots, templates, cutoffs, lists, owner, slides):
    me, owner = lax.axis_index("tpl"), owner[0]
    chips = lax.axis_size("tpl") // CORES
    per_device = lists.shape[1]
    chunks = [chunk for det in range(DET) for chunk in half_chunks(strain_slots, det, owner)]
    parts, places = pick(templates, lists)
    ids = list(range(per_device)) if places is None else places
    near, far = distances(owner)
    where = jnp.stack([jnp.asarray(at, jnp.int32) for at in (me % CORES, near, me, far, *ids)])
    held = {"arrived": exchange(parts[0]), "small": (slide_turns(slides), where, lists.reshape(-1))}

    def templates_here(chunk):
        chunk, held["arrived"], held["small"] = lax.optimization_barrier((chunk, held["arrived"], held["small"]))
        if places is None:
            waves = assemble(held["arrived"], per_device)
        else:
            waves = [[wave] for wave in across(held["arrived"])]
        _, where, flat_list = held["small"]
        held["masked"] = prepare(cutoffs, flat_list, where, waves)
        return chunk

    def masked_here(chunk):
        chunk, held["masked"] = lax.optimization_barrier((chunk, held["masked"]))
        return chunk

    sent, shared = spread(chunks, owner, {TEMPLATE_SLOT: templates_here, MASKED_SLOT: masked_here})
    turns, where, _ = held["small"]
    masked, sigma = held["masked"]
    result = ()
    for det in range(DET):
        result = detector(det, chips, where, sigma, sent, shared, masked, turns, result)
    return result


def solution(mesh):
    in_specs = (
        P(("grp", "tpl"), None, None, None),
        P(None, None, "tpl"),
        P(),
        P(),
        P("grp"),
        P("grp"),
    )
    out_specs = (P(("grp", "tpl")), P(("grp", "tpl")))
    return jax.shard_map(body, mesh=mesh, in_specs=in_specs, out_specs=out_specs, check_vma=False)
```

```python
import functools

import jax
import jax.numpy as jnp
import numpy as np
from jax import lax
from jax.experimental import pallas as pl
from jax.experimental.pallas import tpu as pltpu
from jax.sharding import PartitionSpec as P

DET = 3
ROWS = 512
COLS = 512
RADIX = 4
PART = 128
ROW_STEP = 16
WAVE_ROWS = 32
SEND_ROWS = 32
CORES = 2
HALF_CHUNKS = 2
LAG = 2
TEMPLATE_SLOT = 4
MASKED_SLOT = 18
VMEM_LIMIT = 24 * 1024 * 1024


two_pi = 6.283185307179586
eps_norm = 1e-06


def turn_table(left_ids, right_ids, period):
    angles = (left_ids[:, None] * right_ids[None, :] % period).astype(np.float64) * (2 * np.pi / period)
    return np.cos(angles), np.sin(angles)


def tables():
    part_ids, col_ids = np.arange(PART), np.arange(COLS)
    row_tables, col_tables, turns = [], [], []
    for residue in range(RADIX):
        cos, sin = turn_table(RADIX * part_ids + residue, part_ids, ROWS)
        row_tables.append(np.block([[cos, -sin], [sin, cos]]))
        col_tables.append(np.block([[cos.T, sin.T], [-sin.T, cos.T]] * 2))
        turns.append(np.stack(turn_table(RADIX * part_ids + residue, col_ids, ROWS * COLS)))
    return (
        jnp.asarray(np.stack(row_tables), jnp.float32).astype(jnp.bfloat16),
        jnp.asarray(np.stack(col_tables), jnp.float32).astype(jnp.bfloat16),
        jnp.asarray(np.stack(turns), jnp.float32),
    )


def slide_turns(slides):
    total = ROWS * COLS
    row_turns = (jnp.arange(ROWS, dtype=jnp.int32)[None, :] * (COLS * slides % total)[:, None]) % total
    col_turns = (jnp.arange(COLS, dtype=jnp.int32)[None, :] * slides[:, None]) % total
    row_angles = row_turns.astype(jnp.float32) * (two_pi / total)
    col_angles = col_turns.astype(jnp.float32) * (two_pi / total)
    rows = jnp.concatenate([jnp.cos(row_angles)[:, None], jnp.sin(row_angles)[:, None]] * 4, 1)
    cols = jnp.concatenate([jnp.cos(col_angles)[:, None], jnp.sin(col_angles)[:, None]] * 4, 1)
    return rows, cols


def ring_order(chips):
    return list(range(0, chips, 2)) + list(range(chips - 1 - chips % 2, 0, -2))


def to_partner():
    return [(i, i ^ 1) for i in range(lax.axis_size("tpl"))]


def half_chunks(strain_slots, det, owner):
    core = lax.axis_index("tpl") % CORES
    half = ROWS * COLS // CORES
    bins = half // HALF_CHUNKS
    side = lambda which: lax.dynamic_slice(strain_slots, (0, det, 0, which * half), (1, 1, 2, half))[0, 0]
    got = lax.ppermute(side(1 - core), "tpl", to_partner())
    first = jnp.where(core == owner % CORES, side(core), got)
    return [first[:, at : at + bins].reshape(2, bins // COLS, COLS) for at in range(0, half, bins)]


def spread(chunks, owner, hooks):
    devices = lax.axis_size("tpl")
    chips = devices // CORES
    order = ring_order(chips)
    chip, core = lax.axis_index("tpl") // CORES, lax.axis_index("tpl") % CORES
    on_owner_chip = chip == owner // CORES
    along = []
    for at in range(chips):
        along.append((order[at] * CORES, order[(at + 1) % chips] * CORES))
        along.append((order[(at + 1) % chips] * CORES + 1, order[at] * CORES + 1))
    sent, arrived = [], []
    count = len(chunks)
    for slot in range(count + LAG * (chips - 1)):
        if slot < LAG:
            here = chunks[slot]
        elif slot < count:
            here = jnp.where(on_owner_chip, chunks[slot], arrived[slot - LAG])
        else:
            here = arrived[slot - LAG]
        if slot in hooks:
            here = hooks[slot](here)
        sent.append(here)
        if slot < count + LAG * (chips - 2):
            arrived.append(lax.ppermute(here, "tpl", along))
    shared = [lax.ppermute(here, "tpl", to_partner()) for here in sent]
    return sent, shared


def distances(owner):
    chips = lax.axis_size("tpl") // CORES
    chip, core = lax.axis_index("tpl") // CORES, lax.axis_index("tpl") % CORES
    place = lambda at: jnp.where(at % 2 == 0, at // 2, chips - 1 - at // 2)
    forward = (place(chip) - place(owner // CORES)) % chips
    backward = (place(owner // CORES) - place(chip)) % chips
    return jnp.where(core == 0, forward, backward), jnp.where(core == 0, backward, forward)


def pick(templates, lists):
    devices, groups = lax.axis_size("tpl"), lax.axis_size("grp")
    own_group = lax.axis_index("grp")
    per_device = lists.shape[1]
    rows = templates.shape[2] // COLS
    pieces = per_device * 2
    if pieces % groups:
        groups, own_group = 1, jnp.int32(0)
    size = pieces // groups
    if size == 2 and rows == WAVE_ROWS:
        picked = templates[lax.dynamic_index_in_dim(lists, own_group, 1, keepdims=False)]
        picked = picked.reshape(devices, size, rows, COLS)
        parts = [picked[:, :, at : at + SEND_ROWS] for at in range(0, rows, SEND_ROWS)]
        return parts, [(own_group - turn) % groups for turn in range(groups)]
    picked = templates[lists.reshape(-1)].reshape(devices, pieces, rows, COLS)
    return [lax.dynamic_slice_in_dim(picked, own_group * size, size, 1)], None


def exchange(block):
    return lax.all_to_all(block, "tpl", split_axis=0, concat_axis=0, tiled=True)


def across(own):
    groups = lax.axis_size("grp")
    return [own] + [
        lax.ppermute(own, "grp", [(at, (at + turn) % groups) for at in range(groups)]) for turn in range(1, groups)
    ]


def assemble(own, per_device):
    groups = lax.axis_size("grp")
    found = jnp.stack(across(own) if per_device * 2 % groups == 0 else [own])
    found = found[(lax.axis_index("grp") - jnp.arange(found.shape[0])) % found.shape[0]]
    found = found.transpose(0, 2, 1, 3, 4).reshape(per_device, 2, ROWS // WAVE_ROWS, WAVE_ROWS, COLS)
    return [[found[at].transpose(1, 0, 2, 3)] for at in range(per_device)]


def quarters(parts):
    (re0, im0), (re1, im1), (re2, im2), (re3, im3) = parts
    even_re, even_im, odd_re, odd_im = re0 + re2, im0 + im2, re1 + re3, im1 + im3
    left_re, left_im, right_re, right_im = re0 - re2, im0 - im2, re1 - re3, im1 - im3
    return (
        (even_re + odd_re, even_im + odd_im),
        (left_re - right_im, left_im + right_re),
        (even_re - odd_re, even_im - odd_im),
        (left_re + right_im, left_im - right_re),
    )


def prepare_kernel(count, cut_ref, list_ref, where_ref, *refs):
    piece_refs, (masked_ref, sigma_ref) = refs[:-2], refs[-2:]
    pieces = len(piece_refs) // count
    rows = WAVE_ROWS // pieces
    for tpl in range(count):
        cutoff = cut_ref[list_ref[where_ref[2] * count + where_ref[4 + tpl]]]
        total = jnp.zeros((8, COLS), jnp.float32)
        for piece in range(pieces):
            wave_ref = piece_refs[tpl * pieces + piece]
            for block in range(ROWS // WAVE_ROWS):
                start = block * WAVE_ROWS + piece * rows
                bins = (lax.broadcasted_iota(jnp.int32, (rows, COLS), 0) + start) * COLS
                inside = bins + lax.broadcasted_iota(jnp.int32, (rows, COLS), 1) < cutoff
                wave_re = jnp.where(inside, wave_ref[block, 0].astype(jnp.float32), 0.0)
                wave_im = jnp.where(inside, wave_ref[block, 1].astype(jnp.float32), 0.0)
                masked_ref[tpl, 0, start : start + rows, :] = wave_re.astype(jnp.bfloat16)
                masked_ref[tpl, 1, start : start + rows, :] = wave_im.astype(jnp.bfloat16)
                squares = wave_re * wave_re + wave_im * wave_im
                total = total + jnp.sum(squares.reshape(-1, 8, COLS), axis=0)
        sigma_ref[tpl] = jnp.sum(total)


def detector_kernel(det, chips, where_ref, sigma_ref, *refs):
    first, last = det == 0, det == DET - 1
    slots = HALF_CHUNKS + LAG * (chips - 1)
    near_refs, far_refs, refs = refs[:slots], refs[slots : 2 * slots], refs[2 * slots :]
    masked, rphase_ref, cphase_ref, row_ref, col_ref, twiddle_ref = refs[:6]
    refs = refs[6:]
    before, refs = (None, refs) if first else (refs[0], refs[1:])
    outputs, (strain_ref, strain_sem, turned_ref, slid, stacked, twisted) = refs[:-6], refs[-6:]
    count = masked.shape[0]
    core, near, far = where_ref[0], where_ref[1], where_ref[3]
    half = ROWS // CORES
    rows = half // HALF_CHUNKS

    for slot_refs, distance, side in ((near_refs, near, core), (far_refs, far, 1 - core)):
        for away in range(chips):
            @pl.when(distance == away)
            def _():
                for at in range(HALF_CHUNKS):
                    into = pl.ds(pl.multiple_of(side * half + at * rows, rows), rows)
                    pltpu.make_async_copy(slot_refs[at + LAG * away], strain_ref.at[:, into, :], strain_sem).start()
    turned_ref[...] = rphase_ref[det].T
    cc, cs = cphase_ref[det, 0:1, :], cphase_ref[det, 1:2, :]
    pltpu.make_async_copy(strain_ref, strain_ref, strain_sem).wait()
    for at in range(0, ROWS, PART):
        part = slice(at, at + PART)
        rc, rs = turned_ref[part, 0:1], turned_ref[part, 1:2]
        turn_re = rc * cc - rs * cs
        turn_im = rc * cs + rs * cc
        data_re, data_im = strain_ref[0, part, :].astype(jnp.float32), strain_ref[1, part, :].astype(jnp.float32)
        slid[0, part, :] = data_re * turn_re - data_im * turn_im
        slid[1, part, :] = data_re * turn_im + data_im * turn_re

    largest = []
    for tpl in range(count):
        for at in range(0, PART, ROW_STEP):
            for col_at in range(0, COLS, PART):
                cols = slice(col_at, col_at + PART)
                parts = []
                for quarter in range(RADIX):
                    spot = slice(quarter * PART + at, quarter * PART + at + ROW_STEP)
                    wave_re = masked[tpl, 0, spot, cols].astype(jnp.float32)
                    wave_im = masked[tpl, 1, spot, cols].astype(jnp.float32)
                    data_re, data_im = slid[0, spot, cols], slid[1, spot, cols]
                    parts.append((data_re * wave_re + data_im * wave_im, data_im * wave_re - data_re * wave_im))
                for residue, (re, im) in enumerate(quarters(parts)):
                    stacked[tpl, residue, at : at + ROW_STEP, cols] = re.astype(jnp.bfloat16)
                    stacked[tpl, residue, PART + at : PART + at + ROW_STEP, cols] = im.astype(jnp.bfloat16)
        for residue in range(RADIX):
            section = jnp.dot(row_ref[residue], stacked[tpl, residue], preferred_element_type=jnp.float32)
            for at in range(0, PART, ROW_STEP):
                parts = []
                for quarter in range(RADIX):
                    cols = slice(quarter * PART, (quarter + 1) * PART)
                    re, im = section[at : at + ROW_STEP, cols], section[PART + at : PART + at + ROW_STEP, cols]
                    turn_re = twiddle_ref[residue, 0, at : at + ROW_STEP, cols]
                    turn_im = twiddle_ref[residue, 1, at : at + ROW_STEP, cols]
                    parts.append((re * turn_re - im * turn_im, re * turn_im + im * turn_re))
                spot = slice(residue * PART + at, residue * PART + at + ROW_STEP)
                for other, sums in enumerate(quarters(parts)):
                    for which, value in enumerate(sums):
                        high = value.astype(jnp.bfloat16)
                        low = (value - high.astype(jnp.float32)).astype(jnp.bfloat16)
                        twisted[tpl, other, spot, which * PART : (which + 1) * PART] = high
                        twisted[tpl, other, spot, (which + 2) * PART : (which + 3) * PART] = low
        peak = jnp.zeros((8, PART), jnp.float32)
        for other in range(RADIX):
            series = jnp.dot(twisted[tpl, other], col_ref[other], preferred_element_type=jnp.float32)
            squares = series[:, :PART] * series[:, :PART] + series[:, PART:] * series[:, PART:]
            cols = slice(other * PART, (other + 1) * PART)
            if not first:
                squares = squares + before[tpl, :, cols]
            if last:
                peak = jnp.maximum(peak, jnp.max(squares.reshape(-1, 8, PART), axis=0))
            else:
                outputs[0][tpl, :, cols] = squares
        largest.append(peak)

    if last:
        for tpl in range(count):
            place = where_ref[4 + tpl]
            outputs[0][place] = jnp.max(largest[tpl]) / (2.0 * (sigma_ref[tpl] + eps_norm))
            outputs[1][place] = sigma_ref[tpl] / (ROWS * COLS)


smem = pl.BlockSpec(memory_space=pltpu.SMEM)
vmem = pl.BlockSpec(memory_space=pltpu.VMEM)
anywhere = pl.BlockSpec(memory_space=pl.ANY)


def prepare(cutoffs, lists, where, waves):
    count = len(waves)
    operands = [piece for wave in waves for piece in wave]
    return pl.pallas_call(
        functools.partial(prepare_kernel, count),
        out_shape=(
            jax.ShapeDtypeStruct((count, 2, ROWS, COLS), jnp.bfloat16),
            jax.ShapeDtypeStruct((count,), jnp.float32),
        ),
        in_specs=[smem, smem, smem] + [vmem] * len(operands),
        out_specs=(vmem, smem),
        compiler_params=pltpu.CompilerParams(vmem_limit_bytes=VMEM_LIMIT),
        cost_estimate=pl.CostEstimate(flops=2_000_000_000, bytes_accessed=6_000_000, transcendentals=0),
    )(cutoffs, lists, where, *operands)


def detector(det, chips, where, sigma, sent, shared, masked, turns, before):
    count = masked.shape[0]
    slots = slice(det * HALF_CHUNKS, (det + 1) * HALF_CHUNKS + LAG * (chips - 1))
    found = [*sent[slots], *shared[slots]]
    last = det == DET - 1
    scalars = jax.ShapeDtypeStruct((count,), jnp.float32)
    operands = [masked, *turns, *tables(), *before]
    return pl.pallas_call(
        functools.partial(detector_kernel, det, chips),
        out_shape=(scalars, scalars) if last else (jax.ShapeDtypeStruct((count, ROWS, COLS), jnp.float32),),
        in_specs=[smem, smem] + [anywhere] * len(found) + [vmem] * len(operands),
        out_specs=(smem, smem) if last else (vmem,),
        scratch_shapes=[
            pltpu.VMEM((2, ROWS, COLS), jnp.bfloat16),
            pltpu.SemaphoreType.DMA,
            pltpu.VMEM((ROWS, 8), jnp.float32),
            pltpu.VMEM((2, ROWS, COLS), jnp.float32),
            pltpu.VMEM((count, RADIX, 2 * PART, COLS), jnp.bfloat16),
            pltpu.VMEM((count, RADIX, ROWS, 4 * PART), jnp.bfloat16),
        ],
        compiler_params=pltpu.CompilerParams(vmem_limit_bytes=VMEM_LIMIT),
        cost_estimate=pl.CostEstimate(flops=5_000_000_000, bytes_accessed=10_000_000, transcendentals=0),
    )(where, sigma, *found, *operands)


def body(strain_slots, templates, cutoffs, lists, owner, slides):
    me, owner = lax.axis_index("tpl"), owner[0]
    chips = lax.axis_size("tpl") // CORES
    per_device = lists.shape[1]
    chunks = half_chunks(strain_slots, 0, owner)
    strain_slots, templates, chunks = lax.optimization_barrier((strain_slots, templates, chunks))
    parts, places = pick(templates, lists)
    ids = list(range(per_device)) if places is None else places
    near, far = distances(owner)
    where = jnp.stack([jnp.asarray(at, jnp.int32) for at in (me % CORES, near, me, far, *ids)])
    for det in range(1, DET):
        more = half_chunks(strain_slots, det, owner)
        strain_slots, more = lax.optimization_barrier((strain_slots, more))
        chunks += more
    held = {"arrived": exchange(parts[0]), "small": (slide_turns(slides), where, lists.reshape(-1))}

    def templates_here(chunk):
        chunk, held["arrived"], held["small"] = lax.optimization_barrier((chunk, held["arrived"], held["small"]))
        if places is None:
            waves = assemble(held["arrived"], per_device)
        else:
            waves = [[wave] for wave in across(held["arrived"])]
        _, where, flat_list = held["small"]
        held["masked"] = prepare(cutoffs, flat_list, where, waves)
        return chunk

    def masked_here(chunk):
        chunk, held["masked"] = lax.optimization_barrier((chunk, held["masked"]))
        return chunk

    sent, shared = spread(chunks, owner, {TEMPLATE_SLOT: templates_here, MASKED_SLOT: masked_here})
    turns, where, _ = held["small"]
    masked, sigma = held["masked"]
    result = ()
    for det in range(DET):
        result = detector(det, chips, where, sigma, sent, shared, masked, turns, result)
    return result


def solution(mesh):
    in_specs = (
        P(("grp", "tpl"), None, None, None),
        P(None, None, "tpl"),
        P(),
        P(),
        P("grp"),
        P("grp"),
    )
    out_specs = (P(("grp", "tpl")), P(("grp", "tpl")))
    return jax.shard_map(body, mesh=mesh, in_specs=in_specs, out_specs=out_specs, check_vma=False)
```
